32 devices in a mesh: seq: 8 (over y, x, core), head: 4 (over z).
Axes of the slice: x: 2, y: 2, z: 4, core: 2. Of those that a mesh axis runs over, the one named last changes fastest.
Arguments:
- tokens: bfloat16 [4, 4096, 1792], P(None, ('seq', 'head')), may hold values from -6 to 6
- cotangent: bfloat16 [4, 4096, 1792], P(None, ('seq', 'head')), may hold values from -6 to 6
- segment_ids: int32 [4, 4096], P(None, 'seq'), may hold values from 0 to 15, as said below
- query_weight: bfloat16 [1792, 256], P('seq', 'head'), may hold values from -0.125 to 0.125
- key_weight: bfloat16 [1792, 256], P('seq', 'head'), may hold values from -0.125 to 0.125
- value_weight: bfloat16 [1792, 1792], P('seq', 'head'), may hold values from -0.125 to 0.125
- filter_weight: bfloat16 [1792, 1792], P('seq', 'head'), may hold values from -0.125 to 0.125
- out_weight: bfloat16 [1792, 1792], P('head', 'seq'), may hold values from -3.5 to 3.5
- gate_weight: bfloat16 [1792, 4864], P('seq', 'head'), may hold values from -0.125 to 0.125
- up_weight: bfloat16 [1792, 4864], P('seq', 'head'), may hold values from -0.125 to 0.125
- down_weight: bfloat16 [1792, 4864], P('seq', 'head'), may hold values from -0.078125 to 0.078125
- norm_gain: bfloat16 [1792], P('seq'), may hold values from 0.5 to 1.5
- ffn_gain: bfloat16 [1792], P('seq'), may hold values from 0.5 to 1.5
- conv_taps: bfloat16 [3, 1792], P(None, ('head', 'seq')), may hold values from -2.5 to 2.5
Outputs:
- layer_output: bfloat16 [4, 4096, 1792], P(None, ('seq', 'head'))
- tokens_grad: bfloat16 [4, 4096, 1792], P(None, ('seq', 'head'))
- query_weight_grad: float32 [1792, 256], P('seq', 'head')
- key_weight_grad: float32 [1792, 256], P('seq', 'head')
- value_weight_grad: float32 [1792, 1792], P('seq', 'head')
- filter_weight_grad: float32 [1792, 1792], P('seq', 'head')
- out_weight_grad: float32 [1792, 1792], P('head', 'seq')
- gate_weight_grad: float32 [1792, 4864], P('seq', 'head')
- up_weight_grad: float32 [1792, 4864], P('seq', 'head')
- down_weight_grad: float32 [1792, 4864], P('seq', 'head')
- norm_gain_grad: float32 [1792], P(('head', 'seq'))
- ffn_gain_grad: float32 [1792], P(('head', 'seq'))
- conv_taps_grad: float32 [3, 1792], P(None, ('head', 'seq'))
The draws below stay inside these ranges and needn't reach their ends.
Inputs may be any that keep to these rules, and one draw needn't show every extreme that they name: `segment_ids`: within each sequence the ids start at 0, never fall, rise by at most 1 from one token to the next, and reach 15.
All inputs are finite; a program needn't handle non-finite values.
Results may differ from the reference program's by a relative error of at most 0.02.
Values may be sent and summed in bfloat16 or wider, within the bound.
A program may use at most 384 MiB of HBM per device.

```python
import jax
import jax.numpy as jnp
from jax import lax

D = 1792
HEADS = 16
FEAT = 16
FF = 4864
SEQ_TOK = 512
SEQ_MB = 2
MICRO = 2
COUNT = 16
NSEQ = 4
LEN = 4096


def draw_segment_ids(key, part):
    key = jax.random.fold_in(key, 7)
    cut_count = COUNT - 1
    pick_key, order_key = jax.random.split(key)
    spanning = jax.random.randint(pick_key, (MICRO,), 0, SEQ_MB)
    places = jnp.arange(LEN, dtype=jnp.int32)
    sequence_ids = []
    for seq_num in range(SEQ_MB * MICRO):
        seq_key = jax.random.fold_in(order_key, seq_num)
        drawn_cuts = jax.random.permutation(jax.random.fold_in(seq_key, 1), LEN - 1)[:cut_count] + 1
        edge_cuts = jax.random.permutation(jax.random.fold_in(seq_key, 2), 2 * (SEQ_TOK - 1))[:cut_count]
        edge_cuts = jnp.where(edge_cuts < SEQ_TOK - 1, edge_cuts + 1, edge_cuts - (SEQ_TOK - 1) + LEN - SEQ_TOK + 1)
        chosen = jnp.where(spanning[seq_num // SEQ_MB] == seq_num % SEQ_MB, edge_cuts, drawn_cuts)
        seg_row = jnp.sum((places[:, None] >= chosen[None, :].astype(jnp.int32)).astype(jnp.int32), axis=1)
        sequence_ids.append(seg_row)
    return jnp.stack(sequence_ids).astype(jnp.int32)


def shard_levels(stream_key, shape, cuts, smallest, high):
    level, own = 1.0, jax.random.fold_in(stream_key, 6)
    for axis_at, blocks in cuts:
        draws = jnp.exp(jax.random.uniform(jax.random.fold_in(own, axis_at), (blocks,), jnp.float32, smallest / len(cuts), high / len(cuts)))
        level = level * jnp.repeat(draws, shape[axis_at] // blocks).reshape([-1 if axis == axis_at else 1 for axis in range(len(shape))])
    return level


def gaussian(key, extent, scale, reach, cuts=(), kind=jnp.bfloat16):
    drawn = jax.random.normal(key, extent, jnp.float32) * scale
    if len(cuts) > 0:
        drawn = shard_levels(key, extent, cuts, -0.22, 0.18) * drawn
    return jnp.clip(drawn, min=-reach, max=reach).astype(kind)


def setup_inputs(seed: int = 0) -> dict:
    arg_keys = jax.random.split(jax.random.key(seed), 15)
    tokens = gaussian(arg_keys[0], (NSEQ, LEN, D), 1.0, 6.0, ((1, 32),))
    cotangent = gaussian(arg_keys[1], (NSEQ, LEN, D), 1.0, 6.0, ((1, 32),))
    segment_ids = draw_segment_ids(jax.random.fold_in(arg_keys[14], 71), 0)
    query_weight = gaussian(arg_keys[3], (D, HEADS * FEAT), D ** -0.5, 0.125, ((0, 8), (1, 4)))
    key_weight = gaussian(arg_keys[4], (D, HEADS * FEAT), D ** -0.5, 0.125, ((0, 8), (1, 4)))
    value_weight = gaussian(arg_keys[5], (D, D), D ** -0.5, 0.125, ((0, 8), (1, 4)))
    filter_weight = gaussian(arg_keys[6], (D, D), D ** -0.5, 0.125, ((0, 8), (1, 4)))
    out_weight = gaussian(arg_keys[7], (D, D), (max(1, D // 512)) ** -0.5, 3.5, ((0, 4), (1, 8)))
    gate_weight = gaussian(arg_keys[8], (D, FF), D ** -0.5, 0.125, ((0, 8), (1, 4)))
    up_weight = gaussian(arg_keys[9], (D, FF), D ** -0.5, 0.125, ((0, 8), (1, 4)))
    down_weight = gaussian(arg_keys[10], (D, FF), FF ** -0.5, 0.078125, ((0, 8), (1, 4)))
    norm_gain = jnp.clip(1.0 + 0.1 * jax.random.normal(arg_keys[11], (D,), jnp.float32), 0.5, 1.5).astype(jnp.bfloat16)
    ffn_gain = jnp.clip(1.0 + 0.1 * jax.random.normal(arg_keys[12], (D,), jnp.float32), 0.5, 1.5).astype(jnp.bfloat16)
    conv_taps = gaussian(arg_keys[13], (3, D), 0.6, 2.5, ((1, 32),))
    return dict(tokens=tokens, cotangent=cotangent, segment_ids=segment_ids, query_weight=query_weight, key_weight=key_weight, value_weight=value_weight, filter_weight=filter_weight, out_weight=out_weight, gate_weight=gate_weight, up_weight=up_weight, down_weight=down_weight, norm_gain=norm_gain, ffn_gain=ffn_gain, conv_taps=conv_taps)


@jax.custom_vjp
def low(v):
    return lax.optimization_barrier(v.astype(jnp.bfloat16)).astype(jnp.float32)

@jax.custom_vjp
def low_back(v):
    return v

def low_keep(v):
    return (low(v), None)

def low_pass(kept, grad):
    return (grad,)

def back_keep(v):
    return (v, None)

def back_low(kept, grad):
    return (low(grad),)
low.defvjp(low_keep, low_pass)
low_back.defvjp(back_keep, back_low)
EPSILON = 1e-06
HALF_ROOT = 0.5 ** 0.5
HIGHEST = lax.Precision.HIGHEST

def product(left, right):
    return jnp.dot(left, right, preferred_element_type=jnp.float32, precision=HIGHEST)

def rms_scale(values, gain_vec):
    return values * lax.rsqrt(lax.optimization_barrier(jnp.mean(values * values, axis=-1, keepdims=True)) + EPSILON) * gain_vec

def feature_map(values):
    outer_part = values[..., :, None] * values[..., None, :]
    outer_part = outer_part.reshape(values.shape[:-1] + (values.shape[-1] * values.shape[-1],))
    constant_part = jnp.ones(values.shape[:-1] + (1,), jnp.float32)
    return jnp.concatenate([constant_part, values, outer_part * HALF_ROOT], axis=-1)

def short_filter(values, segments, tap_rows):
    zero_row = jnp.zeros((1, values.shape[1]), jnp.float32)
    one_back = jnp.concatenate([zero_row, values[:-1]], axis=0)
    two_back = jnp.concatenate([zero_row, zero_row, values[:-2]], axis=0)
    same_one = jnp.concatenate([jnp.zeros((1,), jnp.float32), (segments[1:] == segments[:-1]).astype(jnp.float32)])
    same_two = jnp.concatenate([jnp.zeros((2,), jnp.float32), (segments[2:] == segments[:-2]).astype(jnp.float32)])
    return tap_rows[0] * values + tap_rows[1] * one_back * same_one[:, None] + tap_rows[2] * two_back * same_two[:, None]

def attend_block(carry, block_in):
    prior_state, prior_norm, prior_last = carry
    queries, key_rows, values, segments = block_in
    mapped_q = feature_map(queries)
    mapped_k = feature_map(key_rows)
    in_prior = (segments == prior_last).astype(jnp.float32)
    numerator = jnp.einsum('thf,hfe->the', mapped_q, prior_state, precision=HIGHEST) * in_prior[:, None, None]
    denominator = jnp.einsum('thf,hf->th', mapped_q, prior_norm, precision=HIGHEST) * in_prior[:, None]
    scores = jnp.einsum('thf,shf->hts', queries, key_rows, precision=HIGHEST)
    places = jnp.arange(queries.shape[0])
    allowed = (places[:, None] >= places[None, :]) & (segments[:, None] == segments[None, :])
    weights = jnp.where(allowed[None], 1.0 + scores + 0.5 * scores * scores, 0.0)
    numerator = numerator + jnp.einsum('hts,she->the', weights, values, precision=HIGHEST)
    denominator = denominator + jnp.transpose(lax.optimization_barrier(jnp.sum(weights, axis=-1)))
    attended = numerator / denominator[:, :, None]
    last_seg = segments[-1]
    tail_weight = (segments == last_seg).astype(jnp.float32)
    tail_keys = mapped_k * tail_weight[:, None, None]
    tail_state = jnp.einsum('thf,the->hfe', tail_keys, values, precision=HIGHEST)
    tail_norm = lax.optimization_barrier(jnp.sum(tail_keys, axis=0))
    carry_on = (prior_last == last_seg).astype(jnp.float32)
    return ((tail_state + carry_on * prior_state, tail_norm + carry_on * prior_norm, last_seg), attended)

def attention(queries, key_rows, values, segments):
    length = queries.shape[0]
    block = min(512, length)
    steps = length // block
    heads = queries.shape[1]
    mapped_width = 1 + queries.shape[2] + queries.shape[2] * queries.shape[2]

    def split_rows(array):
        return array.reshape((steps, block) + array.shape[1:])
    start = (jnp.zeros((heads, mapped_width, values.shape[2]), jnp.float32), jnp.zeros((heads, mapped_width), jnp.float32), jnp.array(-1.0, jnp.float32))
    _, attended = lax.scan(jax.checkpoint(attend_block), start, (split_rows(queries), split_rows(key_rows), split_rows(values), split_rows(segments)))
    return attended.reshape(length, heads * values.shape[2])

def layer(params, token_rows, segments):
    w_query, w_key, w_value, w_filter, w_out, w_gate, w_up, w_down, gain_one, gain_two, tap_rows = params
    length = token_rows.shape[0]
    normed = low(rms_scale(token_rows, gain_one))
    queries = 0.5 * low(low_back(product(normed, w_query)))
    key_rows = 0.5 * low(low_back(product(normed, w_key)))
    values = low(low_back(product(normed, w_value)))
    filter_pre = low_back(product(normed, w_filter))
    mixed_values = short_filter(values, segments, tap_rows) * jax.nn.silu(filter_pre)
    head_shape = (length, HEADS, FEAT)
    attended = attention(queries.reshape(head_shape), key_rows.reshape(head_shape), mixed_values.reshape(length, HEADS, D // HEADS), segments)
    residual = token_rows + low_back(product(low(attended), w_out))
    normed_two = low(rms_scale(residual, gain_two))
    gate_act = low_back(product(normed_two, w_gate))
    up_act = low_back(product(normed_two, w_up))
    hidden = low(jax.nn.silu(gate_act) * up_act)
    return residual + product(hidden, jnp.transpose(w_down))

def reference(tokens, cotangent, segment_ids, query_weight, key_weight, value_weight, filter_weight, out_weight, gate_weight, up_weight, down_weight, norm_gain, ffn_gain, conv_taps):
    params = (query_weight.astype(jnp.float32), key_weight.astype(jnp.float32), value_weight.astype(jnp.float32), filter_weight.astype(jnp.float32), out_weight.astype(jnp.float32), gate_weight.astype(jnp.float32), up_weight.astype(jnp.float32), down_weight.astype(jnp.float32), norm_gain.astype(jnp.float32), ffn_gain.astype(jnp.float32), conv_taps.astype(jnp.float32))

    def one_sequence(totals, inputs):
        token_rows, cot_rows, segments = inputs

        def forward(weights_in, rows_in):
            return layer(weights_in, rows_in, segments)
        result, pull_back = jax.vjp(forward, params, token_rows.astype(jnp.float32))
        grads, row_grads = pull_back(cot_rows.astype(jnp.float32))
        totals = jax.tree.map(lambda first, second: first + second, totals, grads)
        return (totals, (result.astype(jnp.bfloat16), row_grads.astype(jnp.bfloat16)))
    start = jax.tree.map(jnp.zeros_like, params)
    totals, (outputs, input_grads) = lax.scan(one_sequence, start, (tokens, cotangent, segment_ids.astype(jnp.float32)))
    return (outputs, input_grads, totals[0], totals[1], totals[2], totals[3], totals[4], totals[5], totals[6], totals[7], totals[8], totals[9], totals[10])
```

```python
import functools

import jax
import jax.numpy as jnp
from jax import lax
from jax.experimental import pallas as pl
from jax.experimental.pallas import tpu as pltpu
from jax.sharding import PartitionSpec as P

D = 1792
HEADS = 16
FEAT = 16
WIDTH = D // HEADS
LANES = 128
VMEM = 60 * 2**20
EPSILON = 1e-06
BOTH = ("seq", "head")
CORE, SIDE_X, SIDE_Y = 1, 2, 4

f32 = jnp.float32
bf16 = jnp.bfloat16


def grouped(value, multiple):
    return -(-value // multiple) * multiple


def cost(flops):
    return pl.CostEstimate(flops=int(flops), bytes_accessed=1, transcendentals=0)


def dot(left, right):
    return jnp.dot(left, right, preferred_element_type=f32)


def dot_rt(left, right):
    return lax.dot_general(left, right, (((1,), (1,)), ((), ())), preferred_element_type=f32)


def dot_lt(left, right):
    return lax.dot_general(left, right, (((0,), (0,)), ((), ())), preferred_element_type=f32)


def swap(block, bit, axis="seq"):
    devices = range(lax.axis_size(axis))
    return lax.ppermute(block, axis, [(i, i ^ bit) for i in devices])


def paired():
    return lax.axis_size("seq") == 8 and lax.axis_size("head") == 4


def tie(value, *others):
    return lax.optimization_barrier((value, others))[0]


def gather(shard):
    whole = lax.all_gather(shard, BOTH)
    return whole.reshape((lax.axis_size("seq"), lax.axis_size("head")) + shard.shape)


class Pieces:
    def __init__(self, shard):
        self.shard = shard
        self.columns = shard.shape[1]
        if paired():
            self.own = jnp.stack([shard] + [swap(shard, r, "head") for r in (1, 2, 3)])
        else:
            own = lax.all_gather(shard, "head")
            self.own = lax.all_gather(own, "seq", axis=1, tiled=True)
            self.pieces, self.offsets = [(self.own, 0)], jnp.zeros((1,), jnp.int32)

    def sides(self):
        if paired():
            self.by_x, self.by_y = swap(self.own, SIDE_X), swap(self.own, SIDE_Y)
            return self.by_x, self.by_y
        return ()

    def far(self):
        if not paired():
            return
        far_a, far_b = swap(self.by_x[:2], SIDE_Y), swap(self.by_y[2:], SIDE_X)
        mine = [(self.own, 0), (self.by_x, 0), (self.by_y, 0), (far_a, 0), (far_b, 2)]
        self.pieces = mine + [(swap(piece, CORE), start) for piece, start in mine]
        sides = (0, SIDE_X, SIDE_Y, SIDE_X | SIDE_Y, SIDE_X | SIDE_Y)
        sides = sides + tuple(side | CORE for side in sides)
        rows = self.shard.shape[0]
        self.offsets = (lax.axis_index("seq") ^ jnp.array(sides, jnp.int32)) * rows

    @property
    def places(self):
        return self.own.shape[0]

    def reorder(self, blocks):
        if not paired():
            return blocks
        here = lax.axis_index("head")
        pick = lambda r: lax.dynamic_index_in_dim(blocks, here ^ r, 0, keepdims=False)
        return jnp.stack([pick(r) for r in range(4)])

    def specs(self):
        def spec(piece, start):
            last = piece.shape[0] - 1
            return pl.BlockSpec(
                (1,) + piece.shape[1:], lambda z, o: (jnp.clip(z - start, 0, last), 0, 0)
            )

        return [spec(piece, start) for piece, start in self.pieces]

    def fill(self, offsets, refs, weight):
        z = pl.program_id(0)
        for i, (ref, (piece, start)) in enumerate(zip(refs, self.pieces)):
            count, rows, _ = piece.shape

            def put():
                at = pl.multiple_of(offsets[i], 16)
                weight[pl.ds(at, rows)] = ref[0]

            if count == self.places:
                put()
            else:
                pl.when((z >= start) & (z < start + count))(put)


def grad_kernel(first, plane, left0, left1, right0, right1, send, keep, rows0, rows1):
    _, width, tokens = left0.shape

    @pl.when((pl.program_id(0) == 0) & (pl.program_id(1) == 0))
    def _():
        for i in range(4):
            rows0[i * width : (i + 1) * width] = left0[plane[0] ^ i]
            rows1[i * width : (i + 1) * width] = left1[plane[0] ^ i]

    total = dot(rows0[...], right0[0, 0]) + dot(rows1[...], right1[0, 0])
    total = total.astype(bf16)
    far = first // 2
    near = 3 ^ far
    for i, at in enumerate((0, near)):
        keep[i, 0, 0] = total[at * width : (at + 1) * width]
        at ^= far
        send[i, 0, 0] = total[at * width : (at + 1) * width]


def weight_grads(plane, left0, left1, right0, right1, start, first):
    count, kinds, tokens, columns = right0.shape
    count //= 2
    width = left0.shape[1]
    left = pl.BlockSpec(left0.shape, lambda z, k, p: (0, 0, 0))
    right = pl.BlockSpec((1, 1, tokens, columns), lambda z, k, p: (z + start, k, 0, 0))
    out = pl.BlockSpec((2, 1, 1, width, columns), lambda z, k, p: (0, z, k, 0, 0))
    shape = jax.ShapeDtypeStruct((2, count, kinds, width, columns), bf16)
    return pl.pallas_call(
        functools.partial(grad_kernel, first),
        grid_spec=pltpu.PrefetchScalarGridSpec(
            num_scalar_prefetch=1,
            grid=(count, kinds),
            in_specs=[left, left, right, right],
            out_specs=[out, out],
            scratch_shapes=[pltpu.VMEM((4 * width, tokens), bf16)] * 2,
        ),
        out_shape=[shape, shape],
        compiler_params=pltpu.CompilerParams(vmem_limit_bytes=VMEM),
        cost_estimate=cost(count * kinds * 20 * width * tokens * columns),
    )(plane, left0, left1, right0, right1)


class Scatter:
    def __init__(self, left, right, relative=False):
        self.right = right
        self.left = left
        self.relative = relative
        if paired():
            rows = left.T.reshape(4, 2, D // 8, -1)
            core = lax.axis_index("seq") % 2
            pick = lambda c: lax.dynamic_index_in_dim(rows, c, 1, keepdims=False)
            self.left0, self.left1 = pick(core), swap(pick(1 - core), CORE)
            self.other = swap(right, CORE)

    def first(self):
        if not paired():
            return ()
        half = self.right.shape[0] // 2
        plane = (lax.axis_index("seq") // 2).reshape(1)
        self.kept, self.arrived = [], []
        made = []
        for start, side in ((0, SIDE_X), (half, SIDE_Y)):
            send, keep = weight_grads(
                plane, self.left0, self.left1, self.right, self.other, start, side
            )
            made.append(send)
            self.arrived.append(swap(send, side))
            self.kept.append(keep)
        self.coming = self.arrived
        return tuple(made)

    def second(self, *after):
        if not paired():
            return ()
        self.sums, made = [], []
        for keep, arrived, side in zip(self.kept, self.arrived, (SIDE_Y, SIDE_X)):
            if after:
                arrived = tie(arrived, *after)
            go = (keep[1].astype(f32) + arrived[1].astype(f32)).astype(bf16)
            stay = keep[0].astype(f32) + arrived[0].astype(f32)
            made.append(go)
            self.sums.append((stay, swap(go, side)))
        self.coming = [arrived for _, arrived in self.sums]
        return tuple(made)

    def pending(self):
        return tuple(self.coming) if paired() else ()

    def third(self, *after):
        if not paired():
            whole = jnp.einsum(
                "td,hktc->hkdc", self.left, self.right, preferred_element_type=f32
            ).astype(bf16)
            seq = lax.axis_size("seq")
            whole = whole.reshape(whole.shape[:2] + (seq, D // seq, -1))
            part = lax.psum_scatter(whole, "seq", scatter_dimension=2)
            self.total = lax.psum_scatter(part, "head", scatter_dimension=0)
            return ()
        sums = [(stay + arrived.astype(f32)).astype(bf16) for stay, arrived in self.sums]
        sums = jnp.concatenate(sums, axis=0)
        if after:
            sums = tie(sums, *after)
        here = lax.axis_index("head")
        if self.relative:
            pick = lambda r: sums[r]
        else:
            pick = lambda r: lax.dynamic_index_in_dim(sums, here ^ r, 0, keepdims=False)
        sent = [pick(r) for r in (1, 2, 3)]
        self.coming = [swap(block, r, "head") for r, block in zip((1, 2, 3), sent)]
        self.mine = pick(0)
        return tuple(sent)

    def finish(self, *after):
        if not paired():
            return self.total
        coming = self.coming
        if after:
            coming = [tie(block, *after) for block in coming]
        return sum([block.astype(f32) for block in coming], self.mine.astype(f32))


def whole_rows(ref, kind=0):
    block = ref[:, 0, kind]
    return block.reshape(D, block.shape[-1])


def weight_spec(weight, kinds=1, at=0):
    seq, _, _, _, columns = weight.shape
    return pl.BlockSpec((seq, 1, kinds, D // seq, columns), lambda z: (0, z, at, 0, 0))


def into_kernel(x_ref, w_ref, out_ref):
    out_ref[0] = dot(x_ref[...], whole_rows(w_ref)).astype(out_ref.dtype)


def into(x, weight, kind):
    count, columns = weight.shape[1], weight.shape[-1]
    tokens = x.shape[0]
    return pl.pallas_call(
        into_kernel,
        grid=(count,),
        in_specs=[
            pl.BlockSpec(x.shape, lambda z: (0, 0)),
            weight_spec(weight),
        ],
        out_specs=pl.BlockSpec((1, tokens, columns), lambda z: (z, 0, 0)),
        out_shape=jax.ShapeDtypeStruct((count, tokens, columns), kind),
        compiler_params=pltpu.CompilerParams(vmem_limit_bytes=VMEM),
        cost_estimate=cost(count * 3 * D * tokens * columns),
    )(x, weight)


def out_of_kernel(y_ref, w_ref, out_ref):
    @pl.when(pl.program_id(0) == 0)
    def _():
        out_ref[...] = jnp.zeros_like(out_ref)

    out_ref[...] += dot_rt(y_ref[0], whole_rows(w_ref))


def out_of(y, weight):
    count, tokens, columns = y.shape
    return pl.pallas_call(
        out_of_kernel,
        grid=(count,),
        in_specs=[
            pl.BlockSpec((1, tokens, columns), lambda z: (z, 0, 0)),
            weight_spec(weight),
        ],
        out_specs=pl.BlockSpec((tokens, D), lambda z: (0, 0)),
        out_shape=jax.ShapeDtypeStruct((tokens, D), f32),
        compiler_params=pltpu.CompilerParams(vmem_limit_bytes=VMEM),
        cost_estimate=cost(count * 3 * D * tokens * columns),
    )(y, weight)


def into_pieces_kernel(weights, offsets, x_ref, *refs):
    refs, (out_ref, weight) = refs[:-2], refs[-2:]
    weights.fill(offsets, refs, weight)
    out_ref[0] = dot(x_ref[...], weight[...]).astype(out_ref.dtype)


def into_pieces(x, weights, kind):
    count, columns = weights.places, weights.columns
    tokens = x.shape[0]
    return pl.pallas_call(
        functools.partial(into_pieces_kernel, weights),
        grid_spec=pltpu.PrefetchScalarGridSpec(
            num_scalar_prefetch=1,
            grid=(count,),
            in_specs=[pl.BlockSpec(x.shape, lambda z, o: (0, 0))] + weights.specs(),
            out_specs=pl.BlockSpec((1, tokens, columns), lambda z, o: (z, 0, 0)),
            scratch_shapes=[pltpu.VMEM((D, columns), bf16)],
        ),
        out_shape=jax.ShapeDtypeStruct((count, tokens, columns), kind),
        compiler_params=pltpu.CompilerParams(vmem_limit_bytes=VMEM),
        cost_estimate=cost(count * 3 * D * tokens * columns),
    )(weights.offsets, x, *[piece for piece, _ in weights.pieces])


def out_of_pieces_kernel(weights, offsets, y_ref, *refs):
    refs, (out_ref, weight) = refs[:-2], refs[-2:]
    weights.fill(offsets, refs, weight)

    @pl.when(pl.program_id(0) == 0)
    def _():
        out_ref[...] = jnp.zeros_like(out_ref)

    out_ref[...] += dot_rt(y_ref[0], weight[...])


def out_of_pieces(y, weights):
    count, tokens, columns = y.shape
    return pl.pallas_call(
        functools.partial(out_of_pieces_kernel, weights),
        grid_spec=pltpu.PrefetchScalarGridSpec(
            num_scalar_prefetch=1,
            grid=(count,),
            in_specs=[pl.BlockSpec((1, tokens, columns), lambda z, o: (z, 0, 0))]
            + weights.specs(),
            out_specs=pl.BlockSpec((tokens, D), lambda z, o: (0, 0)),
            scratch_shapes=[pltpu.VMEM((D, columns), bf16)],
        ),
        out_shape=jax.ShapeDtypeStruct((tokens, D), f32),
        compiler_params=pltpu.CompilerParams(vmem_limit_bytes=VMEM),
        cost_estimate=cost(count * 3 * D * tokens * columns),
    )(weights.offsets, y, *[piece for piece, _ in weights.pieces])


def ffn_kernel(x_ref, gu_ref, d_ref, slope_ref, silu_ref, hidden_ref, out_ref):
    @pl.when(pl.program_id(0) == 0)
    def _():
        out_ref[...] = jnp.zeros_like(out_ref)

    gate = dot(x_ref[...], whole_rows(gu_ref, 0))
    sig = jax.nn.sigmoid(gate)
    silu = gate * sig
    up = dot(x_ref[...], whole_rows(gu_ref, 1))
    hidden = (silu * up).astype(bf16)
    slope_ref[0] = (up * sig * (1.0 + gate * (1.0 - sig))).astype(bf16)
    silu_ref[0] = silu.astype(bf16)
    columns = hidden.shape[1]
    hidden_ref[0, 0, :, :columns] = hidden
    hidden_ref[0, 0, :, columns:] = jnp.zeros_like(hidden_ref[0, 0, :, columns:])
    out_ref[...] += dot_rt(hidden, whole_rows(d_ref))


def ffn(x, weight):
    count, columns = weight.shape[1], weight.shape[-1]
    padded = grouped(columns, LANES)
    tokens = x.shape[0]
    act = pl.BlockSpec((1, tokens, columns), lambda z: (z, 0, 0))
    kept = jax.ShapeDtypeStruct((count, tokens, columns), bf16)
    return pl.pallas_call(
        ffn_kernel,
        grid=(count,),
        in_specs=[
            pl.BlockSpec(x.shape, lambda z: (0, 0)),
            weight_spec(weight, kinds=2),
            weight_spec(weight, at=2),
        ],
        out_specs=[
            act,
            act,
            pl.BlockSpec((1, 1, tokens, padded), lambda z: (z, 0, 0, 0)),
            pl.BlockSpec((tokens, D), lambda z: (0, 0)),
        ],
        out_shape=[
            kept,
            kept,
            jax.ShapeDtypeStruct((count, 1, tokens, padded), bf16),
            jax.ShapeDtypeStruct((tokens, D), f32),
        ],
        compiler_params=pltpu.CompilerParams(vmem_limit_bytes=VMEM),
        cost_estimate=cost(count * 9 * D * tokens * columns),
    )(x, weight, weight)


def ffn_back_kernel(dy_ref, gu_ref, d_ref, slope_ref, silu_ref, grads_ref, out_ref):
    @pl.when(pl.program_id(0) == 0)
    def _():
        out_ref[...] = jnp.zeros_like(out_ref)

    grad_hidden = dot(dy_ref[...], whole_rows(d_ref))
    grad_gate = (grad_hidden * slope_ref[0].astype(f32)).astype(bf16)
    grad_up = (grad_hidden * silu_ref[0].astype(f32)).astype(bf16)
    columns = grad_gate.shape[1]
    grads_ref[0, 0, :, :columns] = grad_gate
    grads_ref[0, 1, :, :columns] = grad_up
    grads_ref[0, :, :, columns:] = jnp.zeros_like(grads_ref[0, :, :, columns:])
    out_ref[...] += dot_rt(grad_gate, whole_rows(gu_ref, 0)) + dot_rt(
        grad_up, whole_rows(gu_ref, 1)
    )


def ffn_back(dy, weight, slope, silu):
    count, columns = weight.shape[1], weight.shape[-1]
    padded = grouped(columns, LANES)
    tokens = dy.shape[0]
    act = pl.BlockSpec((1, tokens, columns), lambda z: (z, 0, 0))
    return pl.pallas_call(
        ffn_back_kernel,
        grid=(count,),
        in_specs=[
            pl.BlockSpec(dy.shape, lambda z: (0, 0)),
            weight_spec(weight, kinds=2),
            weight_spec(weight, at=2),
            act,
            act,
        ],
        out_specs=[
            pl.BlockSpec((1, 2, tokens, padded), lambda z: (z, 0, 0, 0)),
            pl.BlockSpec((tokens, D), lambda z: (0, 0)),
        ],
        out_shape=[
            jax.ShapeDtypeStruct((count, 2, tokens, padded), bf16),
            jax.ShapeDtypeStruct((tokens, D), f32),
        ],
        compiler_params=pltpu.CompilerParams(vmem_limit_bytes=VMEM),
        cost_estimate=cost(count * 9 * D * tokens * columns),
    )(dy, weight, weight, slope, silu)


def inverse_rms(rows):
    return lax.rsqrt(jnp.mean(rows * rows, axis=-1, keepdims=True) + EPSILON)


def norm_back(rows, scale, gain, grad):
    unit = rows * scale
    scaled = gain * grad
    return scale * (scaled - unit * jnp.mean(scaled * unit, axis=-1, keepdims=True))


class Layout:
    def __init__(self, batch, tokens):
        seq, head = lax.axis_size("seq"), lax.axis_size("head")
        self.batch, self.tokens, self.head = batch, tokens, head
        self.splits = min(seq // batch, HEADS // head)
        self.heads = HEADS // (head * self.splits)
        self.parts = seq // (batch * self.splits)
        self.inner = seq // self.parts
        self.v_cols, self.q_cols = self.heads * WIDTH, self.heads * FEAT
        self.width = grouped(self.v_cols + self.q_cols, LANES)
        self.sets = self.width // self.q_cols
        self.key_rows = grouped(tokens // self.sets, 16)
        self.length = tokens * seq * head
        count = self.inner * head
        self.groups = None
        if self.parts > 1:
            self.groups = [list(range(k * count, (k + 1) * count)) for k in range(self.parts)]
            self.mates = [[k * count + i for k in range(self.parts)] for i in range(count)]

    def sequence(self):
        return lax.rem(lax.axis_index("seq"), self.inner) // self.splits

    def pack_keys(self, keys):
        lead, each = keys.shape[:-2], self.tokens // self.sets
        keys = keys.reshape(lead + (self.sets, each, self.q_cols))
        keys = jnp.swapaxes(keys, -3, -2).reshape(lead + (each, self.width))
        return jnp.pad(keys, [(0, 0)] * len(lead) + [(0, self.key_rows - each), (0, 0)])

    def unpack_keys(self, rows):
        lead, each = rows.shape[:-2], self.tokens // self.sets
        rows = rows[..., :each, :].reshape(lead + (each, self.sets, self.q_cols))
        return jnp.swapaxes(rows, -3, -2).reshape(lead + (self.tokens, self.q_cols))

    def exchange(self, blocks):
        return lax.all_to_all(blocks, BOTH, 0, 0, tiled=True, axis_index_groups=self.groups)

    def all_parts(self, rows):
        if self.parts > 1:
            rows = lax.all_gather(rows, BOTH, axis=0, tiled=True, axis_index_groups=self.mates)
        return rows

    def own_part(self, blocks):
        if self.parts > 1:
            count = blocks.shape[0] // self.parts
            part = lax.axis_index("seq") // self.inner
            blocks = lax.dynamic_slice_in_dim(blocks, part * count, count, 0)
        return blocks


def fill_rows(lay, chunk, main, k_ref, values, queries, keys):
    ones = lax.broadcasted_iota(jnp.int32, (chunk, LANES - WIDTH), 1) < 2

    def turn(i, _):
        here = pl.ds(pl.multiple_of(i * chunk, chunk), chunk)
        rows, key_rows = main[here], k_ref[here]
        for h in range(lay.heads):
            values[h, here, :WIDTH] = rows[:, h * WIDTH : (h + 1) * WIDTH]
            values[h, here, WIDTH:] = ones.astype(f32).astype(bf16)
            at = lay.v_cols + h * FEAT
            queries[h, here] = rows[:, at : at + FEAT]
            keys[h, here] = key_rows[:, h * FEAT : (h + 1) * FEAT]
        return 0

    lax.fori_loop(0, lay.length // chunk, turn, 0)


def attend_kernel(
    lay, chunk, main, k_ref, seg_col, seg_row, out_ref, low_ref, values, queries, keys
):
    at = pl.program_id(0)

    @pl.when(at == 0)
    def _():
        fill_rows(lay, chunk, main, k_ref, values, queries, keys)

    mine = seg_col[...]
    rows = pl.ds(pl.multiple_of(at * chunk, chunk), chunk)
    out_ref[...] = jnp.zeros_like(out_ref)
    low_ref[...] = jnp.zeros_like(low_ref)
    for h in range(lay.heads):
        query = queries[h, rows]

        def weighted(j, causal):
            here = pl.ds(pl.multiple_of(j * chunk, chunk), chunk)
            scores = dot_rt(query, keys[h, here])
            allowed = mine == seg_row[j]
            if causal:
                later = lax.broadcasted_iota(jnp.int32, scores.shape, 0)
                allowed &= later >= lax.broadcasted_iota(jnp.int32, scores.shape, 1)
            weights = jnp.where(allowed, 1.0 + scores * (1.0 + 0.5 * scores), 0.0).astype(bf16)
            return dot(weights, values[h, here])

        total = lax.fori_loop(
            0, at, lambda j, acc: acc + weighted(j, False), jnp.zeros((chunk, LANES), f32)
        )
        total = total + weighted(at, True)
        norm = total[:, WIDTH : WIDTH + 1]
        attended = total[:, :WIDTH] / norm
        out_ref[:, h * WIDTH : (h + 1) * WIDTH] = attended
        out_ref[:, lay.v_cols + h : lay.v_cols + h + 1] = norm
        low_ref[:, h * WIDTH : (h + 1) * WIDTH] = attended.astype(bf16)


def attend(lay, main, keys, seg):
    length, width = main.shape
    chunk = min(512, length)
    steps = length // chunk
    part = pl.BlockSpec((chunk, width), lambda i: (i, 0))
    return pl.pallas_call(
        functools.partial(attend_kernel, lay, chunk),
        grid=(steps,),
        in_specs=[
            pl.BlockSpec((length, width), lambda i: (0, 0)),
            pl.BlockSpec((length, lay.q_cols), lambda i: (0, 0)),
            pl.BlockSpec((chunk, 1), lambda i: (i, 0)),
            pl.BlockSpec((steps, 1, chunk), lambda i: (0, 0, 0)),
        ],
        out_specs=[part, part],
        out_shape=[
            jax.ShapeDtypeStruct((length, width), f32),
            jax.ShapeDtypeStruct((length, width), bf16),
        ],
        scratch_shapes=[
            pltpu.VMEM((lay.heads, length, LANES), bf16),
            pltpu.VMEM((lay.heads, length, FEAT), bf16),
            pltpu.VMEM((lay.heads, length, FEAT), bf16),
        ],
        compiler_params=pltpu.CompilerParams(vmem_limit_bytes=VMEM),
        cost_estimate=cost(lay.heads * length * length * 12 * LANES),
    )(main, keys, seg.reshape(length, 1), seg.reshape(steps, 1, chunk))


def attend_back_kernel(
    lay,
    chunk,
    main,
    k_ref,
    kept,
    grad,
    seg_col,
    seg_row,
    out_ref,
    gk_ref,
    values,
    queries,
    keys,
    grad_n,
    grad_q,
):
    at = pl.program_id(0)
    steps = lay.length // chunk

    @pl.when(at == 0)
    def _():
        fill_rows(lay, chunk, main, k_ref, values, queries, keys)
        grad_q[...] = jnp.zeros_like(grad_q)

        def turn(i, _):
            here = pl.ds(pl.multiple_of(i * chunk, chunk), chunk)
            rows, low = kept[here], grad[here].astype(f32)
            for h in range(lay.heads):
                inverse = 1.0 / rows[:, lay.v_cols + h : lay.v_cols + h + 1]
                mine = low[:, h * WIDTH : (h + 1) * WIDTH]
                total = jnp.sum(
                    mine * rows[:, h * WIDTH : (h + 1) * WIDTH], axis=1, keepdims=True
                )
                total = -total * inverse
                high = total.astype(bf16)
                rest = (total - high.astype(f32)).astype(bf16)
                lane = lax.broadcasted_iota(jnp.int32, (chunk, LANES - WIDTH), 1)
                tail = jnp.where(lane == 0, high.astype(f32), 0.0)
                tail = jnp.where(lane == 1, rest.astype(f32), tail)
                grad_n[h, here, :WIDTH] = (mine * inverse).astype(bf16)
                grad_n[h, here, WIDTH:] = tail.astype(bf16)
            return 0

        lax.fori_loop(0, steps, turn, 0)

    mine = seg_col[...]
    rows = pl.ds(pl.multiple_of(at * chunk, chunk), chunk)
    for h in range(lay.heads):
        key, value = keys[h, rows], values[h, rows]
        key_t = key.astype(f32).T.astype(bf16)

        def turn(i, carry, causal):
            grad_k, grad_v = carry
            here = pl.ds(pl.multiple_of(i * chunk, chunk), chunk)
            query, grad_here = queries[h, here], grad_n[h, here]
            scores = dot_rt(key, query)
            allowed = mine == seg_row[i]
            if causal:
                key_at = lax.broadcasted_iota(jnp.int32, scores.shape, 0)
                allowed &= key_at <= lax.broadcasted_iota(jnp.int32, scores.shape, 1)
            weights = jnp.where(allowed, 1.0 + scores * (1.0 + 0.5 * scores), 0.0).astype(bf16)
            grad_s = dot_rt(value, grad_here) * (1.0 + scores)
            grad_s = jnp.where(allowed, grad_s, 0.0).astype(bf16)
            grad_q[h, :, here] += dot(key_t, grad_s)
            return grad_k + dot(grad_s, query), grad_v + dot(weights, grad_here)

        carry = (jnp.zeros((chunk, FEAT), f32), jnp.zeros((chunk, LANES), f32))
        carry = turn(at, carry, True)
        grad_k, grad_v = lax.fori_loop(at + 1, steps, lambda i, c: turn(i, c, False), carry)
        gk_ref[:, h * FEAT : (h + 1) * FEAT] = (0.5 * grad_k).astype(bf16)
        out_ref[rows, h * WIDTH : (h + 1) * WIDTH] = grad_v[:, :WIDTH].astype(bf16)

    @pl.when(at == steps - 1)
    def _():
        def turn(i, _):
            here = pl.ds(pl.multiple_of(i * chunk, chunk), chunk)
            for h in range(lay.heads):
                at = lay.v_cols + h * FEAT
                out_ref[here, at : at + FEAT] = (0.5 * grad_q[h, :, here].T).astype(bf16)
            return 0

        lax.fori_loop(0, steps, turn, 0)


def attend_back(lay, main, keys, kept, grad, seg):
    length, width = main.shape
    chunk = min(512, length)
    steps = length // chunk
    whole = pl.BlockSpec((length, width), lambda i: (0, 0))
    return pl.pallas_call(
        functools.partial(attend_back_kernel, lay, chunk),
        grid=(steps,),
        in_specs=[
            whole,
            pl.BlockSpec((length, lay.q_cols), lambda i: (0, 0)),
            whole,
            whole,
            pl.BlockSpec((chunk, 1), lambda i: (i, 0)),
            pl.BlockSpec((steps, 1, chunk), lambda i: (0, 0, 0)),
        ],
        out_specs=[whole, pl.BlockSpec((chunk, lay.q_cols), lambda i: (i, 0))],
        out_shape=[
            jax.ShapeDtypeStruct((length, width), bf16),
            jax.ShapeDtypeStruct((length, lay.q_cols), bf16),
        ],
        scratch_shapes=[
            pltpu.VMEM((lay.heads, length, LANES), bf16),
            pltpu.VMEM((lay.heads, length, FEAT), bf16),
            pltpu.VMEM((lay.heads, length, FEAT), bf16),
            pltpu.VMEM((lay.heads, length, LANES), bf16),
            pltpu.VMEM((lay.heads, FEAT, length), f32),
        ],
        compiler_params=pltpu.CompilerParams(vmem_limit_bytes=VMEM),
        cost_estimate=cost(lay.heads * length * length * 24 * LANES),
    )(main, keys, kept, grad, seg.reshape(length, 1), seg.reshape(steps, 1, chunk))


def earlier(rows, before, distance):
    moved = pltpu.roll(rows, distance, 0)
    place = lax.broadcasted_iota(jnp.int32, rows.shape, 0)
    for i in range(distance):
        at = 2 - distance + i
        moved = jnp.where(place == i, before[at : at + 1], moved)
    return moved


def later(rows, after, distance):
    count = rows.shape[0]
    moved = pltpu.roll(rows, count - distance, 0)
    place = lax.broadcasted_iota(jnp.int32, rows.shape, 0)
    for i in range(distance):
        moved = jnp.where(place == count - distance + i, after[i : i + 1], moved)
    return moved


def short_filter(taps, same, values, before):
    one_back = earlier(values, before, 1) * same[:, 0:1]
    two_back = earlier(values, before, 2) * same[:, 1:2]
    return taps[0:1] * values + taps[1:2] * one_back + taps[2:3] * two_back, one_back, two_back


def project_kernel(lay, x_ref, side_ref, same_ref, taps_ref, w_ref, main, k_ref, v_ref, f_ref, side_out):
    weight = whole_rows(w_ref)
    q_width = lay.splits * lay.q_cols
    v_at, f_at = 2 * q_width, 2 * q_width + lay.splits * lay.v_cols
    full = dot(x_ref[...], weight)
    side = dot(side_ref[...], weight)
    low = full[:, v_at:f_at].astype(bf16)
    v_ref[0] = low
    f_ref[0] = full[:, f_at:]
    side_v = side[:, v_at:f_at].astype(bf16).astype(f32)
    side_out[0, 0] = side_v
    side_out[0, 1] = side[:, f_at:]
    taps = taps_ref[0]
    for b in range(lay.batch):
        rows = slice(b * lay.tokens, (b + 1) * lay.tokens)
        pre = full[rows, f_at:]
        filtered, _, _ = short_filter(
            taps, same_ref[rows], low[rows].astype(f32), side_v[2 * b : 2 * b + 2]
        )
        mixed = filtered * (pre * jax.nn.sigmoid(pre))
        query = 0.5 * full[rows, :q_width].astype(bf16).astype(f32)
        key = 0.5 * full[rows, q_width:v_at].astype(bf16).astype(f32)
        for i in range(lay.splits):
            v_cols, q_cols = lay.v_cols, lay.q_cols
            main[b, i, 0, :, :v_cols] = mixed[:, i * v_cols : (i + 1) * v_cols].astype(bf16)
            q_here = query[:, i * q_cols : (i + 1) * q_cols].astype(bf16)
            main[b, i, 0, :, v_cols : v_cols + q_cols] = q_here
            k_ref[b, i, 0] = key[:, i * q_cols : (i + 1) * q_cols].astype(bf16)


def project(lay, x, side, same, taps, weight):
    tokens, head = x.shape[0], lay.head
    q_width, v_width = lay.splits * lay.q_cols, lay.splits * lay.v_cols
    columns = 2 * (q_width + v_width)
    beside = side.shape[0]
    to_all = lambda width: pl.BlockSpec(
        (lay.batch, lay.splits, 1, lay.tokens, width), lambda z: (0, 0, z, 0, 0)
    )
    shape = lambda width: jax.ShapeDtypeStruct(
        (lay.batch, lay.splits, head, lay.tokens, width), bf16
    )
    kept = pl.BlockSpec((1, tokens, v_width), lambda z: (z, 0, 0))
    return pl.pallas_call(
        functools.partial(project_kernel, lay),
        grid=(head,),
        in_specs=[
            pl.BlockSpec(x.shape, lambda z: (0, 0)),
            pl.BlockSpec(side.shape, lambda z: (0, 0)),
            pl.BlockSpec(same.shape, lambda z: (0, 0)),
            pl.BlockSpec((1, 3, v_width), lambda z: (z, 0, 0)),
            weight_spec(weight),
        ],
        out_specs=[
            to_all(lay.width),
            to_all(lay.q_cols),
            kept,
            kept,
            pl.BlockSpec((1, 2, beside, v_width), lambda z: (z, 0, 0, 0)),
        ],
        out_shape=[
            shape(lay.width),
            shape(lay.q_cols),
            jax.ShapeDtypeStruct((head, tokens, v_width), bf16),
            jax.ShapeDtypeStruct((head, tokens, v_width), f32),
            jax.ShapeDtypeStruct((head, 2, beside, v_width), f32),
        ],
        compiler_params=pltpu.CompilerParams(vmem_limit_bytes=VMEM),
        cost_estimate=cost(head * 3 * D * tokens * columns),
    )(x, side, same, taps, weight)


def project_back_kernel(
    lay, back_ref, gk_ref, v_ref, f_ref, side_ref, same_ref, taps_ref, out_ref, tap_ref, mixed, after
):
    q_width = lay.splits * lay.q_cols
    v_at, f_at = 2 * q_width, 2 * q_width + lay.splits * lay.v_cols
    v_cols, q_cols = lay.v_cols, lay.q_cols
    taps = taps_ref[0]
    below = lay.tokens + lay.key_rows
    tap_ref[...] = jnp.zeros_like(tap_ref)
    out_ref[0, :, q_width:v_at] = gk_ref[0]
    for b in range(lay.batch):
        rows = slice(b * lay.tokens, (b + 1) * lay.tokens)
        for i in range(lay.splits):
            block = back_ref[b, i, 0, : lay.tokens]
            mixed[:, i * v_cols : (i + 1) * v_cols] = block[:, :v_cols].astype(f32)
            out_ref[0, rows, i * q_cols : (i + 1) * q_cols] = block[:, v_cols : v_cols + q_cols]
            after[:, i * v_cols : (i + 1) * v_cols] = back_ref[
                b, i, 0, below : below + 16, :v_cols
            ].astype(f32)
        grad_mixed = mixed[...]
        pre = f_ref[0, rows]
        sig = jax.nn.sigmoid(pre)
        values = v_ref[0, rows].astype(f32)
        same = same_ref[rows]
        at = 2 * b
        filtered, one_back, two_back = short_filter(
            taps, same, values, side_ref[0, 0, at : at + 2]
        )
        grad = grad_mixed * pre * sig
        at = 2 * (lay.batch + b)
        pre_after = side_ref[0, 1, at : at + 2]
        grad_after = after[0:2] * pre_after * jax.nn.sigmoid(pre_after)
        grad_v = (
            taps[0:1] * grad
            + taps[1:2] * later(grad, grad_after, 1) * same[:, 2:3]
            + taps[2:3] * later(grad, grad_after, 2) * same[:, 3:4]
        )
        out_ref[0, rows, v_at:f_at] = grad_v.astype(bf16)
        grad_f = grad_mixed * filtered * sig * (1.0 + pre * (1.0 - sig))
        out_ref[0, rows, f_at:] = grad_f.astype(bf16)
        for k, term in enumerate((values, one_back, two_back)):
            tap_ref[0, k : k + 1] += jnp.sum(grad * term, axis=0, keepdims=True)


def project_back(lay, back, grad_keys, values, pre, side, same, taps):
    head, tokens, v_width = values.shape
    columns = 2 * (lay.splits * lay.q_cols + v_width)
    kept = pl.BlockSpec((1, tokens, v_width), lambda z: (z, 0, 0))
    return pl.pallas_call(
        functools.partial(project_back_kernel, lay),
        grid=(head,),
        in_specs=[
            pl.BlockSpec(
                (lay.batch, lay.splits, 1) + back.shape[3:], lambda z: (0, 0, z, 0, 0)
            ),
            pl.BlockSpec((1,) + grad_keys.shape[1:], lambda z: (z, 0, 0)),
            kept,
            kept,
            pl.BlockSpec((1,) + side.shape[1:], lambda z: (z, 0, 0, 0)),
            pl.BlockSpec(same.shape, lambda z: (0, 0)),
            pl.BlockSpec((1, 3, v_width), lambda z: (z, 0, 0)),
        ],
        out_specs=[
            pl.BlockSpec((1, tokens, columns), lambda z: (z, 0, 0)),
            pl.BlockSpec((1, 3, v_width), lambda z: (z, 0, 0)),
        ],
        out_shape=[
            jax.ShapeDtypeStruct((head, tokens, columns), bf16),
            jax.ShapeDtypeStruct((head, 3, v_width), f32),
        ],
        scratch_shapes=[
            pltpu.VMEM((lay.tokens, v_width), f32),
            pltpu.VMEM((16, v_width), f32),
        ],
        compiler_params=pltpu.CompilerParams(vmem_limit_bytes=VMEM),
        cost_estimate=cost(head * 2500 * tokens * columns),
    )(back, grad_keys, values, pre, side, same, taps)


def shift(block, distance):
    devices = range(lax.axis_size("seq") * lax.axis_size("head"))
    return lax.ppermute(
        block, BOTH, [(i, i + distance) for i in devices if i + distance in devices]
    )


def local(
    tokens,
    cotangent,
    segment_ids,
    query_weight,
    key_weight,
    value_weight,
    filter_weight,
    out_weight,
    gate_weight,
    up_weight,
    down_weight,
    norm_gain,
    ffn_gain,
    conv_taps,
):
    seq, head = lax.axis_size("seq"), lax.axis_size("head")
    batch, span, _ = tokens.shape
    count = batch * span
    length = segment_ids.shape[1] * seq
    place = lax.axis_index("seq") * head + lax.axis_index("head")
    heads_here = HEADS // head
    qk_width, v_width = heads_here * FEAT, heads_here * WIDTH
    ff_width = gate_weight.shape[1]

    lay = Layout(batch, span)
    out_pad = grouped(v_width, LANES) - v_width
    first = jnp.concatenate([query_weight, key_weight, value_weight, filter_weight], axis=1)
    rows_here, columns = first.shape
    small = [norm_gain, ffn_gain, conv_taps.reshape(-1), segment_ids.astype(bf16).reshape(-1)]
    ends = [0]
    for part in small:
        ends.append(ends[-1] + part.size)
    below = grouped(-(-ends[-1] // columns), 16)
    small = jnp.pad(jnp.concatenate(small), (0, below * columns - ends[-1]))
    first_w = gather(jnp.concatenate([first, small.reshape(below, columns)])[None])
    out_w = Pieces(jnp.pad(out_weight.T, ((0, 0), (0, out_pad))))
    out_w.sides()
    out_w.far()
    ffn_w = gather(jnp.stack([gate_weight, up_weight, down_weight]))
    beside = jnp.concatenate([shift(tokens[:, -2:], 1), shift(tokens[:, :2], -1)], axis=0)

    small = first_w[:, :, 0, rows_here:].reshape(seq, head, -1).astype(f32)
    part = lambda i: small[:, :, ends[i] : ends[i + 1]]
    gain_one, gain_two = part(0)[:, 0].reshape(1, D), part(1)[:, 0].reshape(1, D)
    taps = jnp.transpose(part(2).reshape(seq, head, 3, -1), (1, 2, 0, 3))
    taps = taps.reshape(head, 3, v_width)
    segs = jnp.swapaxes(part(3)[:, 0].reshape(seq, batch, -1), 0, 1).reshape(batch, length)
    x = tokens.reshape(count, D).astype(f32)
    cot_low = cotangent.reshape(count, D)

    def normed_of(rows):
        scale = inverse_rms(rows)
        return scale, (rows * scale * gain_one).astype(bf16)

    scale_one, normed = normed_of(x)
    _, normed_beside = normed_of(beside.reshape(-1, D).astype(f32))
    around = lax.dynamic_slice(
        jnp.pad(segs, ((0, 0), (2, 2)), constant_values=-1.0),
        (0, place * span),
        (batch, span + 4),
    )
    seg_here = around[:, 2:-2]
    others = (around[:, 1:-3], around[:, :-4], around[:, 3:-1], around[:, 4:])
    same = jnp.stack([(seg_here == other).astype(f32) for other in others], axis=-1)
    same = same.reshape(count, 4)
    normed = tie(normed, *[piece for piece, _ in out_w.pieces])
    main, keys, v_low, filter_pre, side = project(lay, normed, normed_beside, same, taps, first_w)
    arrived = jnp.concatenate([main, lay.pack_keys(keys)], axis=3)
    arrived = lay.exchange(arrived.reshape(-1, span + lay.key_rows, lay.width))
    main = lay.all_parts(arrived[:, :span].reshape(-1, lay.width))
    keys = lay.all_parts(lay.unpack_keys(arrived[:, span:]).reshape(-1, lay.q_cols))
    my_seg = lax.dynamic_index_in_dim(segs, lay.sequence(), 0, keepdims=False)
    attended, sent = attend(lay, main, keys, my_seg)
    arrived = lay.exchange(lay.own_part(sent.reshape(-1, span, lay.width)))

    def side_by_side(blocks, width):
        blocks = blocks.reshape(batch, lay.splits, head, span, -1)[..., :width]
        blocks = [blocks[:, i] for i in range(lay.splits)]
        return jnp.swapaxes(jnp.concatenate(blocks, axis=-1), 0, 1).reshape(head, count, -1)

    att_low = side_by_side(arrived, lay.v_cols)
    out_wide = lambda rows: jnp.pad(rows, ((0, 0), (0, 0), (0, out_pad)))
    att_low = out_w.reorder(out_wide(att_low))

    residual = x + out_of_pieces(att_low, out_w)
    scale_two = inverse_rms(residual)
    normed_two = (residual * scale_two * gain_two).astype(bf16)
    slope, silu, hidden, ffn_out = ffn(normed_two, ffn_w)
    layer_output = (residual + ffn_out).astype(bf16).reshape(tokens.shape)

    down_sum = Scatter(cot_low, hidden)
    grads_gu, back_two = ffn_back(cot_low, ffn_w, slope, silu)
    gate_up_sum = Scatter(normed_two, grads_gu)
    down_sends = down_sum.first()
    gain_two_grad = jnp.sum(back_two * residual * scale_two, axis=0)
    grad_residual = cot_low.astype(f32) + norm_back(residual, scale_two, gain_two, back_two)
    grad_res_low = grad_residual.astype(bf16)
    out_sum = Scatter(grad_res_low, att_low[:, None], True)

    grad_att = out_w.reorder(into_pieces(grad_res_low, out_w, bf16))
    sent = jnp.stack(
        [
            grad_att[..., i * lay.v_cols : (i + 1) * lay.v_cols].reshape(head, batch, span, -1)
            for i in range(lay.splits)
        ]
    )
    sent = jnp.pad(sent, [(0, 0)] * 4 + [(0, lay.width - lay.v_cols)])
    sent = jnp.transpose(sent, (2, 0, 1, 3, 4)).reshape(-1, span, lay.width)
    arrived = lay.exchange(tie(sent, *down_sends))
    gate_up_sends = gate_up_sum.first()
    out_sends = out_sum.first()
    grad_rows = lay.all_parts(arrived.reshape(-1, lay.width))
    grad_rows = tie(grad_rows, *gate_up_sends, *out_sends, *down_sum.pending())
    down_sends = down_sum.second()
    grad_rows = tie(grad_rows, *down_sends)
    grad_main, grad_keys = attend_back(lay, main, keys, attended, grad_rows, my_seg)
    grad_main = tie(grad_main, *gate_up_sum.pending(), *out_sum.pending(), *down_sum.pending())
    blocks = grad_main.reshape(-1, span, lay.width)
    ahead = jnp.pad(blocks[1:, :16], ((0, 1), (0, 0), (0, 0)))
    packed = lay.pack_keys(grad_keys.reshape(-1, span, lay.q_cols))
    sent = jnp.concatenate([blocks, packed, ahead], axis=1)
    arrived = lay.exchange(lay.own_part(sent))
    gate_up_sum.second(grad_main)
    out_sum.second(grad_main)
    arrived = tie(arrived, *gate_up_sum.pending(), *out_sum.pending())
    gate_up_sends = gate_up_sum.third(arrived)
    down_sends = down_sum.third(arrived)
    out_sends = out_sum.third(arrived)
    arrived = tie(arrived, *gate_up_sends, *out_sends, *down_sends)

    grad_keys = lay.unpack_keys(arrived[:, span : span + lay.key_rows])
    grad_keys = side_by_side(grad_keys, lay.q_cols)
    arrived = arrived.reshape((batch, lay.splits, head) + arrived.shape[1:])
    grad_first, tap_grads = project_back(
        lay, arrived, grad_keys, v_low, filter_pre, side, same, taps
    )
    tap_grads = jnp.swapaxes(tap_grads, 0, 1).reshape(3, D)
    first_sum = Scatter(normed, grad_first[:, None])
    first_sends = first_sum.first()
    back_one = out_of(tie(grad_first, *first_sends), first_w)
    gain_one_grad = jnp.sum(back_one * x * scale_one, axis=0)
    first_sends = first_sum.second(back_one)
    first_sum.third()
    gate_up_grad = gate_up_sum.finish(*first_sends)
    down_grad = down_sum.finish(*first_sends)
    out_grad = out_sum.finish(*first_sends)
    first_grad = first_sum.finish()[0].astype(f32)
    grad_x = (grad_residual + norm_back(x, scale_one, gain_one, back_one)).astype(bf16)
    tokens_grad = grad_x.reshape(tokens.shape)

    small = jnp.concatenate([jnp.stack([gain_one_grad, gain_two_grad]), tap_grads], axis=0)
    small = jnp.swapaxes(small.reshape(5, head * seq, -1), 0, 1)
    small = lax.all_to_all(small, ("head", "seq"), 0, 0, tiled=True)
    small = jnp.sum(small, axis=0)

    q_end, k_end, v_end = qk_width, 2 * qk_width, 2 * qk_width + v_width
    return (
        layer_output,
        tokens_grad,
        first_grad[:, :q_end],
        first_grad[:, q_end:k_end],
        first_grad[:, k_end:v_end],
        first_grad[:, v_end:],
        out_grad[0][:, :v_width].astype(f32).T,
        gate_up_grad[0][:, :ff_width].astype(f32),
        gate_up_grad[1][:, :ff_width].astype(f32),
        down_grad[0][:, :ff_width].astype(f32),
        small[0],
        small[1],
        small[2:],
    )


def solution(mesh):
    rows = P(None, BOTH, None)
    return jax.shard_map(
        local,
        mesh=mesh,
        in_specs=(
            rows,
            rows,
            P(None, "seq"),
            P("seq", "head"),
            P("seq", "head"),
            P("seq", "head"),
            P("seq", "head"),
            P("head", "seq"),
            P("seq", "head"),
            P("seq", "head"),
            P("seq", "head"),
            P("seq"),
            P("seq"),
            P(None, ("head", "seq")),
        ),
        out_specs=(
            rows,
            rows,
            P("seq", "head"),
            P("seq", "head"),
            P("seq", "head"),
            P("seq", "head"),
            P("head", "seq"),
            P("seq", "head"),
            P("seq", "head"),
            P("seq", "head"),
            P(("head", "seq")),
            P(("head", "seq")),
            P(None, ("head", "seq")),
        ),
        check_vma=False,
    )
```

```python
import functools

import jax
import jax.numpy as jnp
from jax import lax
from jax.experimental import pallas as pl
from jax.experimental.pallas import tpu as pltpu
from jax.sharding import PartitionSpec as P

D = 1792
HEADS = 16
FEAT = 16
WIDTH = D // HEADS
LANES = 128
VMEM = 60 * 2**20
EPSILON = 1e-06
BOTH = ("seq", "head")
CORE, SIDE_X, SIDE_Y = 1, 2, 4

f32 = jnp.float32
bf16 = jnp.bfloat16
MESH = pl.DeviceIdType.MESH


def grouped(value, multiple):
    return -(-value // multiple) * multiple


def cost(flops):
    return pl.CostEstimate(flops=int(flops), bytes_accessed=1, transcendentals=0)


def dot(left, right):
    return jnp.dot(left, right, preferred_element_type=f32)


def dot_rt(left, right):
    return lax.dot_general(left, right, (((1,), (1,)), ((), ())), preferred_element_type=f32)


def dot_lt(left, right):
    return lax.dot_general(left, right, (((0,), (0,)), ((), ())), preferred_element_type=f32)


def swap(block, bit, axis="seq"):
    devices = range(lax.axis_size(axis))
    return lax.ppermute(block, axis, [(i, i ^ bit) for i in devices])


def paired():
    return lax.axis_size("seq") == 8 and lax.axis_size("head") == 4


def tie(value, *others):
    return lax.optimization_barrier((value, others))[0]


def gather(shard):
    whole = lax.all_gather(shard, BOTH)
    return whole.reshape((lax.axis_size("seq"), lax.axis_size("head")) + shard.shape)


def by_place(blocks):
    if not paired():
        return blocks
    here = lax.axis_index("head")
    if blocks.ndim == 1:
        return blocks ^ here
    pick = lambda r: lax.dynamic_index_in_dim(blocks, here ^ r, 0, keepdims=False)
    return jnp.stack([pick(r) for r in range(4)])


def flipped(here, bit):
    return here + bit - 2 * bit * ((here // bit) % 2)


def gather_kernel(shard, edge, *refs):
    count = (len(refs) - 9) // 2
    others, (whole, edges), rest = refs[:count], refs[count : count + 2], refs[count + 2 :]
    lined, (send, recv, local, line_send, line_recv, edge_send, edge_recv) = (
        rest[:count],
        rest[count:],
    )
    place, line = lax.axis_index("seq"), lax.axis_index("head")
    seq, head = lax.axis_size("seq"), lax.axis_size("head")
    lines = [line, flipped(line, 1), flipped(line, 2), 3 - line]
    by_x, by_y, by_core = (flipped(place, bit) for bit in (SIDE_X, SIDE_Y, CORE))
    corner = flipped(by_x, SIDE_Y)
    to = lambda at, z: {"seq": at, "head": z}
    linear = place * head + line
    after, before = (linear + 1) % (seq * head), (linear + seq * head - 1) % (seq * head)
    sides = [to(at // head, at % head) for at in (after, before)]
    partners = [to(place, z) for z in lines[1:]] + [to(at, line) for at in (by_x, by_y, by_core)]
    partners += sides

    barrier = pltpu.get_barrier_semaphore()
    for partner in partners:
        pl.semaphore_signal(barrier, inc=1, device_id=partner, device_id_type=MESH)
    pl.semaphore_wait(barrier, len(partners))

    def remote(source, target, send_sem, recv_sem, partner):
        return pltpu.make_async_remote_copy(
            src_ref=source,
            dst_ref=target,
            send_sem=send_sem,
            recv_sem=recv_sem,
            device_id=partner,
            device_id_type=MESH,
        )

    copies = [pltpu.make_async_copy(shard, whole.at[place, line, 0], local.at[0])]
    copies += [
        pltpu.make_async_copy(other, target.at[0], local.at[1 + i])
        for i, (other, target) in enumerate(zip(others, lined))
    ]
    started = {}

    def start(row, r, source, at, z, partner):
        started[row, r] = remote(
            source, whole.at[at, z, 0], send.at[row, r], recv.at[row, r], partner
        )
        started[row, r].start()

    for r in (1, 2, 3):
        start(0, r, shard, place, line, to(place, lines[r]))
    copies += [
        remote(edge, edges.at[i], edge_send.at[i], edge_recv.at[i], partner)
        for i, partner in enumerate(sides)
    ]
    for each in copies:
        each.start()
    for r in range(4):
        if r > 0:
            started[0, r].wait_recv()
        source = shard if r == 0 else whole.at[place, lines[r], 0]
        start(1, r, source, place, lines[r], to(by_x, line))
        start(2, r, source, place, lines[r], to(by_y, line))
        start(3, r, source, place, lines[r], to(by_core, line))
    more = [
        remote(other, target.at[r], line_send.at[i, r], line_recv.at[i, r], to(place, lines[r]))
        for i, (other, target) in enumerate(zip(others, lined))
        for r in (1, 2, 3)
    ]
    for each in more:
        each.start()
    for r in range(4):
        z = lines[r]
        started[1, r].wait_recv()
        if r < 2:
            start(4, r, whole.at[by_x, z, 0], by_x, z, to(by_y, line))
        start(5, r, whole.at[by_x, z, 0], by_x, z, to(by_core, line))
        started[2, r].wait_recv()
        if r >= 2:
            start(4, r, whole.at[by_y, z, 0], by_y, z, to(by_x, line))
        start(6, r, whole.at[by_y, z, 0], by_y, z, to(by_core, line))
    for r in range(4):
        z = lines[r]
        started[4, r].wait_recv()
        start(7, r, whole.at[corner, z, 0], corner, z, to(by_core, line))
    for (row, r), each in started.items():
        each.wait_send()
        if row in (3, 5, 6, 7):
            each.wait_recv()
    for each in copies + more:
        each.wait()


def gather_first(shard, edge, others):
    seq, head = lax.axis_size("seq"), lax.axis_size("head")
    if not paired():
        return gather(shard[None]), jnp.stack([shift(edge, 1), shift(edge, -1)]), [None] * len(others)
    anywhere = pl.BlockSpec(memory_space=pl.ANY)
    count = len(others)
    dma = pltpu.SemaphoreType.DMA
    whole, edges, *lined = pl.pallas_call(
        gather_kernel,
        in_specs=[anywhere] * (2 + count),
        out_specs=[anywhere] * (2 + count),
        out_shape=[
            jax.ShapeDtypeStruct((seq, head, 1) + shard.shape, bf16),
            jax.ShapeDtypeStruct((2,) + edge.shape, bf16),
        ]
        + [jax.ShapeDtypeStruct((head,) + other.shape, bf16) for other in others],
        scratch_shapes=[
            dma((8, 4)),
            dma((8, 4)),
            dma((1 + count,)),
            dma((count, 4)),
            dma((count, 4)),
            dma((2,)),
            dma((2,)),
        ],
        compiler_params=pltpu.CompilerParams(collective_id=0, has_side_effects=True),
        cost_estimate=cost(100e9),
    )(shard, edge, *others)
    return whole, edges, lined


class Pieces:
    def __init__(self, shard, own=None):
        self.shard = shard
        self.columns = shard.shape[1]
        self.order = by_place(jnp.arange(lax.axis_size("head"), dtype=jnp.int32))
        if paired():
            if own is None:
                own = jnp.stack([shard] + [swap(shard, r, "head") for r in (1, 2, 3)])
            self.own = own
        else:
            own = lax.all_gather(shard, "head")
            self.own = lax.all_gather(own, "seq", axis=1, tiled=True)
            self.pieces, self.offsets = [(self.own, 0)], jnp.zeros((1,), jnp.int32)

    def sides(self, *after):
        if paired():
            own = tie(self.own, *after) if after else self.own
            self.by_x, self.by_y = swap(own, SIDE_X), swap(own, SIDE_Y)
            return self.by_x, self.by_y
        return ()

    def far(self, *after):
        if not paired():
            return
        by_x, by_y = self.by_x[:2], self.by_y[2:]
        if after:
            by_x, by_y = tie(by_x, *after), tie(by_y, *after)
        far_a, far_b = swap(by_x, SIDE_Y), swap(by_y, SIDE_X)
        mine = [(self.own, 0), (self.by_x, 0), (self.by_y, 0), (far_a, 0), (far_b, 2)]
        self.pieces = mine + [(swap(piece, CORE), start) for piece, start in mine]
        sides = (0, SIDE_X, SIDE_Y, SIDE_X | SIDE_Y, SIDE_X | SIDE_Y)
        sides = sides + tuple(side | CORE for side in sides)
        rows = self.shard.shape[0]
        self.offsets = (lax.axis_index("seq") ^ jnp.array(sides, jnp.int32)) * rows

    @property
    def places(self):
        return self.own.shape[0]

    def specs(self):
        def spec(piece, start):
            last = piece.shape[0] - 1
            return pl.BlockSpec(
                (1,) + piece.shape[1:], lambda z, o, p: (jnp.clip(z - start, 0, last), 0, 0)
            )

        return [spec(piece, start) for piece, start in self.pieces]

    def fill(self, offsets, refs, weight):
        z = pl.program_id(0)
        for i, (ref, (piece, start)) in enumerate(zip(refs, self.pieces)):
            count, rows, _ = piece.shape

            def put():
                at = pl.multiple_of(offsets[i], 16)
                weight[pl.ds(at, rows)] = ref[0]

            if count == self.places:
                put()
            else:
                pl.when((z >= start) & (z < start + count))(put)


def grad_kernel(first, plane, left0, left1, right0, right1, send, keep, rows0, rows1):
    _, width, tokens = left0.shape

    @pl.when(pl.program_id(0) == 0)
    def _():
        for i in range(4):
            rows0[i * width : (i + 1) * width] = left0[plane[0] ^ i]
            rows1[i * width : (i + 1) * width] = left1[plane[0] ^ i]

    total = dot(rows0[...], right0[0, 0]) + dot(rows1[...], right1[0, 0])
    total = total.astype(bf16)
    far = first // 2
    near = 3 ^ far
    for i, at in enumerate((0, near)):
        keep[i, 0] = total[at * width : (at + 1) * width]
        at ^= far
        send[i, 0] = total[at * width : (at + 1) * width]


def weight_grads(plane, left0, left1, right0, right1, kind, start, first, light):
    count, _, tokens, columns = right0.shape
    count //= 2
    width = left0.shape[1]
    left = pl.BlockSpec(left0.shape, lambda z, p: (0, 0, 0))
    right = pl.BlockSpec((1, 1, tokens, columns), lambda z, p: (z + start, kind, 0, 0))
    out = pl.BlockSpec((2, 1, width, columns), lambda z, p: (0, z, 0, 0))
    shape = jax.ShapeDtypeStruct((2, count, width, columns), bf16)
    return pl.pallas_call(
        functools.partial(grad_kernel, first),
        grid_spec=pltpu.PrefetchScalarGridSpec(
            num_scalar_prefetch=1,
            grid=(count,),
            in_specs=[left, left, right, right],
            out_specs=[out, out],
            scratch_shapes=[pltpu.VMEM((4 * width, tokens), bf16)] * 2,
        ),
        out_shape=[shape, shape],
        compiler_params=pltpu.CompilerParams(vmem_limit_bytes=VMEM),
        cost_estimate=cost(1 if light else count * 20 * width * tokens * columns),
    )(plane, left0, left1, right0, right1)


class Left:
    def __init__(self, rows):
        self.rows = rows
        if paired():
            blocks = rows.T.reshape(4, 2, D // 8, -1)
            core = lax.axis_index("seq") % 2
            pick = lambda c: lax.dynamic_index_in_dim(blocks, c, 1, keepdims=False)
            self.near, self.far = pick(core), swap(pick(1 - core), CORE)

    def pending(self):
        return (self.far,) if paired() else ()


class Scatter:
    def __init__(self, left, right, relative=False, other=None, kind=0):
        self.right = right
        self.left = left
        self.relative = relative
        self.kind = kind
        if paired():
            self.other = swap(right, CORE) if other is None else other

    def given(self):
        return (self.other,) + self.left.pending() if paired() else ()

    def other_side(self):
        return (self.other,) if paired() else (None,)

    def first(self):
        made = self.products()
        self.go()
        return made

    def products(self, light=False):
        self.made = []
        if not paired():
            return ()
        half = self.right.shape[0] // 2
        plane = (lax.axis_index("seq") // 2).reshape(1)
        self.kept = []
        for start, side in ((0, SIDE_X), (half, SIDE_Y)):
            send, keep = weight_grads(
                plane,
                self.left.near,
                self.left.far,
                self.right,
                self.other,
                self.kind,
                start,
                side,
                light,
            )
            self.made.append(send)
            self.kept.append(keep)
        return tuple(self.made)

    def go(self, *after):
        if paired():
            made = [tie(send, *after) for send in self.made] if after else self.made
            self.arrived = [swap(send, side) for send, side in zip(made, (SIDE_X, SIDE_Y))]
            self.coming = self.arrived

    def second(self, *after):
        if not paired():
            return ()
        self.sums, made = [], []
        for keep, arrived, side in zip(self.kept, self.arrived, (SIDE_Y, SIDE_X)):
            if after:
                arrived = tie(arrived, *after)
            go = (keep[1].astype(f32) + arrived[1].astype(f32)).astype(bf16)
            stay = keep[0].astype(f32) + arrived[0].astype(f32)
            made.append(go)
            self.sums.append((stay, swap(go, side)))
        self.coming = [arrived for _, arrived in self.sums]
        return tuple(made)

    def pending(self):
        return tuple(self.coming) if paired() else ()

    def last(self, *after):
        if not paired():
            whole = jnp.einsum(
                "td,htc->hdc", self.left.rows, self.right[:, self.kind], preferred_element_type=f32
            ).astype(bf16)
            seq = lax.axis_size("seq")
            whole = whole.reshape(whole.shape[:1] + (seq, D // seq, -1))
            return lax.psum_scatter(whole, "seq", scatter_dimension=1)
        sums = []
        for stay, arrived in self.sums:
            if after:
                arrived = tie(arrived, *after)
            sums.append((stay + arrived.astype(f32)).astype(bf16))
        sums = jnp.concatenate(sums, axis=0)
        if self.relative:
            sums = by_place(sums)
        return sums


class Along:
    def __init__(self, blocks, *after):
        if not paired():
            self.mine, self.coming = lax.psum_scatter(blocks, "head", scatter_dimension=0), []
            self.sent = ()
            return
        here = lax.axis_index("head")
        pick = lambda r: lax.dynamic_index_in_dim(blocks, here ^ r, 0, keepdims=False)
        sent = [pick(r) for r in (1, 2, 3)]
        self.sent = tuple(sent)
        if after:
            sent = [tie(block, *after) for block in sent]
        self.mine = pick(0)
        self.coming = [swap(block, r, "head") for r, block in zip((1, 2, 3), sent)]

    def finish(self, *after):
        coming = [tie(block, *after) for block in self.coming] if after else self.coming
        return sum([block.astype(f32) for block in coming], self.mine.astype(f32))


def whole_rows(ref, kind=0):
    block = ref[:, 0, kind]
    return block.reshape(D, block.shape[-1])


def weight_spec(weight, kinds=1, at=0):
    seq, _, _, _, columns = weight.shape
    return pl.BlockSpec((seq, 1, kinds, D // seq, columns), lambda z: (0, z, at, 0, 0))


def into_kernel(x_ref, w_ref, out_ref):
    out_ref[0] = dot(x_ref[...], whole_rows(w_ref)).astype(out_ref.dtype)


def into(x, weight, kind):
    count, columns = weight.shape[1], weight.shape[-1]
    tokens = x.shape[0]
    return pl.pallas_call(
        into_kernel,
        grid=(count,),
        in_specs=[
            pl.BlockSpec(x.shape, lambda z: (0, 0)),
            weight_spec(weight),
        ],
        out_specs=pl.BlockSpec((1, tokens, columns), lambda z: (z, 0, 0)),
        out_shape=jax.ShapeDtypeStruct((count, tokens, columns), kind),
        compiler_params=pltpu.CompilerParams(vmem_limit_bytes=VMEM),
        cost_estimate=cost(count * 3 * D * tokens * columns),
    )(x, weight)


def out_of_kernel(y_ref, w_ref, out_ref):
    @pl.when(pl.program_id(0) == 0)
    def _():
        out_ref[...] = jnp.zeros_like(out_ref)

    out_ref[...] += dot_rt(y_ref[0], whole_rows(w_ref))


def out_of(y, weight):
    count, tokens, columns = y.shape
    return pl.pallas_call(
        out_of_kernel,
        grid=(count,),
        in_specs=[
            pl.BlockSpec((1, tokens, columns), lambda z: (z, 0, 0)),
            weight_spec(weight),
        ],
        out_specs=pl.BlockSpec((tokens, D), lambda z: (0, 0)),
        out_shape=jax.ShapeDtypeStruct((tokens, D), f32),
        compiler_params=pltpu.CompilerParams(vmem_limit_bytes=VMEM),
        cost_estimate=cost(1),
    )(y, weight)


def into_pieces_kernel(lay, weights, offsets, places, x_ref, *refs):
    count = len(weights.pieces)
    refs, outs, weight = refs[:count], refs[count:-1], refs[-1]
    weights.fill(offsets, refs, weight)
    rows = dot(x_ref[...], weight[...])
    for b in range(lay.batch):
        here = slice(b * lay.tokens, (b + 1) * lay.tokens)
        for i in range(lay.splits):
            for j, out in enumerate(outs):
                out[b, i, 0, :, :WIDTH] = rows[here, lay.columns(i, j)[0]].astype(bf16)
                out[b, i, 0, :, WIDTH:] = jnp.zeros_like(out[b, i, 0, :, WIDTH:])


def into_pieces(lay, x, weights):
    count, columns = weights.places, weights.columns
    block = (lay.batch, lay.splits, 1, lay.tokens, LANES)
    return pl.pallas_call(
        functools.partial(into_pieces_kernel, lay, weights),
        grid_spec=pltpu.PrefetchScalarGridSpec(
            num_scalar_prefetch=2,
            grid=(count,),
            in_specs=[pl.BlockSpec(x.shape, lambda z, o, p: (0, 0))] + weights.specs(),
            out_specs=[pl.BlockSpec(block, lambda z, o, p: (0, 0, p[z], 0, 0))] * lay.heads,
            scratch_shapes=[pltpu.VMEM((D, columns), bf16)],
        ),
        out_shape=[jax.ShapeDtypeStruct(block[:2] + (count,) + block[3:], bf16)] * lay.heads,
        compiler_params=pltpu.CompilerParams(vmem_limit_bytes=VMEM),
        cost_estimate=cost(count * 3 * D * x.shape[0] * columns),
    )(weights.offsets, weights.order, x, *[piece for piece, _ in weights.pieces])


def out_of_pieces_kernel(lay, weights, offsets, places, *refs):
    ys, refs, (rows_ref, out_ref, weight) = refs[: lay.heads], refs[lay.heads : -3], refs[-3:]
    weights.fill(offsets, refs, weight)

    @pl.when(pl.program_id(0) == 0)
    def _():
        out_ref[...] = jnp.zeros_like(out_ref)

    end = lay.splits * lay.heads * WIDTH
    rows_ref[0, 0, :, end:] = jnp.zeros_like(rows_ref[0, 0, :, end:])
    for b in range(lay.batch):
        here = slice(b * lay.tokens, (b + 1) * lay.tokens)
        for i in range(lay.splits):
            for j, y_ref in enumerate(ys):
                rows_ref[0, 0, here, lay.columns(i, j)[0]] = y_ref[b, i, 0, :, :WIDTH]
    out_ref[...] += dot_rt(rows_ref[0, 0], weight[...])


def out_of_pieces(lay, ys, weights):
    count, columns = weights.places, weights.columns
    tokens = lay.batch * lay.tokens
    block = (lay.batch, lay.splits, 1, lay.tokens, LANES)
    return pl.pallas_call(
        functools.partial(out_of_pieces_kernel, lay, weights),
        grid_spec=pltpu.PrefetchScalarGridSpec(
            num_scalar_prefetch=2,
            grid=(count,),
            in_specs=[pl.BlockSpec(block, lambda z, o, p: (0, 0, p[z], 0, 0))] * lay.heads
            + weights.specs(),
            out_specs=[
                pl.BlockSpec((1, 1, tokens, columns), lambda z, o, p: (z, 0, 0, 0)),
                pl.BlockSpec((tokens, D), lambda z, o, p: (0, 0)),
            ],
            scratch_shapes=[pltpu.VMEM((D, columns), bf16)],
        ),
        out_shape=[
            jax.ShapeDtypeStruct((count, 1, tokens, columns), bf16),
            jax.ShapeDtypeStruct((tokens, D), f32),
        ],
        compiler_params=pltpu.CompilerParams(vmem_limit_bytes=VMEM),
        cost_estimate=cost(count * 3 * D * tokens * columns),
    )(weights.offsets, weights.order, *ys, *[piece for piece, _ in weights.pieces])


def spread_kernel(weights, offsets, places, x_ref, *refs):
    refs, (out_ref, weight) = refs[:-2], refs[-2:]
    weights.fill(offsets, refs, weight)
    out_ref[0] = dot(x_ref[...], weight[...])


def spread(x, weights):
    count, columns = weights.places, weights.columns
    tokens = x.shape[0]
    return pl.pallas_call(
        functools.partial(spread_kernel, weights),
        grid_spec=pltpu.PrefetchScalarGridSpec(
            num_scalar_prefetch=2,
            grid=(count,),
            in_specs=[pl.BlockSpec(x.shape, lambda z, o, p: (0, 0))] + weights.specs(),
            out_specs=pl.BlockSpec((1, tokens, columns), lambda z, o, p: (p[z], 0, 0)),
            scratch_shapes=[pltpu.VMEM((D, columns), bf16)],
        ),
        out_shape=jax.ShapeDtypeStruct((count, tokens, columns), f32),
        compiler_params=pltpu.CompilerParams(vmem_limit_bytes=VMEM),
        cost_estimate=cost(count * 3 * D * tokens * columns),
    )(weights.offsets, weights.order, x, *[piece for piece, _ in weights.pieces])


def collect_kernel(weights, offsets, places, y_ref, *refs):
    refs, (out_ref, weight) = refs[:-2], refs[-2:]
    weights.fill(offsets, refs, weight)

    @pl.when(pl.program_id(0) == 0)
    def _():
        out_ref[...] = jnp.zeros_like(out_ref)

    out_ref[...] += dot_rt(y_ref[0, 0], weight[...])


def collect(y, weights):
    count, _, tokens, columns = y.shape
    return pl.pallas_call(
        functools.partial(collect_kernel, weights),
        grid_spec=pltpu.PrefetchScalarGridSpec(
            num_scalar_prefetch=2,
            grid=(count,),
            in_specs=[pl.BlockSpec((1,) + y.shape[1:], lambda z, o, p: (p[z], 0, 0, 0))]
            + weights.specs(),
            out_specs=pl.BlockSpec((tokens, D), lambda z, o, p: (0, 0)),
            scratch_shapes=[pltpu.VMEM((D, columns), bf16)],
        ),
        out_shape=jax.ShapeDtypeStruct((tokens, D), f32),
        compiler_params=pltpu.CompilerParams(vmem_limit_bytes=VMEM),
        cost_estimate=cost(count * 3 * D * tokens * columns),
    )(weights.offsets, weights.order, y, *[piece for piece, _ in weights.pieces])


def hidden_kernel(x_ref, gu_ref, slope_ref, silu_ref, hidden_ref):
    gate = dot(x_ref[...], whole_rows(gu_ref, 0))
    sig = jax.nn.sigmoid(gate)
    silu = gate * sig
    up = dot(x_ref[...], whole_rows(gu_ref, 1))
    slope_ref[0] = (up * sig * (1.0 + gate * (1.0 - sig))).astype(bf16)
    silu_ref[0] = silu.astype(bf16)
    columns = gate.shape[1]
    hidden_ref[0, 0, :, :columns] = (silu * up).astype(bf16)
    hidden_ref[0, 0, :, columns:] = jnp.zeros_like(hidden_ref[0, 0, :, columns:])


def hidden_of(x, weight):
    count, columns = weight.shape[1], weight.shape[-1]
    padded = grouped(columns, LANES)
    tokens = x.shape[0]
    act = pl.BlockSpec((1, tokens, columns), lambda z: (z, 0, 0))
    kept = jax.ShapeDtypeStruct((count, tokens, columns), bf16)
    return pl.pallas_call(
        hidden_kernel,
        grid=(count,),
        in_specs=[pl.BlockSpec(x.shape, lambda z: (0, 0)), weight_spec(weight, kinds=2)],
        out_specs=[act, act, pl.BlockSpec((1, 1, tokens, padded), lambda z: (z, 0, 0, 0))],
        out_shape=[kept, kept, jax.ShapeDtypeStruct((count, 1, tokens, padded), bf16)],
        compiler_params=pltpu.CompilerParams(vmem_limit_bytes=VMEM),
        cost_estimate=cost(count * 6 * D * tokens * columns),
    )(x, weight)


def hidden_back_kernel(grad_ref, gu_ref, slope_ref, silu_ref, grads_ref, out_ref):
    @pl.when(pl.program_id(0) == 0)
    def _():
        out_ref[...] = jnp.zeros_like(out_ref)

    columns = slope_ref.shape[-1]
    grad_hidden = grad_ref[0, :, :columns]
    grad_gate = (grad_hidden * slope_ref[0].astype(f32)).astype(bf16)
    grad_up = (grad_hidden * silu_ref[0].astype(f32)).astype(bf16)
    grads_ref[0, 0, :, :columns] = grad_gate
    grads_ref[0, 1, :, :columns] = grad_up
    grads_ref[0, :, :, columns:] = jnp.zeros_like(grads_ref[0, :, :, columns:])
    out_ref[...] += dot_rt(grad_gate, whole_rows(gu_ref, 0)) + dot_rt(
        grad_up, whole_rows(gu_ref, 1)
    )


def hidden_back(grad, weight, slope, silu):
    count, columns = weight.shape[1], weight.shape[-1]
    padded = grouped(columns, LANES)
    tokens = grad.shape[1]
    act = pl.BlockSpec((1, tokens, columns), lambda z: (z, 0, 0))
    return pl.pallas_call(
        hidden_back_kernel,
        grid=(count,),
        in_specs=[
            pl.BlockSpec((1, tokens, padded), lambda z: (z, 0, 0)),
            weight_spec(weight, kinds=2),
            act,
            act,
        ],
        out_specs=[
            pl.BlockSpec((1, 2, tokens, padded), lambda z: (z, 0, 0, 0)),
            pl.BlockSpec((tokens, D), lambda z: (0, 0)),
        ],
        out_shape=[
            jax.ShapeDtypeStruct((count, 2, tokens, padded), bf16),
            jax.ShapeDtypeStruct((tokens, D), f32),
        ],
        compiler_params=pltpu.CompilerParams(vmem_limit_bytes=VMEM),
        cost_estimate=cost(1),
    )(grad, weight, slope, silu)


def inverse_rms(rows):
    return lax.rsqrt(jnp.mean(rows * rows, axis=-1, keepdims=True) + EPSILON)


def norm_back(rows, scale, gain, grad):
    unit = rows * scale
    scaled = gain * grad
    return scale * (scaled - unit * jnp.mean(scaled * unit, axis=-1, keepdims=True))


class Layout:
    def __init__(self, batch, tokens):
        seq, head = lax.axis_size("seq"), lax.axis_size("head")
        self.batch, self.tokens, self.head = batch, tokens, head
        self.splits = min(seq // batch, HEADS // head)
        self.heads = HEADS // (head * self.splits)
        self.parts = seq // (batch * self.splits)
        self.inner = seq // self.parts
        self.sets = LANES // FEAT
        self.key_rows = grouped(tokens // self.sets, 16)
        self.length = tokens * seq * head
        count = self.inner * head
        self.groups = None
        if self.parts > 1:
            self.groups = [list(range(k * count, (k + 1) * count)) for k in range(self.parts)]
            self.mates = [[k * count + i for k in range(self.parts)] for i in range(count)]

    def sequence(self):
        return lax.rem(lax.axis_index("seq"), self.inner) // self.splits

    def pack_keys(self, keys):
        lead, each = keys.shape[:-2], self.tokens // self.sets
        keys = keys.reshape(lead + (self.sets, each, FEAT))
        keys = jnp.swapaxes(keys, -3, -2).reshape(lead + (each, LANES))
        return jnp.pad(keys, [(0, 0)] * len(lead) + [(0, self.key_rows - each), (0, 0)])

    def unpack_keys(self, rows):
        lead, each = rows.shape[:-2], self.tokens // self.sets
        rows = rows[..., :each, :].reshape(lead + (each, self.sets, FEAT))
        return jnp.swapaxes(rows, -3, -2).reshape(lead + (self.tokens, FEAT))

    def columns(self, i, j):
        at = i * self.heads + j
        return slice(at * WIDTH, (at + 1) * WIDTH), slice(at * FEAT, (at + 1) * FEAT)

    def by_place(self, blocks):
        return blocks.reshape((self.batch, self.splits, self.head) + blocks.shape[1:])

    def exchange(self, blocks):
        return lax.all_to_all(blocks, BOTH, 0, 0, tiled=True, axis_index_groups=self.groups)

    def all_parts(self, rows):
        if self.parts > 1:
            rows = lax.all_gather(rows, BOTH, axis=0, tiled=True, axis_index_groups=self.mates)
        return rows

    def own_part(self, blocks):
        if self.parts > 1:
            count = blocks.shape[0] // self.parts
            part = lax.axis_index("seq") // self.inner
            blocks = lax.dynamic_slice_in_dim(blocks, part * count, count, 0)
        return blocks


def fill_values(chunk, main, values, queries):
    lane = lax.broadcasted_iota(jnp.int32, (chunk, LANES), 1)
    ones = jnp.where(lane < WIDTH + 2, 1.0, 0.0)

    def turn(i, _):
        here = pl.ds(pl.multiple_of(i * chunk, chunk), chunk)
        rows = main[here]
        values[here] = jnp.where(lane < WIDTH, rows.astype(f32), ones).astype(bf16)
        queries[here] = rows[:, WIDTH:]
        return 0

    lax.fori_loop(0, main.shape[0] // chunk, turn, 0)


def attend_kernel(chunk, main, keys, seg_col, seg_row, out_ref, low_ref, values, queries):
    at = pl.program_id(0)

    @pl.when(at == 0)
    def _():
        fill_values(chunk, main, values, queries)

    mine = seg_col[...]
    query = queries[pl.ds(pl.multiple_of(at * chunk, chunk), chunk)]

    def weighted(j, causal):
        here = pl.ds(pl.multiple_of(j * chunk, chunk), chunk)
        scores = dot_rt(query, keys[here])
        allowed = mine == seg_row[j]
        if causal:
            later = lax.broadcasted_iota(jnp.int32, scores.shape, 0)
            allowed &= later >= lax.broadcasted_iota(jnp.int32, scores.shape, 1)
        weights = jnp.where(allowed, 1.0 + scores * (1.0 + 0.5 * scores), 0.0).astype(bf16)
        return dot(weights, values[here])

    total = lax.fori_loop(
        0, at, lambda j, acc: acc + weighted(j, False), jnp.zeros((chunk, LANES), f32)
    )
    total = total + weighted(at, True)
    norm = total[:, WIDTH : WIDTH + 1]
    lane = lax.broadcasted_iota(jnp.int32, total.shape, 1)
    total = jnp.where(lane < WIDTH, total / norm, norm)
    out_ref[...] = total
    low_ref[...] = total.astype(bf16)


def attend(main, keys, seg):
    length = main.shape[0]
    chunk = min(512, length)
    steps = length // chunk
    part = pl.BlockSpec((chunk, LANES), lambda i: (i, 0))
    return pl.pallas_call(
        functools.partial(attend_kernel, chunk),
        grid=(steps,),
        in_specs=[
            pl.BlockSpec((length, LANES), lambda i: (0, 0)),
            pl.BlockSpec((length, FEAT), lambda i: (0, 0)),
            pl.BlockSpec((chunk, 1), lambda i: (i, 0)),
            pl.BlockSpec((steps, 1, chunk), lambda i: (0, 0, 0)),
        ],
        out_specs=[part, part],
        out_shape=[
            jax.ShapeDtypeStruct((length, LANES), f32),
            jax.ShapeDtypeStruct((length, LANES), bf16),
        ],
        scratch_shapes=[pltpu.VMEM((length, LANES), bf16), pltpu.VMEM((length, FEAT), bf16)],
        compiler_params=pltpu.CompilerParams(vmem_limit_bytes=VMEM),
        cost_estimate=cost(length * length * 12 * LANES),
    )(main, keys, seg.reshape(length, 1), seg.reshape(steps, 1, chunk))


def attend_back_kernel(
    chunk,
    main,
    keys,
    kept,
    grad,
    seg_col,
    seg_row,
    out_ref,
    gk_ref,
    values,
    queries,
    grad_n,
    grad_q,
):
    at = pl.program_id(0)
    steps = main.shape[0] // chunk

    @pl.when(at == 0)
    def _():
        fill_values(chunk, main, values, queries)
        grad_q[...] = jnp.zeros_like(grad_q)
        lane = lax.broadcasted_iota(jnp.int32, (chunk, LANES), 1)

        def turn(i, _):
            here = pl.ds(pl.multiple_of(i * chunk, chunk), chunk)
            rows = kept[here]
            low = jnp.where(lane < WIDTH, grad[here].astype(f32), 0.0)
            inverse = 1.0 / rows[:, WIDTH : WIDTH + 1]
            total = -jnp.sum(low * rows, axis=1, keepdims=True) * inverse
            high = total.astype(bf16).astype(f32)
            low = low * inverse
            low = jnp.where(lane == WIDTH, high, low)
            grad_n[here] = jnp.where(lane == WIDTH + 1, total - high, low).astype(bf16)
            return 0

        lax.fori_loop(0, steps, turn, 0)

    mine = seg_col[...]
    rows = pl.ds(pl.multiple_of(at * chunk, chunk), chunk)
    key, value = keys[rows], values[rows]
    key_t = key.astype(f32).T.astype(bf16)

    def turn(i, carry, causal):
        grad_k, grad_v = carry
        here = pl.ds(pl.multiple_of(i * chunk, chunk), chunk)
        query, grad_here = queries[here], grad_n[here]
        scores = dot_rt(key, query)
        allowed = mine == seg_row[i]
        if causal:
            key_at = lax.broadcasted_iota(jnp.int32, scores.shape, 0)
            allowed &= key_at <= lax.broadcasted_iota(jnp.int32, scores.shape, 1)
        weights = jnp.where(allowed, 1.0 + scores * (1.0 + 0.5 * scores), 0.0).astype(bf16)
        grad_s = dot_rt(value, grad_here) * (1.0 + scores)
        grad_s = jnp.where(allowed, grad_s, 0.0).astype(bf16)
        grad_q[:, here] += dot(key_t, grad_s)
        return grad_k + dot(grad_s, query), grad_v + dot(weights, grad_here)

    carry = (jnp.zeros((chunk, FEAT), f32), jnp.zeros((chunk, LANES), f32))
    carry = turn(at, carry, True)
    grad_k, grad_v = lax.fori_loop(at + 1, steps, lambda i, c: turn(i, c, False), carry)
    gk_ref[...] = (0.5 * grad_k).astype(bf16)
    out_ref[rows] = grad_v.astype(bf16)

    @pl.when(at == steps - 1)
    def _():
        def turn(i, _):
            here = pl.ds(pl.multiple_of(i * chunk, chunk), chunk)
            out_ref[here, WIDTH:] = (0.5 * grad_q[:, here].T).astype(bf16)
            return 0

        lax.fori_loop(0, steps, turn, 0)


def attend_back(main, keys, kept, grad, seg):
    length = main.shape[0]
    chunk = min(512, length)
    steps = length // chunk
    whole = pl.BlockSpec((length, LANES), lambda i: (0, 0))
    return pl.pallas_call(
        functools.partial(attend_back_kernel, chunk),
        grid=(steps,),
        in_specs=[
            whole,
            pl.BlockSpec((length, FEAT), lambda i: (0, 0)),
            whole,
            whole,
            pl.BlockSpec((chunk, 1), lambda i: (i, 0)),
            pl.BlockSpec((steps, 1, chunk), lambda i: (0, 0, 0)),
        ],
        out_specs=[whole, pl.BlockSpec((chunk, FEAT), lambda i: (i, 0))],
        out_shape=[
            jax.ShapeDtypeStruct((length, LANES), bf16),
            jax.ShapeDtypeStruct((length, FEAT), bf16),
        ],
        scratch_shapes=[
            pltpu.VMEM((length, LANES), bf16),
            pltpu.VMEM((length, FEAT), bf16),
            pltpu.VMEM((length, LANES), bf16),
            pltpu.VMEM((FEAT, length), f32),
        ],
        compiler_params=pltpu.CompilerParams(vmem_limit_bytes=VMEM),
        cost_estimate=cost(length * length * 24 * LANES),
    )(main, keys, kept, grad, seg.reshape(length, 1), seg.reshape(steps, 1, chunk))


def earlier(rows, before, distance):
    moved = pltpu.roll(rows, distance, 0)
    place = lax.broadcasted_iota(jnp.int32, rows.shape, 0)
    for i in range(distance):
        at = 2 - distance + i
        moved = jnp.where(place == i, before[at : at + 1], moved)
    return moved


def later(rows, after, distance):
    count = rows.shape[0]
    moved = pltpu.roll(rows, count - distance, 0)
    place = lax.broadcasted_iota(jnp.int32, rows.shape, 0)
    for i in range(distance):
        moved = jnp.where(place == count - distance + i, after[i : i + 1], moved)
    return moved


def short_filter(taps, same, values, before):
    one_back = earlier(values, before, 1) * same[:, 0:1]
    two_back = earlier(values, before, 2) * same[:, 1:2]
    return taps[0:1] * values + taps[1:2] * one_back + taps[2:3] * two_back, one_back, two_back


def project_kernel(lay, x_ref, side_ref, same_ref, taps_ref, w_ref, v_ref, f_ref, side_out, *outs):
    weight = whole_rows(w_ref)
    q_width, v_width = lay.splits * lay.heads * FEAT, v_ref.shape[-1]
    v_at, f_at = 2 * q_width, 2 * q_width + v_width
    full = dot(x_ref[...], weight)
    side = dot(side_ref[...], weight)
    low = full[:, v_at:f_at].astype(bf16)
    v_ref[0] = low
    f_ref[0] = full[:, f_at:]
    side_v = side[:, v_at:f_at].astype(bf16).astype(f32)
    side_out[0, 0] = side_v
    side_out[0, 1] = side[:, f_at:]
    taps = taps_ref[0]
    for b in range(lay.batch):
        rows = slice(b * lay.tokens, (b + 1) * lay.tokens)
        pre = full[rows, f_at:]
        filtered, _, _ = short_filter(
            taps, same_ref[rows], low[rows].astype(f32), side_v[2 * b : 2 * b + 2]
        )
        mixed = filtered * (pre * jax.nn.sigmoid(pre))
        query = 0.5 * full[rows, :q_width].astype(bf16).astype(f32)
        key = 0.5 * full[rows, q_width:v_at].astype(bf16).astype(f32)
        for i in range(lay.splits):
            for j in range(lay.heads):
                main, k_ref = outs[2 * j : 2 * j + 2]
                v_cols, q_cols = lay.columns(i, j)
                main[b, i, 0, :, :WIDTH] = mixed[:, v_cols].astype(bf16)
                main[b, i, 0, :, WIDTH:] = query[:, q_cols].astype(bf16)
                k_ref[b, i, 0] = key[:, q_cols].astype(bf16)


def project(lay, x, side, same, taps, weight):
    tokens, head = x.shape[0], lay.head
    v_width = taps.shape[-1]
    beside = side.shape[0]
    to_all = lambda width: pl.BlockSpec(
        (lay.batch, lay.splits, 1, lay.tokens, width), lambda z: (0, 0, z, 0, 0)
    )
    shape = lambda width: jax.ShapeDtypeStruct(
        (lay.batch, lay.splits, head, lay.tokens, width), bf16
    )
    kept = pl.BlockSpec((1, tokens, v_width), lambda z: (z, 0, 0))
    return pl.pallas_call(
        functools.partial(project_kernel, lay),
        grid=(head,),
        in_specs=[
            pl.BlockSpec(x.shape, lambda z: (0, 0)),
            pl.BlockSpec(side.shape, lambda z: (0, 0)),
            pl.BlockSpec(same.shape, lambda z: (0, 0)),
            pl.BlockSpec((1, 3, v_width), lambda z: (z, 0, 0)),
            weight_spec(weight),
        ],
        out_specs=[
            kept,
            kept,
            pl.BlockSpec((1, 2, beside, v_width), lambda z: (z, 0, 0, 0)),
        ]
        + [to_all(LANES), to_all(FEAT)] * lay.heads,
        out_shape=[
            jax.ShapeDtypeStruct((head, tokens, v_width), bf16),
            jax.ShapeDtypeStruct((head, tokens, v_width), f32),
            jax.ShapeDtypeStruct((head, 2, beside, v_width), f32),
        ]
        + [shape(LANES), shape(FEAT)] * lay.heads,
        compiler_params=pltpu.CompilerParams(vmem_limit_bytes=VMEM),
        cost_estimate=cost(head * 3 * D * tokens * weight.shape[-1]),
    )(x, side, same, taps, weight)


def project_back_kernel(
    lay, v_ref, f_ref, side_ref, same_ref, taps_ref, gk_ref, *refs
):
    backs, (out_ref, tap_ref, mixed, after) = refs[:-4], refs[-4:]
    q_width, v_width = gk_ref.shape[-1], v_ref.shape[-1]
    v_at, f_at = 2 * q_width, 2 * q_width + v_width
    taps = taps_ref[0]
    below = lay.tokens + lay.key_rows
    tap_ref[...] = jnp.zeros_like(tap_ref)
    out_ref[0, :, q_width:v_at] = gk_ref[0]
    for b in range(lay.batch):
        rows = slice(b * lay.tokens, (b + 1) * lay.tokens)
        for i in range(lay.splits):
            for j, back in enumerate(backs):
                v_cols, q_cols = lay.columns(i, j)
                block = back[b, i, 0, : lay.tokens]
                mixed[:, v_cols] = block[:, :WIDTH].astype(f32)
                out_ref[0, rows, q_cols] = block[:, WIDTH:]
                after[:, v_cols] = back[b, i, 0, below : below + 16, :WIDTH].astype(f32)
        grad_mixed = mixed[...]
        pre = f_ref[0, rows]
        sig = jax.nn.sigmoid(pre)
        values = v_ref[0, rows].astype(f32)
        same = same_ref[rows]
        at = 2 * b
        filtered, one_back, two_back = short_filter(
            taps, same, values, side_ref[0, 0, at : at + 2]
        )
        grad = grad_mixed * pre * sig
        at = 2 * (lay.batch + b)
        pre_after = side_ref[0, 1, at : at + 2]
        grad_after = after[0:2] * pre_after * jax.nn.sigmoid(pre_after)
        grad_v = (
            taps[0:1] * grad
            + taps[1:2] * later(grad, grad_after, 1) * same[:, 2:3]
            + taps[2:3] * later(grad, grad_after, 2) * same[:, 3:4]
        )
        out_ref[0, rows, v_at:f_at] = grad_v.astype(bf16)
        grad_f = grad_mixed * filtered * sig * (1.0 + pre * (1.0 - sig))
        out_ref[0, rows, f_at:] = grad_f.astype(bf16)
        for k, term in enumerate((values, one_back, two_back)):
            tap_ref[0, k : k + 1] += jnp.sum(grad * term, axis=0, keepdims=True)


def project_back(lay, backs, grad_keys, values, pre, side, same, taps):
    head, tokens, v_width = values.shape
    columns = 2 * (grad_keys.shape[-1] + v_width)
    kept = pl.BlockSpec((1, tokens, v_width), lambda z: (z, 0, 0))
    return pl.pallas_call(
        functools.partial(project_back_kernel, lay),
        grid=(head,),
        in_specs=[
            kept,
            kept,
            pl.BlockSpec((1,) + side.shape[1:], lambda z: (z, 0, 0, 0)),
            pl.BlockSpec(same.shape, lambda z: (0, 0)),
            pl.BlockSpec((1, 3, v_width), lambda z: (z, 0, 0)),
            pl.BlockSpec((1,) + grad_keys.shape[1:], lambda z: (z, 0, 0)),
        ]
        + [
            pl.BlockSpec(
                (lay.batch, lay.splits, 1) + back.shape[3:], lambda z: (0, 0, z, 0, 0)
            )
            for back in backs
        ],
        out_specs=[
            pl.BlockSpec((1, tokens, columns), lambda z: (z, 0, 0)),
            pl.BlockSpec((1, 3, v_width), lambda z: (z, 0, 0)),
        ],
        out_shape=[
            jax.ShapeDtypeStruct((head, tokens, columns), bf16),
            jax.ShapeDtypeStruct((head, 3, v_width), f32),
        ],
        scratch_shapes=[
            pltpu.VMEM((lay.tokens, v_width), f32),
            pltpu.VMEM((16, v_width), f32),
        ],
        compiler_params=pltpu.CompilerParams(vmem_limit_bytes=VMEM),
        cost_estimate=cost(1),
    )(values, pre, side, same, taps, grad_keys, *backs)


def shift(block, distance):
    devices = range(lax.axis_size("seq") * lax.axis_size("head"))
    return lax.ppermute(
        block, BOTH, [(i, i + distance) for i in devices if i + distance in devices]
    )


def local(
    tokens,
    cotangent,
    segment_ids,
    query_weight,
    key_weight,
    value_weight,
    filter_weight,
    out_weight,
    gate_weight,
    up_weight,
    down_weight,
    norm_gain,
    ffn_gain,
    conv_taps,
):
    seq, head = lax.axis_size("seq"), lax.axis_size("head")
    batch, span, _ = tokens.shape
    count = batch * span
    length = segment_ids.shape[1] * seq
    place = lax.axis_index("seq") * head + lax.axis_index("head")
    heads_here = HEADS // head
    qk_width, v_width = heads_here * FEAT, heads_here * WIDTH
    ff_width = gate_weight.shape[1]

    lay = Layout(batch, span)
    out_pad = grouped(v_width, LANES) - v_width
    first = jnp.concatenate([query_weight, key_weight, value_weight, filter_weight], axis=1)
    rows_here, columns = first.shape
    small = [norm_gain, ffn_gain, conv_taps.reshape(-1), segment_ids.astype(bf16).reshape(-1)]
    ends = [0]
    for part in small:
        ends.append(ends[-1] + part.size)
    below = grouped(-(-ends[-1] // columns), 16)
    small = jnp.pad(jnp.concatenate(small), (0, below * columns - ends[-1]))
    ff_pad = grouped(ff_width, LANES) - ff_width
    down_shard = jnp.pad(down_weight, ((0, 0), (0, ff_pad)))
    out_shard = jnp.pad(out_weight.T, ((0, 0), (0, out_pad)))
    edge = jnp.stack([tokens[:, -2:], tokens[:, :2]]).reshape(-1, D)
    edge = jnp.pad(edge, ((0, grouped(edge.shape[0], 16) - edge.shape[0]), (0, 0)))
    first_w, edges, lined = gather_first(
        jnp.concatenate([first, small.reshape(below, columns)]), edge, [down_shard]
    )
    beside = jnp.concatenate([edges[0, : 2 * batch], edges[1, 2 * batch : 4 * batch]])
    gate_up_w = gather(jnp.stack([gate_weight, up_weight]))
    down_w = Pieces(down_shard, lined[0])

    small = first_w[:, :, 0, rows_here:].reshape(seq, head, -1).astype(f32)
    part = lambda i: small[:, :, ends[i] : ends[i + 1]]
    gain_one, gain_two = part(0)[:, 0].reshape(1, D), part(1)[:, 0].reshape(1, D)
    taps = jnp.transpose(part(2).reshape(seq, head, 3, -1), (1, 2, 0, 3))
    taps = taps.reshape(head, 3, v_width)
    segs = jnp.swapaxes(part(3)[:, 0].reshape(seq, batch, -1), 0, 1).reshape(batch, length)
    x = tokens.reshape(count, D).astype(f32)
    cot_low = cotangent.reshape(count, D)

    def normed_of(rows):
        scale = inverse_rms(rows)
        return scale, (rows * scale * gain_one).astype(bf16)

    scale_one, normed = normed_of(x)
    _, normed_beside = normed_of(beside.astype(f32))
    around = lax.dynamic_slice(
        jnp.pad(segs, ((0, 0), (2, 2)), constant_values=-1.0),
        (0, place * span),
        (batch, span + 4),
    )
    seg_here = around[:, 2:-2]
    others = (around[:, 1:-3], around[:, :-4], around[:, 3:-1], around[:, 4:])
    same = jnp.stack([(seg_here == other).astype(f32) for other in others], axis=-1)
    same = same.reshape(count, 4)
    cot_left = Left(cot_low)
    normed = tie(normed, down_w.own, *cot_left.pending())
    down_sides = down_w.sides(first_w)
    v_low, filter_pre, side, *sent = project(lay, normed, normed_beside, same, taps, first_w)
    my_seg = lax.dynamic_index_in_dim(segs, lay.sequence(), 0, keepdims=False)
    heads = range(lay.heads)
    mains, all_keys, kept, low = [], [], [], []
    for j in heads:
        blocks = jnp.concatenate([sent[2 * j], lay.pack_keys(sent[2 * j + 1])], axis=3)
        if j > 0:
            blocks = tie(blocks, mains[-1])
        blocks = lay.exchange(blocks.reshape(-1, span + lay.key_rows, LANES))
        mains.append(lay.all_parts(blocks[:, :span].reshape(-1, LANES)))
        all_keys.append(lay.all_parts(lay.unpack_keys(blocks[:, span:]).reshape(-1, FEAT)))
    mains[0] = tie(mains[0], *down_sides)
    down_w.far(mains[0])
    for j in heads:
        attended, sent = attend(mains[j], all_keys[j], my_seg)
        kept.append(attended)
        blocks = lay.own_part(sent.reshape(-1, span, LANES))
        if j == 0:
            out_w = Pieces(tie(out_shard, blocks))
        if j == lay.heads - 1:
            blocks = tie(blocks, out_w.own, *[piece for piece, _ in down_w.pieces])
            out_sides = out_w.sides(blocks)
        if j > 0:
            blocks = tie(blocks, low[-1])
        low.append(lay.exchange(blocks))
    grad_hidden = spread(tie(cot_low, blocks), down_w)
    low[-1] = tie(low[-1], grad_hidden, *out_sides)
    out_w.far(grad_hidden)
    att_low, projected = out_of_pieces(lay, [lay.by_place(blocks) for blocks in low], out_w)

    residual = x + projected
    scale_two = inverse_rms(residual)
    normed_two = (residual * scale_two * gain_two).astype(bf16)
    out_sum = Scatter(None, att_low, True)
    normed_two = tie(normed_two, out_sum.other_side())
    slope, silu, hidden = hidden_of(normed_two, gate_up_w)
    down_sum = Scatter(cot_left, hidden)
    ffn_out = collect(hidden, down_w)
    layer_output = (residual + ffn_out).astype(bf16).reshape(tokens.shape)

    down_sum.right = tie(down_sum.right, ffn_out)
    down_sends = down_sum.first()
    grads_gu, back_two = hidden_back(tie(grad_hidden, *down_sends), gate_up_w, slope, silu)
    two_left = Left(normed_two)
    gate_sum = Scatter(two_left, grads_gu)
    up_sum = Scatter(two_left, grads_gu, False, *gate_sum.other_side(), kind=1)
    gain_two_grad = jnp.sum(back_two * residual * scale_two, axis=0)
    grad_residual = cot_low.astype(f32) + norm_back(residual, scale_two, gain_two, back_two)
    grad_res_low = grad_residual.astype(bf16)

    sent = [rows.reshape(-1, span, LANES) for rows in into_pieces(lay, grad_res_low, out_w)]
    arrived = [lay.exchange(blocks) for blocks in sent]
    down_sends = down_sum.second(*sent)
    out_sum.left = Left(tie(grad_res_low, *sent))
    for terms in (gate_sum, up_sum, out_sum):
        terms.right = tie(terms.right, *down_sends)
    up_sum.right = tie(up_sum.right, *arrived[1:])
    made = gate_sum.products() + up_sum.products() + out_sum.products()
    down_sum = Along(down_sum.last(*made))
    gate_sum.go(*down_sum.sent)
    arrived[0] = tie(arrived[0], *made, *down_sum.sent)
    backs, grad_keys = [], []
    for j in heads:
        grad_rows = lay.all_parts(arrived[j].reshape(-1, LANES))
        if j == lay.heads - 1:
            if j > 0:
                grad_rows = tie(grad_rows, sent)
            up_sum.go(grad_rows, *gate_sum.pending())
            grad_rows = tie(grad_rows, *gate_sum.pending(), *down_sum.coming)
        grad_main, grad_key = attend_back(mains[j], all_keys[j], kept[j], grad_rows, my_seg)
        if j == lay.heads - 1:
            grad_main = tie(grad_main, *up_sum.pending())
        blocks = grad_main.reshape(-1, span, LANES)
        ahead = jnp.pad(blocks[1:, :16], ((0, 1), (0, 0), (0, 0)))
        packed = lay.pack_keys(grad_key.reshape(-1, span, FEAT))
        sent = lay.own_part(jnp.concatenate([blocks, packed, ahead], axis=1))
        if j > 0:
            sent = tie(sent, backs[-1])
        blocks = lay.exchange(sent)
        grad_keys.append(lay.unpack_keys(blocks[:, span : span + lay.key_rows]))
        backs.append(lay.by_place(blocks))
    gate_sum.second(sent)
    up_sum.second(sent)
    backs[-1] = tie(backs[-1], *gate_sum.pending(), *up_sum.pending())
    gate_up_sum = Along(jnp.stack([gate_sum.last(backs[-1]), up_sum.last(backs[-1])], axis=1))
    backs[-1] = tie(backs[-1], *gate_up_sum.sent)
    out_sum.go(backs[-1])

    grad_keys = jnp.stack([lay.by_place(rows) for rows in grad_keys])
    grad_keys = jnp.transpose(grad_keys, (3, 1, 4, 2, 0, 5)).reshape(head, count, -1)
    grad_first, tap_grads = project_back(
        lay, backs, grad_keys, v_low, filter_pre, side, same, taps
    )
    tap_grads = jnp.swapaxes(tap_grads, 0, 1).reshape(3, D)
    grad_first = tie(grad_first, *out_sum.pending(), *gate_up_sum.coming[:1])
    first_sum = Scatter(Left(tie(normed, grad_first)), grad_first[:, None])
    out_sends = out_sum.second(*first_sum.given())
    first_sum.right = tie(first_sum.right, *out_sends)
    first_sum.products(True)
    first_sum.go(*out_sum.pending())
    out_grad = lax.psum_scatter(out_sum.last(*first_sum.made), "head", scatter_dimension=0)
    back_one = out_of(tie(grad_first, *first_sum.made), first_w)
    gain_one_grad = jnp.sum(back_one * x * scale_one, axis=0)
    first_sends = first_sum.second(back_one, *gate_up_sum.coming[1:])
    gate_up_grad = gate_up_sum.finish(*first_sends)
    down_grad = down_sum.finish(*first_sends)
    first_sum = Along(first_sum.last(*first_sends))
    out_grad = tie(out_grad, *first_sum.sent)
    first_grad = first_sum.finish()
    grad_x = (grad_residual + norm_back(x, scale_one, gain_one, back_one)).astype(bf16)
    tokens_grad = grad_x.reshape(tokens.shape)

    small = jnp.concatenate([jnp.stack([gain_one_grad, gain_two_grad]), tap_grads], axis=0)
    small = tie(small, *first_sum.sent)
    small = jnp.swapaxes(small.reshape(5, head * seq, -1), 0, 1)
    small = lax.all_to_all(small, ("head", "seq"), 0, 0, tiled=True)
    small = jnp.sum(small, axis=0)

    q_end, k_end, v_end = qk_width, 2 * qk_width, 2 * qk_width + v_width
    return (
        layer_output,
        tokens_grad,
        first_grad[:, :q_end],
        first_grad[:, q_end:k_end],
        first_grad[:, k_end:v_end],
        first_grad[:, v_end:],
        out_grad[:, :v_width].astype(f32).T,
        gate_up_grad[0][:, :ff_width].astype(f32),
        gate_up_grad[1][:, :ff_width].astype(f32),
        down_grad[:, :ff_width].astype(f32),
        small[0],
        small[1],
        small[2:],
    )


def solution(mesh):
    rows = P(None, BOTH, None)
    return jax.shard_map(
        local,
        mesh=mesh,
        in_specs=(
            rows,
            rows,
            P(None, "seq"),
            P("seq", "head"),
            P("seq", "head"),
            P("seq", "head"),
            P("seq", "head"),
            P("head", "seq"),
            P("seq", "head"),
            P("seq", "head"),
            P("seq", "head"),
            P("seq"),
            P("seq"),
            P(None, ("head", "seq")),
        ),
        out_specs=(
            rows,
            rows,
            P("seq", "head"),
            P("seq", "head"),
            P("seq", "head"),
            P("seq", "head"),
            P("head", "seq"),
            P("seq", "head"),
            P("seq", "head"),
            P("seq", "head"),
            P(("head", "seq")),
            P(("head", "seq")),
            P(None, ("head", "seq")),
        ),
        check_vma=False,
    )
```

```python
import functools

import jax
import jax.numpy as jnp
from jax import lax
from jax.experimental import pallas as pl
from jax.experimental.pallas import tpu as pltpu
from jax.sharding import PartitionSpec as P

D = 1792
HEADS = 16
FEAT = 16
WIDTH = D // HEADS
LANES = 128
VMEM = 60 * 2**20
EPSILON = 1e-06
BOTH = ("seq", "head")
CORE, SIDE_X, SIDE_Y = 1, 2, 4

f32 = jnp.float32
bf16 = jnp.bfloat16
MESH = pl.DeviceIdType.MESH


def grouped(value, multiple):
    return -(-value // multiple) * multiple


def cost(flops):
    return pl.CostEstimate(flops=int(flops), bytes_accessed=1, transcendentals=0)


def dot(left, right):
    return jnp.dot(left, right, preferred_element_type=f32)


def dot_rt(left, right):
    return lax.dot_general(left, right, (((1,), (1,)), ((), ())), preferred_element_type=f32)


def dot_lt(left, right):
    return lax.dot_general(left, right, (((0,), (0,)), ((), ())), preferred_element_type=f32)


def swap(block, bit, axis="seq"):
    devices = range(lax.axis_size(axis))
    return lax.ppermute(block, axis, [(i, i ^ bit) for i in devices])


def paired():
    return lax.axis_size("seq") == 8 and lax.axis_size("head") == 4


def tie(value, *others):
    return lax.optimization_barrier((value, others))[0]


def gather(shard):
    whole = lax.all_gather(shard, BOTH)
    return whole.reshape((lax.axis_size("seq"), lax.axis_size("head")) + shard.shape)


def by_place(blocks):
    if not paired():
        return blocks
    here = lax.axis_index("head")
    if blocks.ndim == 1:
        return blocks ^ here
    pick = lambda r: lax.dynamic_index_in_dim(blocks, here ^ r, 0, keepdims=False)
    return jnp.stack([pick(r) for r in range(4)])


def flipped(here, bit):
    return here + bit - 2 * bit * ((here // bit) % 2)


def gather_kernel(shard, edge, *refs):
    count = (len(refs) - 9) // 2
    others, (whole, edges), rest = refs[:count], refs[count : count + 2], refs[count + 2 :]
    lined, (send, recv, local, line_send, line_recv, edge_send, edge_recv) = (
        rest[:count],
        rest[count:],
    )
    place, line = lax.axis_index("seq"), lax.axis_index("head")
    seq, head = lax.axis_size("seq"), lax.axis_size("head")
    lines = [line, flipped(line, 1), flipped(line, 2), 3 - line]
    by_x, by_y, by_core = (flipped(place, bit) for bit in (SIDE_X, SIDE_Y, CORE))
    corner = flipped(by_x, SIDE_Y)
    to = lambda at, z: {"seq": at, "head": z}
    linear = place * head + line
    after, before = (linear + 1) % (seq * head), (linear + seq * head - 1) % (seq * head)
    sides = [to(at // head, at % head) for at in (after, before)]
    partners = [to(place, z) for z in lines[1:]] + [to(at, line) for at in (by_x, by_y, by_core)]
    partners += sides

    barrier = pltpu.get_barrier_semaphore()
    for partner in partners:
        pl.semaphore_signal(barrier, inc=1, device_id=partner, device_id_type=MESH)
    pl.semaphore_wait(barrier, len(partners))

    def remote(source, target, send_sem, recv_sem, partner):
        return pltpu.make_async_remote_copy(
            src_ref=source,
            dst_ref=target,
            send_sem=send_sem,
            recv_sem=recv_sem,
            device_id=partner,
            device_id_type=MESH,
        )

    copies = [pltpu.make_async_copy(shard, whole.at[place, line, 0], local.at[0])]
    copies += [
        pltpu.make_async_copy(other, target.at[0], local.at[1 + i])
        for i, (other, target) in enumerate(zip(others, lined))
    ]
    started = {}

    def start(row, r, source, at, z, partner):
        started[row, r] = remote(
            source, whole.at[at, z, 0], send.at[row, r], recv.at[row, r], partner
        )
        started[row, r].start()

    for r in (2, 1):
        start(0, r, shard, place, line, to(place, lines[r]))
    copies += [
        remote(edge, edges.at[i], edge_send.at[i], edge_recv.at[i], partner)
        for i, partner in enumerate(sides)
    ]
    for each in copies:
        each.start()
    for r in (0, 2, 1, 3):
        if r > 0:
            started[0, r].wait_recv()
        source = shard if r == 0 else whole.at[place, lines[r], 0]
        if r == 2:
            start(0, 3, source, place, lines[r], to(place, lines[1]))
        start(1, r, source, place, lines[r], to(by_x, line))
        start(2, r, source, place, lines[r], to(by_y, line))
        start(3, r, source, place, lines[r], to(by_core, line))
    more = {
        (i, r): remote(
            target.at[2] if r == 3 else other,
            target.at[r],
            line_send.at[i, r],
            line_recv.at[i, r],
            to(place, lines[2 if r == 2 else 1]),
        )
        for i, (other, target) in enumerate(zip(others, lined))
        for r in (2, 1, 3)
    }
    for (i, r), each in more.items():
        if r < 3:
            each.start()
    for r in (0, 2, 1, 3):
        z = lines[r]
        started[1, r].wait_recv()
        if r < 2:
            start(4, r, whole.at[by_x, z, 0], by_x, z, to(by_y, line))
        start(5, r, whole.at[by_x, z, 0], by_x, z, to(by_core, line))
        started[2, r].wait_recv()
        if r >= 2:
            start(4, r, whole.at[by_y, z, 0], by_y, z, to(by_x, line))
        start(6, r, whole.at[by_y, z, 0], by_y, z, to(by_core, line))
    for i in range(count):
        more[i, 2].wait_recv()
        more[i, 3].start()
    for r in (0, 2, 1, 3):
        z = lines[r]
        started[4, r].wait_recv()
        start(7, r, whole.at[corner, z, 0], corner, z, to(by_core, line))
    for (row, r), each in started.items():
        each.wait_send()
        if row in (3, 5, 6, 7):
            each.wait_recv()
    for (i, r), each in more.items():
        each.wait_send()
        if r != 2:
            each.wait_recv()
    for each in copies:
        each.wait()


def gather_first(shard, edge, others):
    seq, head = lax.axis_size("seq"), lax.axis_size("head")
    if not paired():
        return gather(shard[None]), jnp.stack([shift(edge, 1), shift(edge, -1)]), [None] * len(others)
    anywhere = pl.BlockSpec(memory_space=pl.ANY)
    count = len(others)
    dma = pltpu.SemaphoreType.DMA
    whole, edges, *lined = pl.pallas_call(
        gather_kernel,
        in_specs=[anywhere] * (2 + count),
        out_specs=[anywhere] * (2 + count),
        out_shape=[
            jax.ShapeDtypeStruct((seq, head, 1) + shard.shape, bf16),
            jax.ShapeDtypeStruct((2,) + edge.shape, bf16),
        ]
        + [jax.ShapeDtypeStruct((head,) + other.shape, bf16) for other in others],
        scratch_shapes=[
            dma((8, 4)),
            dma((8, 4)),
            dma((1 + count,)),
            dma((count, 4)),
            dma((count, 4)),
            dma((2,)),
            dma((2,)),
        ],
        compiler_params=pltpu.CompilerParams(collective_id=0, has_side_effects=True),
        cost_estimate=cost(100e9),
    )(shard, edge, *others)
    return whole, edges, lined


class Pieces:
    def __init__(self, shard, own=None):
        self.shard = shard
        self.columns = shard.shape[1]
        self.order = by_place(jnp.arange(lax.axis_size("head"), dtype=jnp.int32))
        if paired():
            if own is None:
                two = swap(shard, 2, "head")
                one = swap(jnp.stack([shard, two]), 1, "head")
                own = jnp.stack([shard, one[0], two, one[1]])
            self.own = own
        else:
            own = lax.all_gather(shard, "head")
            self.own = lax.all_gather(own, "seq", axis=1, tiled=True)
            self.pieces, self.offsets = [(self.own, 0)], jnp.zeros((1,), jnp.int32)

    def sides(self, *after):
        if paired():
            own = tie(self.own, *after) if after else self.own
            self.by_x, self.by_y = swap(own, SIDE_X), swap(own, SIDE_Y)
            return self.by_x, self.by_y
        return ()

    def far(self, *after):
        if not paired():
            return
        by_x, by_y = self.by_x[:2], self.by_y[2:]
        if after:
            by_x, by_y = tie(by_x, *after), tie(by_y, *after)
        far_a, far_b = swap(by_x, SIDE_Y), swap(by_y, SIDE_X)
        mine = [(self.own, 0), (self.by_x, 0), (self.by_y, 0), (far_a, 0), (far_b, 2)]
        self.pieces = mine + [(swap(piece, CORE), start) for piece, start in mine]
        sides = (0, SIDE_X, SIDE_Y, SIDE_X | SIDE_Y, SIDE_X | SIDE_Y)
        sides = sides + tuple(side | CORE for side in sides)
        rows = self.shard.shape[0]
        self.offsets = (lax.axis_index("seq") ^ jnp.array(sides, jnp.int32)) * rows

    @property
    def places(self):
        return self.own.shape[0]

    def specs(self):
        def spec(piece, start):
            last = piece.shape[0] - 1
            return pl.BlockSpec(
                (1,) + piece.shape[1:], lambda z, o, p: (jnp.clip(z - start, 0, last), 0, 0)
            )

        return [spec(piece, start) for piece, start in self.pieces]

    def fill(self, offsets, refs, weight):
        z = pl.program_id(0)
        for i, (ref, (piece, start)) in enumerate(zip(refs, self.pieces)):
            count, rows, _ = piece.shape

            def put():
                at = pl.multiple_of(offsets[i], 16)
                weight[pl.ds(at, rows)] = ref[0]

            if count == self.places:
                put()
            else:
                pl.when((z >= start) & (z < start + count))(put)


def grad_kernel(first, plane, left0, left1, right0, right1, send, keep, rows0, rows1):
    _, width, tokens = left0.shape

    @pl.when(pl.program_id(0) == 0)
    def _():
        for i in range(4):
            rows0[i * width : (i + 1) * width] = left0[plane[0] ^ i]
            rows1[i * width : (i + 1) * width] = left1[plane[0] ^ i]

    total = dot(rows0[...], right0[0, 0]) + dot(rows1[...], right1[0, 0])
    total = total.astype(bf16)
    far = first // 2
    near = 3 ^ far
    for i, at in enumerate((0, near)):
        keep[i, 0] = total[at * width : (at + 1) * width]
        at ^= far
        send[i, 0] = total[at * width : (at + 1) * width]


def weight_grads(plane, left0, left1, right0, right1, kind, start, first, light):
    count, _, tokens, columns = right0.shape
    count //= 2
    width = left0.shape[1]
    left = pl.BlockSpec(left0.shape, lambda z, p: (0, 0, 0))
    right = pl.BlockSpec((1, 1, tokens, columns), lambda z, p: (z + start, kind, 0, 0))
    out = pl.BlockSpec((2, 1, width, columns), lambda z, p: (0, z, 0, 0))
    shape = jax.ShapeDtypeStruct((2, count, width, columns), bf16)
    return pl.pallas_call(
        functools.partial(grad_kernel, first),
        grid_spec=pltpu.PrefetchScalarGridSpec(
            num_scalar_prefetch=1,
            grid=(count,),
            in_specs=[left, left, right, right],
            out_specs=[out, out],
            scratch_shapes=[pltpu.VMEM((4 * width, tokens), bf16)] * 2,
        ),
        out_shape=[shape, shape],
        compiler_params=pltpu.CompilerParams(vmem_limit_bytes=VMEM),
        cost_estimate=cost(1 if light else count * 20 * width * tokens * columns),
    )(plane, left0, left1, right0, right1)


class Left:
    def __init__(self, rows):
        self.rows = rows
        if paired():
            blocks = rows.T.reshape(4, 2, D // 8, -1)
            core = lax.axis_index("seq") % 2
            pick = lambda c: lax.dynamic_index_in_dim(blocks, c, 1, keepdims=False)
            self.near, self.far = pick(core), swap(pick(1 - core), CORE)

    def pending(self):
        return (self.far,) if paired() else ()


class Scatter:
    def __init__(self, left, right, relative=False, other=None, kind=0):
        self.right = right
        self.left = left
        self.relative = relative
        self.kind = kind
        if paired():
            self.other = swap(right, CORE) if other is None else other

    def given(self):
        return (self.other,) + self.left.pending() if paired() else ()

    def other_side(self):
        return (self.other,) if paired() else (None,)

    def first(self):
        made = self.products()
        self.go()
        return made

    def products(self, light=False):
        self.made = []
        if not paired():
            return ()
        half = self.right.shape[0] // 2
        plane = (lax.axis_index("seq") // 2).reshape(1)
        self.kept = []
        for start, side in ((0, SIDE_X), (half, SIDE_Y)):
            send, keep = weight_grads(
                plane,
                self.left.near,
                self.left.far,
                self.right,
                self.other,
                self.kind,
                start,
                side,
                light,
            )
            self.made.append(send)
            self.kept.append(keep)
        return tuple(self.made)

    def go(self, *after):
        if paired():
            made = [tie(send, *after) for send in self.made] if after else self.made
            self.arrived = [swap(send, side) for send, side in zip(made, (SIDE_X, SIDE_Y))]
            self.coming = self.arrived

    def second(self, *after):
        if not paired():
            return ()
        self.sums, made = [], []
        for keep, arrived, side in zip(self.kept, self.arrived, (SIDE_Y, SIDE_X)):
            if after:
                arrived = tie(arrived, *after)
            go = (keep[1].astype(f32) + arrived[1].astype(f32)).astype(bf16)
            stay = keep[0].astype(f32) + arrived[0].astype(f32)
            made.append(go)
            self.sums.append((stay, swap(go, side)))
        self.coming = [arrived for _, arrived in self.sums]
        return tuple(made)

    def pending(self):
        return tuple(self.coming) if paired() else ()

    def last(self, *after):
        if not paired():
            whole = jnp.einsum(
                "td,htc->hdc", self.left.rows, self.right[:, self.kind], preferred_element_type=f32
            ).astype(bf16)
            seq = lax.axis_size("seq")
            whole = whole.reshape(whole.shape[:1] + (seq, D // seq, -1))
            return lax.psum_scatter(whole, "seq", scatter_dimension=1)
        sums = []
        for stay, arrived in self.sums:
            if after:
                arrived = tie(arrived, *after)
            sums.append((stay + arrived.astype(f32)).astype(bf16))
        sums = jnp.concatenate(sums, axis=0)
        if self.relative:
            sums = by_place(sums)
        return sums


class Along:
    def __init__(self, blocks):
        if not paired():
            self.total = lax.psum_scatter(blocks, "head", scatter_dimension=0).astype(f32)
            self.coming, self.sent = (), ()
            return
        here = lax.axis_index("head")
        pick = lambda r: lax.dynamic_index_in_dim(blocks, here ^ r, 0, keepdims=False)
        self.kept = (pick(0), pick(2))
        sent = jnp.stack([pick(1), pick(3)])
        self.sent = (sent,)
        self.coming = (swap(sent, 1, "head"),)

    def go(self, *after):
        if not paired():
            return
        (arrived,) = self.coming
        if after:
            arrived = tie(arrived, *after)
        self.stay = self.kept[0].astype(f32) + arrived[0].astype(f32)
        sent = (self.kept[1].astype(f32) + arrived[1].astype(f32)).astype(bf16)
        self.sent = (sent,)
        self.coming = (swap(sent, 2, "head"),)

    def finish(self, *after):
        if not paired():
            return self.total
        (arrived,) = self.coming
        if after:
            arrived = tie(arrived, *after)
        return self.stay + arrived.astype(f32)


def whole_rows(ref, kind=0):
    block = ref[:, 0, kind]
    return block.reshape(D, block.shape[-1])


def weight_spec(weight, kinds=1, at=0):
    seq, _, _, _, columns = weight.shape
    return pl.BlockSpec((seq, 1, kinds, D // seq, columns), lambda z: (0, z, at, 0, 0))


def into_kernel(x_ref, w_ref, out_ref):
    out_ref[0] = dot(x_ref[...], whole_rows(w_ref)).astype(out_ref.dtype)


def into(x, weight, kind):
    count, columns = weight.shape[1], weight.shape[-1]
    tokens = x.shape[0]
    return pl.pallas_call(
        into_kernel,
        grid=(count,),
        in_specs=[
            pl.BlockSpec(x.shape, lambda z: (0, 0)),
            weight_spec(weight),
        ],
        out_specs=pl.BlockSpec((1, tokens, columns), lambda z: (z, 0, 0)),
        out_shape=jax.ShapeDtypeStruct((count, tokens, columns), kind),
        compiler_params=pltpu.CompilerParams(vmem_limit_bytes=VMEM),
        cost_estimate=cost(count * 3 * D * tokens * columns),
    )(x, weight)


def out_of_kernel(y_ref, w_ref, out_ref):
    @pl.when(pl.program_id(0) == 0)
    def _():
        out_ref[...] = jnp.zeros_like(out_ref)

    out_ref[...] += dot_rt(y_ref[0], whole_rows(w_ref))


def out_of(y, weight):
    count, tokens, columns = y.shape
    return pl.pallas_call(
        out_of_kernel,
        grid=(count,),
        in_specs=[
            pl.BlockSpec((1, tokens, columns), lambda z: (z, 0, 0)),
            weight_spec(weight),
        ],
        out_specs=pl.BlockSpec((tokens, D), lambda z: (0, 0)),
        out_shape=jax.ShapeDtypeStruct((tokens, D), f32),
        compiler_params=pltpu.CompilerParams(vmem_limit_bytes=VMEM),
        cost_estimate=cost(1),
    )(y, weight)


def into_pieces_kernel(lay, weights, offsets, places, x_ref, *refs):
    count = len(weights.pieces)
    refs, outs, weight = refs[:count], refs[count:-1], refs[-1]
    weights.fill(offsets, refs, weight)
    rows = dot(x_ref[...], weight[...])
    for b in range(lay.batch):
        here = slice(b * lay.tokens, (b + 1) * lay.tokens)
        for i in range(lay.splits):
            for j, out in enumerate(outs):
                out[b, i, 0, :, :WIDTH] = rows[here, lay.columns(i, j)[0]].astype(bf16)
                out[b, i, 0, :, WIDTH:] = jnp.zeros_like(out[b, i, 0, :, WIDTH:])


def into_pieces(lay, x, weights):
    count, columns = weights.places, weights.columns
    block = (lay.batch, lay.splits, 1, lay.tokens, LANES)
    return pl.pallas_call(
        functools.partial(into_pieces_kernel, lay, weights),
        grid_spec=pltpu.PrefetchScalarGridSpec(
            num_scalar_prefetch=2,
            grid=(count,),
            in_specs=[pl.BlockSpec(x.shape, lambda z, o, p: (0, 0))] + weights.specs(),
            out_specs=[pl.BlockSpec(block, lambda z, o, p: (0, 0, p[z], 0, 0))] * lay.heads,
            scratch_shapes=[pltpu.VMEM((D, columns), bf16)],
        ),
        out_shape=[jax.ShapeDtypeStruct(block[:2] + (count,) + block[3:], bf16)] * lay.heads,
        compiler_params=pltpu.CompilerParams(vmem_limit_bytes=VMEM),
        cost_estimate=cost(count * 3 * D * x.shape[0] * columns),
    )(weights.offsets, weights.order, x, *[piece for piece, _ in weights.pieces])


def out_of_pieces_kernel(lay, weights, offsets, places, *refs):
    ys, refs, (rows_ref, out_ref, weight) = refs[: lay.heads], refs[lay.heads : -3], refs[-3:]
    weights.fill(offsets, refs, weight)

    @pl.when(pl.program_id(0) == 0)
    def _():
        out_ref[...] = jnp.zeros_like(out_ref)

    end = lay.splits * lay.heads * WIDTH
    rows_ref[0, 0, :, end:] = jnp.zeros_like(rows_ref[0, 0, :, end:])
    for b in range(lay.batch):
        here = slice(b * lay.tokens, (b + 1) * lay.tokens)
        for i in range(lay.splits):
            for j, y_ref in enumerate(ys):
                rows_ref[0, 0, here, lay.columns(i, j)[0]] = y_ref[b, i, 0, :, :WIDTH]
    out_ref[...] += dot_rt(rows_ref[0, 0], weight[...])


def out_of_pieces(lay, ys, weights):
    count, columns = weights.places, weights.columns
    tokens = lay.batch * lay.tokens
    block = (lay.batch, lay.splits, 1, lay.tokens, LANES)
    return pl.pallas_call(
        functools.partial(out_of_pieces_kernel, lay, weights),
        grid_spec=pltpu.PrefetchScalarGridSpec(
            num_scalar_prefetch=2,
            grid=(count,),
            in_specs=[pl.BlockSpec(block, lambda z, o, p: (0, 0, p[z], 0, 0))] * lay.heads
            + weights.specs(),
            out_specs=[
                pl.BlockSpec((1, 1, tokens, columns), lambda z, o, p: (z, 0, 0, 0)),
                pl.BlockSpec((tokens, D), lambda z, o, p: (0, 0)),
            ],
            scratch_shapes=[pltpu.VMEM((D, columns), bf16)],
        ),
        out_shape=[
            jax.ShapeDtypeStruct((count, 1, tokens, columns), bf16),
            jax.ShapeDtypeStruct((tokens, D), f32),
        ],
        compiler_params=pltpu.CompilerParams(vmem_limit_bytes=VMEM),
        cost_estimate=cost(count * 3 * D * tokens * columns),
    )(weights.offsets, weights.order, *ys, *[piece for piece, _ in weights.pieces])


def spread_kernel(weights, offsets, places, x_ref, *refs):
    refs, (out_ref, weight) = refs[:-2], refs[-2:]
    weights.fill(offsets, refs, weight)
    out_ref[0] = dot(x_ref[...], weight[...])


def spread(x, weights):
    count, columns = weights.places, weights.columns
    tokens = x.shape[0]
    return pl.pallas_call(
        functools.partial(spread_kernel, weights),
        grid_spec=pltpu.PrefetchScalarGridSpec(
            num_scalar_prefetch=2,
            grid=(count,),
            in_specs=[pl.BlockSpec(x.shape, lambda z, o, p: (0, 0))] + weights.specs(),
            out_specs=pl.BlockSpec((1, tokens, columns), lambda z, o, p: (p[z], 0, 0)),
            scratch_shapes=[pltpu.VMEM((D, columns), bf16)],
        ),
        out_shape=jax.ShapeDtypeStruct((count, tokens, columns), f32),
        compiler_params=pltpu.CompilerParams(vmem_limit_bytes=VMEM),
        cost_estimate=cost(count * 3 * D * tokens * columns),
    )(weights.offsets, weights.order, x, *[piece for piece, _ in weights.pieces])


def collect_kernel(weights, offsets, places, y_ref, *refs):
    refs, (out_ref, weight) = refs[:-2], refs[-2:]
    weights.fill(offsets, refs, weight)

    @pl.when(pl.program_id(0) == 0)
    def _():
        out_ref[...] = jnp.zeros_like(out_ref)

    out_ref[...] += dot_rt(y_ref[0, 0], weight[...])


def collect(y, weights):
    count, _, tokens, columns = y.shape
    return pl.pallas_call(
        functools.partial(collect_kernel, weights),
        grid_spec=pltpu.PrefetchScalarGridSpec(
            num_scalar_prefetch=2,
            grid=(count,),
            in_specs=[pl.BlockSpec((1,) + y.shape[1:], lambda z, o, p: (p[z], 0, 0, 0))]
            + weights.specs(),
            out_specs=pl.BlockSpec((tokens, D), lambda z, o, p: (0, 0)),
            scratch_shapes=[pltpu.VMEM((D, columns), bf16)],
        ),
        out_shape=jax.ShapeDtypeStruct((tokens, D), f32),
        compiler_params=pltpu.CompilerParams(vmem_limit_bytes=VMEM),
        cost_estimate=cost(count * 3 * D * tokens * columns),
    )(weights.offsets, weights.order, y, *[piece for piece, _ in weights.pieces])


def hidden_kernel(x_ref, gu_ref, slope_ref, silu_ref, hidden_ref):
    gate = dot(x_ref[...], whole_rows(gu_ref, 0))
    sig = jax.nn.sigmoid(gate)
    silu = gate * sig
    up = dot(x_ref[...], whole_rows(gu_ref, 1))
    slope_ref[0] = (up * sig * (1.0 + gate * (1.0 - sig))).astype(bf16)
    silu_ref[0] = silu.astype(bf16)
    columns = gate.shape[1]
    hidden_ref[0, 0, :, :columns] = (silu * up).astype(bf16)
    hidden_ref[0, 0, :, columns:] = jnp.zeros_like(hidden_ref[0, 0, :, columns:])


def hidden_of(x, weight):
    count, columns = weight.shape[1], weight.shape[-1]
    padded = grouped(columns, LANES)
    tokens = x.shape[0]
    act = pl.BlockSpec((1, tokens, columns), lambda z: (z, 0, 0))
    kept = jax.ShapeDtypeStruct((count, tokens, columns), bf16)
    return pl.pallas_call(
        hidden_kernel,
        grid=(count,),
        in_specs=[pl.BlockSpec(x.shape, lambda z: (0, 0)), weight_spec(weight, kinds=2)],
        out_specs=[act, act, pl.BlockSpec((1, 1, tokens, padded), lambda z: (z, 0, 0, 0))],
        out_shape=[kept, kept, jax.ShapeDtypeStruct((count, 1, tokens, padded), bf16)],
        compiler_params=pltpu.CompilerParams(vmem_limit_bytes=VMEM),
        cost_estimate=cost(count * 6 * D * tokens * columns),
    )(x, weight)


def hidden_back_kernel(grad_ref, gu_ref, slope_ref, silu_ref, grads_ref, out_ref):
    @pl.when(pl.program_id(0) == 0)
    def _():
        out_ref[...] = jnp.zeros_like(out_ref)

    columns = slope_ref.shape[-1]
    grad_hidden = grad_ref[0, :, :columns]
    grad_gate = (grad_hidden * slope_ref[0].astype(f32)).astype(bf16)
    grad_up = (grad_hidden * silu_ref[0].astype(f32)).astype(bf16)
    grads_ref[0, 0, :, :columns] = grad_gate
    grads_ref[0, 1, :, :columns] = grad_up
    grads_ref[0, :, :, columns:] = jnp.zeros_like(grads_ref[0, :, :, columns:])
    out_ref[...] += dot_rt(grad_gate, whole_rows(gu_ref, 0)) + dot_rt(
        grad_up, whole_rows(gu_ref, 1)
    )


def hidden_back(grad, weight, slope, silu):
    count, columns = weight.shape[1], weight.shape[-1]
    padded = grouped(columns, LANES)
    tokens = grad.shape[1]
    act = pl.BlockSpec((1, tokens, columns), lambda z: (z, 0, 0))
    return pl.pallas_call(
        hidden_back_kernel,
        grid=(count,),
        in_specs=[
            pl.BlockSpec((1, tokens, padded), lambda z: (z, 0, 0)),
            weight_spec(weight, kinds=2),
            act,
            act,
        ],
        out_specs=[
            pl.BlockSpec((1, 2, tokens, padded), lambda z: (z, 0, 0, 0)),
            pl.BlockSpec((tokens, D), lambda z: (0, 0)),
        ],
        out_shape=[
            jax.ShapeDtypeStruct((count, 2, tokens, padded), bf16),
            jax.ShapeDtypeStruct((tokens, D), f32),
        ],
        compiler_params=pltpu.CompilerParams(vmem_limit_bytes=VMEM),
        cost_estimate=cost(1),
    )(grad, weight, slope, silu)


def inverse_rms(rows):
    return lax.rsqrt(jnp.mean(rows * rows, axis=-1, keepdims=True) + EPSILON)


def norm_back(rows, scale, gain, grad):
    unit = rows * scale
    scaled = gain * grad
    return scale * (scaled - unit * jnp.mean(scaled * unit, axis=-1, keepdims=True))


class Layout:
    def __init__(self, batch, tokens):
        seq, head = lax.axis_size("seq"), lax.axis_size("head")
        self.batch, self.tokens, self.head = batch, tokens, head
        self.splits = min(seq // batch, HEADS // head)
        self.heads = HEADS // (head * self.splits)
        self.parts = seq // (batch * self.splits)
        self.inner = seq // self.parts
        self.sets = LANES // FEAT
        self.key_rows = grouped(tokens // self.sets, 16)
        self.length = tokens * seq * head
        count = self.inner * head
        self.groups = None
        if self.parts > 1:
            self.groups = [list(range(k * count, (k + 1) * count)) for k in range(self.parts)]
            self.mates = [[k * count + i for k in range(self.parts)] for i in range(count)]

    def sequence(self):
        return lax.rem(lax.axis_index("seq"), self.inner) // self.splits

    def pack_keys(self, keys):
        lead, each = keys.shape[:-2], self.tokens // self.sets
        keys = keys.reshape(lead + (self.sets, each, FEAT))
        keys = jnp.swapaxes(keys, -3, -2).reshape(lead + (each, LANES))
        return jnp.pad(keys, [(0, 0)] * len(lead) + [(0, self.key_rows - each), (0, 0)])

    def unpack_keys(self, rows):
        lead, each = rows.shape[:-2], self.tokens // self.sets
        rows = rows[..., :each, :].reshape(lead + (each, self.sets, FEAT))
        return jnp.swapaxes(rows, -3, -2).reshape(lead + (self.tokens, FEAT))

    def columns(self, i, j):
        at = i * self.heads + j
        return slice(at * WIDTH, (at + 1) * WIDTH), slice(at * FEAT, (at + 1) * FEAT)

    def by_place(self, blocks):
        return blocks.reshape((self.batch, self.splits, self.head) + blocks.shape[1:])

    def exchange(self, blocks):
        return lax.all_to_all(blocks, BOTH, 0, 0, tiled=True, axis_index_groups=self.groups)

    def all_parts(self, rows):
        if self.parts > 1:
            rows = lax.all_gather(rows, BOTH, axis=0, tiled=True, axis_index_groups=self.mates)
        return rows

    def own_part(self, blocks):
        if self.parts > 1:
            count = blocks.shape[0] // self.parts
            part = lax.axis_index("seq") // self.inner
            blocks = lax.dynamic_slice_in_dim(blocks, part * count, count, 0)
        return blocks


def fill_values(chunk, main, values, queries):
    lane = lax.broadcasted_iota(jnp.int32, (chunk, LANES), 1)
    ones = jnp.where(lane < WIDTH + 2, 1.0, 0.0)

    def turn(i, _):
        here = pl.ds(pl.multiple_of(i * chunk, chunk), chunk)
        rows = main[here]
        values[here] = jnp.where(lane < WIDTH, rows.astype(f32), ones).astype(bf16)
        queries[here] = rows[:, WIDTH:]
        return 0

    lax.fori_loop(0, main.shape[0] // chunk, turn, 0)


def attend_kernel(chunk, main, keys, seg_col, seg_row, out_ref, low_ref, values, queries):
    at = pl.program_id(0)

    @pl.when(at == 0)
    def _():
        fill_values(chunk, main, values, queries)

    mine = seg_col[...]
    query = queries[pl.ds(pl.multiple_of(at * chunk, chunk), chunk)]

    def weighted(j, causal):
        here = pl.ds(pl.multiple_of(j * chunk, chunk), chunk)
        scores = dot_rt(query, keys[here])
        allowed = mine == seg_row[j]
        if causal:
            later = lax.broadcasted_iota(jnp.int32, scores.shape, 0)
            allowed &= later >= lax.broadcasted_iota(jnp.int32, scores.shape, 1)
        weights = jnp.where(allowed, 1.0 + scores * (1.0 + 0.5 * scores), 0.0).astype(bf16)
        return dot(weights, values[here])

    total = lax.fori_loop(
        0, at, lambda j, acc: acc + weighted(j, False), jnp.zeros((chunk, LANES), f32)
    )
    total = total + weighted(at, True)
    norm = total[:, WIDTH : WIDTH + 1]
    lane = lax.broadcasted_iota(jnp.int32, total.shape, 1)
    total = jnp.where(lane < WIDTH, total / norm, norm)
    out_ref[...] = total
    low_ref[...] = total.astype(bf16)


def attend(main, keys, seg):
    length = main.shape[0]
    chunk = min(512, length)
    steps = length // chunk
    part = pl.BlockSpec((chunk, LANES), lambda i: (i, 0))
    return pl.pallas_call(
        functools.partial(attend_kernel, chunk),
        grid=(steps,),
        in_specs=[
            pl.BlockSpec((length, LANES), lambda i: (0, 0)),
            pl.BlockSpec((length, FEAT), lambda i: (0, 0)),
            pl.BlockSpec((chunk, 1), lambda i: (i, 0)),
            pl.BlockSpec((steps, 1, chunk), lambda i: (0, 0, 0)),
        ],
        out_specs=[part, part],
        out_shape=[
            jax.ShapeDtypeStruct((length, LANES), f32),
            jax.ShapeDtypeStruct((length, LANES), bf16),
        ],
        scratch_shapes=[pltpu.VMEM((length, LANES), bf16), pltpu.VMEM((length, FEAT), bf16)],
        compiler_params=pltpu.CompilerParams(vmem_limit_bytes=VMEM),
        cost_estimate=cost(length * length * 12 * LANES),
    )(main, keys, seg.reshape(length, 1), seg.reshape(steps, 1, chunk))


def attend_back_kernel(
    chunk,
    main,
    keys,
    kept,
    grad,
    seg_col,
    seg_row,
    out_ref,
    gk_ref,
    values,
    queries,
    grad_n,
    grad_q,
):
    at = pl.program_id(0)
    steps = main.shape[0] // chunk

    @pl.when(at == 0)
    def _():
        fill_values(chunk, main, values, queries)
        grad_q[...] = jnp.zeros_like(grad_q)
        lane = lax.broadcasted_iota(jnp.int32, (chunk, LANES), 1)

        def turn(i, _):
            here = pl.ds(pl.multiple_of(i * chunk, chunk), chunk)
            rows = kept[here]
            low = jnp.where(lane < WIDTH, grad[here].astype(f32), 0.0)
            inverse = 1.0 / rows[:, WIDTH : WIDTH + 1]
            total = -jnp.sum(low * rows, axis=1, keepdims=True) * inverse
            high = total.astype(bf16).astype(f32)
            low = low * inverse
            low = jnp.where(lane == WIDTH, high, low)
            grad_n[here] = jnp.where(lane == WIDTH + 1, total - high, low).astype(bf16)
            return 0

        lax.fori_loop(0, steps, turn, 0)

    mine = seg_col[...]
    rows = pl.ds(pl.multiple_of(at * chunk, chunk), chunk)
    key, value = keys[rows], values[rows]
    key_t = key.astype(f32).T.astype(bf16)

    def turn(i, carry, causal):
        grad_k, grad_v = carry
        here = pl.ds(pl.multiple_of(i * chunk, chunk), chunk)
        query, grad_here = queries[here], grad_n[here]
        scores = dot_rt(key, query)
        allowed = mine == seg_row[i]
        if causal:
            key_at = lax.broadcasted_iota(jnp.int32, scores.shape, 0)
            allowed &= key_at <= lax.broadcasted_iota(jnp.int32, scores.shape, 1)
        weights = jnp.where(allowed, 1.0 + scores * (1.0 + 0.5 * scores), 0.0).astype(bf16)
        grad_s = dot_rt(value, grad_here) * (1.0 + scores)
        grad_s = jnp.where(allowed, grad_s, 0.0).astype(bf16)
        grad_q[:, here] += dot(key_t, grad_s)
        return grad_k + dot(grad_s, query), grad_v + dot(weights, grad_here)

    carry = (jnp.zeros((chunk, FEAT), f32), jnp.zeros((chunk, LANES), f32))
    carry = turn(at, carry, True)
    grad_k, grad_v = lax.fori_loop(at + 1, steps, lambda i, c: turn(i, c, False), carry)
    gk_ref[...] = (0.5 * grad_k).astype(bf16)
    out_ref[rows] = grad_v.astype(bf16)

    @pl.when(at == steps - 1)
    def _():
        def turn(i, _):
            here = pl.ds(pl.multiple_of(i * chunk, chunk), chunk)
            out_ref[here, WIDTH:] = (0.5 * grad_q[:, here].T).astype(bf16)
            return 0

        lax.fori_loop(0, steps, turn, 0)


def attend_back(main, keys, kept, grad, seg):
    length = main.shape[0]
    chunk = min(512, length)
    steps = length // chunk
    whole = pl.BlockSpec((length, LANES), lambda i: (0, 0))
    return pl.pallas_call(
        functools.partial(attend_back_kernel, chunk),
        grid=(steps,),
        in_specs=[
            whole,
            pl.BlockSpec((length, FEAT), lambda i: (0, 0)),
            whole,
            whole,
            pl.BlockSpec((chunk, 1), lambda i: (i, 0)),
            pl.BlockSpec((steps, 1, chunk), lambda i: (0, 0, 0)),
        ],
        out_specs=[whole, pl.BlockSpec((chunk, FEAT), lambda i: (i, 0))],
        out_shape=[
            jax.ShapeDtypeStruct((length, LANES), bf16),
            jax.ShapeDtypeStruct((length, FEAT), bf16),
        ],
        scratch_shapes=[
            pltpu.VMEM((length, LANES), bf16),
            pltpu.VMEM((length, FEAT), bf16),
            pltpu.VMEM((length, LANES), bf16),
            pltpu.VMEM((FEAT, length), f32),
        ],
        compiler_params=pltpu.CompilerParams(vmem_limit_bytes=VMEM),
        cost_estimate=cost(length * length * 24 * LANES),
    )(main, keys, kept, grad, seg.reshape(length, 1), seg.reshape(steps, 1, chunk))


def earlier(rows, before, distance):
    moved = pltpu.roll(rows, distance, 0)
    place = lax.broadcasted_iota(jnp.int32, rows.shape, 0)
    for i in range(distance):
        at = 2 - distance + i
        moved = jnp.where(place == i, before[at : at + 1], moved)
    return moved


def later(rows, after, distance):
    count = rows.shape[0]
    moved = pltpu.roll(rows, count - distance, 0)
    place = lax.broadcasted_iota(jnp.int32, rows.shape, 0)
    for i in range(distance):
        moved = jnp.where(place == count - distance + i, after[i : i + 1], moved)
    return moved


def short_filter(taps, same, values, before):
    one_back = earlier(values, before, 1) * same[:, 0:1]
    two_back = earlier(values, before, 2) * same[:, 1:2]
    return taps[0:1] * values + taps[1:2] * one_back + taps[2:3] * two_back, one_back, two_back


def project_kernel(lay, x_ref, side_ref, same_ref, taps_ref, w_ref, v_ref, f_ref, side_out, *outs):
    weight = whole_rows(w_ref)
    q_width, v_width = lay.splits * lay.heads * FEAT, v_ref.shape[-1]
    v_at, f_at = 2 * q_width, 2 * q_width + v_width
    full = dot(x_ref[...], weight)
    side = dot(side_ref[...], weight)
    low = full[:, v_at:f_at].astype(bf16)
    v_ref[0] = low
    f_ref[0] = full[:, f_at:]
    side_v = side[:, v_at:f_at].astype(bf16).astype(f32)
    side_out[0, 0] = side_v
    side_out[0, 1] = side[:, f_at:]
    taps = taps_ref[0]
    for b in range(lay.batch):
        rows = slice(b * lay.tokens, (b + 1) * lay.tokens)
        pre = full[rows, f_at:]
        filtered, _, _ = short_filter(
            taps, same_ref[rows], low[rows].astype(f32), side_v[2 * b : 2 * b + 2]
        )
        mixed = filtered * (pre * jax.nn.sigmoid(pre))
        query = 0.5 * full[rows, :q_width].astype(bf16).astype(f32)
        key = 0.5 * full[rows, q_width:v_at].astype(bf16).astype(f32)
        for i in range(lay.splits):
            for j in range(lay.heads):
                main, k_ref = outs[2 * j : 2 * j + 2]
                v_cols, q_cols = lay.columns(i, j)
                main[b, i, 0, :, :WIDTH] = mixed[:, v_cols].astype(bf16)
                main[b, i, 0, :, WIDTH:] = query[:, q_cols].astype(bf16)
                k_ref[b, i, 0] = key[:, q_cols].astype(bf16)


def project(lay, x, side, same, taps, weight):
    tokens, head = x.shape[0], lay.head
    v_width = taps.shape[-1]
    beside = side.shape[0]
    to_all = lambda width: pl.BlockSpec(
        (lay.batch, lay.splits, 1, lay.tokens, width), lambda z: (0, 0, z, 0, 0)
    )
    shape = lambda width: jax.ShapeDtypeStruct(
        (lay.batch, lay.splits, head, lay.tokens, width), bf16
    )
    kept = pl.BlockSpec((1, tokens, v_width), lambda z: (z, 0, 0))
    return pl.pallas_call(
        functools.partial(project_kernel, lay),
        grid=(head,),
        in_specs=[
            pl.BlockSpec(x.shape, lambda z: (0, 0)),
            pl.BlockSpec(side.shape, lambda z: (0, 0)),
            pl.BlockSpec(same.shape, lambda z: (0, 0)),
            pl.BlockSpec((1, 3, v_width), lambda z: (z, 0, 0)),
            weight_spec(weight),
        ],
        out_specs=[
            kept,
            kept,
            pl.BlockSpec((1, 2, beside, v_width), lambda z: (z, 0, 0, 0)),
        ]
        + [to_all(LANES), to_all(FEAT)] * lay.heads,
        out_shape=[
            jax.ShapeDtypeStruct((head, tokens, v_width), bf16),
            jax.ShapeDtypeStruct((head, tokens, v_width), f32),
            jax.ShapeDtypeStruct((head, 2, beside, v_width), f32),
        ]
        + [shape(LANES), shape(FEAT)] * lay.heads,
        compiler_params=pltpu.CompilerParams(vmem_limit_bytes=VMEM),
        cost_estimate=cost(head * 3 * D * tokens * weight.shape[-1]),
    )(x, side, same, taps, weight)


def project_back_kernel(
    lay, v_ref, f_ref, side_ref, same_ref, taps_ref, gk_ref, *refs
):
    backs, (out_ref, tap_ref, mixed, after) = refs[:-4], refs[-4:]
    q_width, v_width = gk_ref.shape[-1], v_ref.shape[-1]
    v_at, f_at = 2 * q_width, 2 * q_width + v_width
    taps = taps_ref[0]
    below = lay.tokens + lay.key_rows
    tap_ref[...] = jnp.zeros_like(tap_ref)
    out_ref[0, :, q_width:v_at] = gk_ref[0]
    for b in range(lay.batch):
        rows = slice(b * lay.tokens, (b + 1) * lay.tokens)
        for i in range(lay.splits):
            for j, back in enumerate(backs):
                v_cols, q_cols = lay.columns(i, j)
                block = back[b, i, 0, : lay.tokens]
                mixed[:, v_cols] = block[:, :WIDTH].astype(f32)
                out_ref[0, rows, q_cols] = block[:, WIDTH:]
                after[:, v_cols] = back[b, i, 0, below : below + 16, :WIDTH].astype(f32)
        grad_mixed = mixed[...]
        pre = f_ref[0, rows]
        sig = jax.nn.sigmoid(pre)
        values = v_ref[0, rows].astype(f32)
        same = same_ref[rows]
        at = 2 * b
        filtered, one_back, two_back = short_filter(
            taps, same, values, side_ref[0, 0, at : at + 2]
        )
        grad = grad_mixed * pre * sig
        at = 2 * (lay.batch + b)
        pre_after = side_ref[0, 1, at : at + 2]
        grad_after = after[0:2] * pre_after * jax.nn.sigmoid(pre_after)
        grad_v = (
            taps[0:1] * grad
            + taps[1:2] * later(grad, grad_after, 1) * same[:, 2:3]
            + taps[2:3] * later(grad, grad_after, 2) * same[:, 3:4]
        )
        out_ref[0, rows, v_at:f_at] = grad_v.astype(bf16)
        grad_f = grad_mixed * filtered * sig * (1.0 + pre * (1.0 - sig))
        out_ref[0, rows, f_at:] = grad_f.astype(bf16)
        for k, term in enumerate((values, one_back, two_back)):
            tap_ref[0, k : k + 1] += jnp.sum(grad * term, axis=0, keepdims=True)


def project_back(lay, backs, grad_keys, values, pre, side, same, taps):
    head, tokens, v_width = values.shape
    columns = 2 * (grad_keys.shape[-1] + v_width)
    kept = pl.BlockSpec((1, tokens, v_width), lambda z: (z, 0, 0))
    return pl.pallas_call(
        functools.partial(project_back_kernel, lay),
        grid=(head,),
        in_specs=[
            kept,
            kept,
            pl.BlockSpec((1,) + side.shape[1:], lambda z: (z, 0, 0, 0)),
            pl.BlockSpec(same.shape, lambda z: (0, 0)),
            pl.BlockSpec((1, 3, v_width), lambda z: (z, 0, 0)),
            pl.BlockSpec((1,) + grad_keys.shape[1:], lambda z: (z, 0, 0)),
        ]
        + [
            pl.BlockSpec(
                (lay.batch, lay.splits, 1) + back.shape[3:], lambda z: (0, 0, z, 0, 0)
            )
            for back in backs
        ],
        out_specs=[
            pl.BlockSpec((1, tokens, columns), lambda z: (z, 0, 0)),
            pl.BlockSpec((1, 3, v_width), lambda z: (z, 0, 0)),
        ],
        out_shape=[
            jax.ShapeDtypeStruct((head, tokens, columns), bf16),
            jax.ShapeDtypeStruct((head, 3, v_width), f32),
        ],
        scratch_shapes=[
            pltpu.VMEM((lay.tokens, v_width), f32),
            pltpu.VMEM((16, v_width), f32),
        ],
        compiler_params=pltpu.CompilerParams(vmem_limit_bytes=VMEM),
        cost_estimate=cost(1),
    )(values, pre, side, same, taps, grad_keys, *backs)


def shift(block, distance):
    devices = range(lax.axis_size("seq") * lax.axis_size("head"))
    return lax.ppermute(
        block, BOTH, [(i, i + distance) for i in devices if i + distance in devices]
    )


def local(
    tokens,
    cotangent,
    segment_ids,
    query_weight,
    key_weight,
    value_weight,
    filter_weight,
    out_weight,
    gate_weight,
    up_weight,
    down_weight,
    norm_gain,
    ffn_gain,
    conv_taps,
):
    seq, head = lax.axis_size("seq"), lax.axis_size("head")
    batch, span, _ = tokens.shape
    count = batch * span
    length = segment_ids.shape[1] * seq
    place = lax.axis_index("seq") * head + lax.axis_index("head")
    heads_here = HEADS // head
    qk_width, v_width = heads_here * FEAT, heads_here * WIDTH
    ff_width = gate_weight.shape[1]

    lay = Layout(batch, span)
    out_pad = grouped(v_width, LANES) - v_width
    first = jnp.concatenate([query_weight, key_weight, value_weight, filter_weight], axis=1)
    rows_here, columns = first.shape
    small = [norm_gain, ffn_gain, conv_taps.reshape(-1), segment_ids.astype(bf16).reshape(-1)]
    ends = [0]
    for part in small:
        ends.append(ends[-1] + part.size)
    below = grouped(-(-ends[-1] // columns), 16)
    small = jnp.pad(jnp.concatenate(small), (0, below * columns - ends[-1]))
    ff_pad = grouped(ff_width, LANES) - ff_width
    down_shard = jnp.pad(down_weight, ((0, 0), (0, ff_pad)))
    out_shard = jnp.pad(out_weight.T, ((0, 0), (0, out_pad)))
    edge = jnp.stack([tokens[:, -2:], tokens[:, :2]]).reshape(-1, D)
    edge = jnp.pad(edge, ((0, grouped(edge.shape[0], 16) - edge.shape[0]), (0, 0)))
    first_w, edges, lined = gather_first(
        jnp.concatenate([first, small.reshape(below, columns)]), edge, [down_shard, out_shard]
    )
    beside = jnp.concatenate([edges[0, : 2 * batch], edges[1, 2 * batch : 4 * batch]])
    gate_up_w = gather(tie(jnp.stack([gate_weight, up_weight]), first_w))
    down_w = Pieces(down_shard, lined[0])

    small = first_w[:, :, 0, rows_here:].reshape(seq, head, -1).astype(f32)
    part = lambda i: small[:, :, ends[i] : ends[i + 1]]
    gain_one, gain_two = part(0)[:, 0].reshape(1, D), part(1)[:, 0].reshape(1, D)
    taps = jnp.transpose(part(2).reshape(seq, head, 3, -1), (1, 2, 0, 3))
    taps = taps.reshape(head, 3, v_width)
    segs = jnp.swapaxes(part(3)[:, 0].reshape(seq, batch, -1), 0, 1).reshape(batch, length)
    x = tokens.reshape(count, D).astype(f32)
    cot_low = cotangent.reshape(count, D)

    def normed_of(rows):
        scale = inverse_rms(rows)
        return scale, (rows * scale * gain_one).astype(bf16)

    scale_one, normed = normed_of(x)
    _, normed_beside = normed_of(beside.astype(f32))
    around = lax.dynamic_slice(
        jnp.pad(segs, ((0, 0), (2, 2)), constant_values=-1.0),
        (0, place * span),
        (batch, span + 4),
    )
    seg_here = around[:, 2:-2]
    others = (around[:, 1:-3], around[:, :-4], around[:, 3:-1], around[:, 4:])
    same = jnp.stack([(seg_here == other).astype(f32) for other in others], axis=-1)
    same = same.reshape(count, 4)
    cot_left = Left(cot_low)
    normed = tie(normed, down_w.own, *cot_left.pending())
    out_w = Pieces(out_shard, lined[1])
    out_sides = out_w.sides(first_w)
    down_sides = down_w.sides(first_w)
    v_low, filter_pre, side, *sent = project(lay, normed, normed_beside, same, taps, first_w)
    my_seg = lax.dynamic_index_in_dim(segs, lay.sequence(), 0, keepdims=False)
    heads = range(lay.heads)
    mains, all_keys, kept, low = [], [], [], []
    for j in heads:
        blocks = jnp.concatenate([sent[2 * j], lay.pack_keys(sent[2 * j + 1])], axis=3)
        if j > 0:
            blocks = tie(blocks, mains[-1])
        blocks = lay.exchange(blocks.reshape(-1, span + lay.key_rows, LANES))
        mains.append(lay.all_parts(blocks[:, :span].reshape(-1, LANES)))
        all_keys.append(lay.all_parts(lay.unpack_keys(blocks[:, span:]).reshape(-1, FEAT)))
    mains[-1] = tie(mains[-1], *out_sides, *down_sides)
    out_w.far(mains[-1])
    down_w.far(mains[-1])
    for j in heads:
        attended, sent = attend(mains[j], all_keys[j], my_seg)
        kept.append(attended)
        blocks = lay.own_part(sent.reshape(-1, span, LANES))
        if j > 0:
            blocks = tie(blocks, low[-1])
        low.append(lay.exchange(blocks))
    att_low, projected = out_of_pieces(lay, [lay.by_place(blocks) for blocks in low], out_w)

    residual = x + projected
    scale_two = inverse_rms(residual)
    normed_two = (residual * scale_two * gain_two).astype(bf16)
    out_sum = Scatter(None, att_low, True)
    grad_hidden = spread(tie(cot_low, att_low), down_w)
    normed_two = tie(normed_two, out_sum.other_side(), grad_hidden)
    slope, silu, hidden = hidden_of(normed_two, gate_up_w)
    down_sum = Scatter(cot_left, hidden)
    ffn_out = collect(hidden, down_w)
    layer_output = (residual + ffn_out).astype(bf16).reshape(tokens.shape)

    down_sum.right = tie(down_sum.right, ffn_out)
    down_sends = down_sum.first()
    grads_gu, back_two = hidden_back(tie(grad_hidden, *down_sends), gate_up_w, slope, silu)
    two_left = Left(normed_two)
    gate_sum = Scatter(two_left, grads_gu)
    up_sum = Scatter(two_left, grads_gu, False, *gate_sum.other_side(), kind=1)
    gain_two_grad = jnp.sum(back_two * residual * scale_two, axis=0)
    grad_residual = cot_low.astype(f32) + norm_back(residual, scale_two, gain_two, back_two)
    grad_res_low = grad_residual.astype(bf16)

    sent = [rows.reshape(-1, span, LANES) for rows in into_pieces(lay, grad_res_low, out_w)]
    arrived = [lay.exchange(blocks) for blocks in sent]
    down_sends = down_sum.second(*sent)
    out_sum.left = Left(tie(grad_res_low, *sent))
    for terms in (gate_sum, up_sum, out_sum):
        terms.right = tie(terms.right, *down_sends)
    up_sum.right = tie(up_sum.right, *arrived[1:])
    made = gate_sum.products() + up_sum.products() + out_sum.products()
    down_sum = Along(down_sum.last(*made))
    gate_sum.go(*down_sum.sent)
    arrived[0] = tie(arrived[0], *made, *down_sum.sent)
    backs, grad_keys = [], []
    for j in heads:
        grad_rows = lay.all_parts(arrived[j].reshape(-1, LANES))
        if j == lay.heads - 1:
            if j > 0:
                grad_rows = tie(grad_rows, sent)
            up_sum.go(grad_rows, *gate_sum.pending())
            down_sum.go(grad_rows)
            grad_rows = tie(grad_rows, *gate_sum.pending(), *down_sum.sent)
        grad_main, grad_key = attend_back(mains[j], all_keys[j], kept[j], grad_rows, my_seg)
        if j == lay.heads - 1:
            grad_main = tie(grad_main, *up_sum.pending(), *down_sum.coming)
        blocks = grad_main.reshape(-1, span, LANES)
        ahead = jnp.pad(blocks[1:, :16], ((0, 1), (0, 0), (0, 0)))
        packed = lay.pack_keys(grad_key.reshape(-1, span, FEAT))
        sent = lay.own_part(jnp.concatenate([blocks, packed, ahead], axis=1))
        if j > 0:
            sent = tie(sent, backs[-1])
        blocks = lay.exchange(sent)
        grad_keys.append(lay.unpack_keys(blocks[:, span : span + lay.key_rows]))
        backs.append(lay.by_place(blocks))
    gate_sum.second(sent)
    up_sum.second(sent)
    backs[-1] = tie(backs[-1], *gate_sum.pending(), *up_sum.pending())
    gate_up_sum = Along(jnp.stack([gate_sum.last(backs[-1]), up_sum.last(backs[-1])], axis=1))
    backs[-1] = tie(backs[-1], *gate_up_sum.sent)
    out_sum.go(backs[-1])

    grad_keys = jnp.stack([lay.by_place(rows) for rows in grad_keys])
    grad_keys = jnp.transpose(grad_keys, (3, 1, 4, 2, 0, 5)).reshape(head, count, -1)
    grad_first, tap_grads = project_back(
        lay, backs, grad_keys, v_low, filter_pre, side, same, taps
    )
    tap_grads = jnp.swapaxes(tap_grads, 0, 1).reshape(3, D)
    grad_first = tie(grad_first, *out_sum.pending())
    first_sum = Scatter(Left(tie(normed, grad_first)), grad_first[:, None])
    out_sends = out_sum.second(*first_sum.given())
    first_sum.right = tie(first_sum.right, *out_sends)
    first_sum.products(True)
    first_sum.go()
    back_one = out_of(tie(grad_first, *first_sum.made), first_w)
    gate_up_sum.go(back_one)
    gain_one_grad = jnp.sum(back_one * x * scale_one, axis=0)
    first_sends = first_sum.second(back_one)
    out_sum = Along(out_sum.last(*first_sends))
    first_sum = Along(first_sum.last(*out_sum.sent))
    gate_up_grad = gate_up_sum.finish(*first_sum.sent)
    down_grad = down_sum.finish(*first_sum.sent)
    out_sum.go(*first_sum.sent)
    first_sum.go(*out_sum.sent)
    out_grad = out_sum.finish(*first_sum.sent)
    first_grad = first_sum.finish()
    grad_x = (grad_residual + norm_back(x, scale_one, gain_one, back_one)).astype(bf16)
    tokens_grad = grad_x.reshape(tokens.shape)

    small = jnp.concatenate([jnp.stack([gain_one_grad, gain_two_grad]), tap_grads], axis=0)
    small = tie(small, *first_sum.sent)
    small = jnp.swapaxes(small.reshape(5, head * seq, -1), 0, 1)
    small = lax.all_to_all(small, ("head", "seq"), 0, 0, tiled=True)
    small = jnp.sum(small, axis=0)

    q_end, k_end, v_end = qk_width, 2 * qk_width, 2 * qk_width + v_width
    return (
        layer_output,
        tokens_grad,
        first_grad[:, :q_end],
        first_grad[:, q_end:k_end],
        first_grad[:, k_end:v_end],
        first_grad[:, v_end:],
        out_grad[:, :v_width].astype(f32).T,
        gate_up_grad[0][:, :ff_width].astype(f32),
        gate_up_grad[1][:, :ff_width].astype(f32),
        down_grad[:, :ff_width].astype(f32),
        small[0],
        small[1],
        small[2:],
    )


def solution(mesh):
    rows = P(None, BOTH, None)
    return jax.shard_map(
        local,
        mesh=mesh,
        in_specs=(
            rows,
            rows,
            P(None, "seq"),
            P("seq", "head"),
            P("seq", "head"),
            P("seq", "head"),
            P("seq", "head"),
            P("head", "seq"),
            P("seq", "head"),
            P("seq", "head"),
            P("seq", "head"),
            P("seq"),
            P("seq"),
            P(None, ("head", "seq")),
        ),
        out_specs=(
            rows,
            rows,
            P("seq", "head"),
            P("seq", "head"),
            P("seq", "head"),
            P("seq", "head"),
            P("head", "seq"),
            P("seq", "head"),
            P("seq", "head"),
            P("seq", "head"),
            P(("head", "seq")),
            P(("head", "seq")),
            P(None, ("head", "seq")),
        ),
        check_vma=False,
    )
```

```python
import functools

import jax
import jax.numpy as jnp
from jax import lax
from jax.experimental import pallas as pl
from jax.experimental.pallas import tpu as pltpu
from jax.sharding import PartitionSpec as P

D = 1792
HEADS = 16
FEAT = 16
WIDTH = D // HEADS
LANES = 128
VMEM = 60 * 2**20
EPSILON = 1e-06
BOTH = ("seq", "head")
CORE, SIDE_X, SIDE_Y = 1, 2, 4

f32 = jnp.float32
bf16 = jnp.bfloat16
MESH = pl.DeviceIdType.MESH


def grouped(value, multiple):
    return -(-value // multiple) * multiple


def cost(flops):
    return pl.CostEstimate(flops=int(flops), bytes_accessed=1, transcendentals=0)


def dot(left, right):
    return jnp.dot(left, right, preferred_element_type=f32)


def dot_rt(left, right):
    return lax.dot_general(left, right, (((1,), (1,)), ((), ())), preferred_element_type=f32)


def dot_lt(left, right):
    return lax.dot_general(left, right, (((0,), (0,)), ((), ())), preferred_element_type=f32)


def swap(block, bit, axis="seq"):
    devices = range(lax.axis_size(axis))
    return lax.ppermute(block, axis, [(i, i ^ bit) for i in devices])


def paired():
    return lax.axis_size("seq") == 8 and lax.axis_size("head") == 4


def tie(value, *others):
    return lax.optimization_barrier((value, others))[0]


def gather(shard):
    whole = lax.all_gather(shard, BOTH)
    return whole.reshape((lax.axis_size("seq"), lax.axis_size("head")) + shard.shape)


def by_place(blocks):
    if not paired():
        return blocks
    here = lax.axis_index("head")
    if blocks.ndim == 1:
        return blocks ^ here
    pick = lambda r: lax.dynamic_index_in_dim(blocks, here ^ r, 0, keepdims=False)
    return jnp.stack([pick(r) for r in range(4)])


def flipped(here, bit):
    return here + bit - 2 * bit * ((here // bit) % 2)


def gather_kernel(shard, edge, *refs):
    count = (len(refs) - 9) // 2
    others, (whole, edges), rest = refs[:count], refs[count : count + 2], refs[count + 2 :]
    lined, (send, recv, local, line_send, line_recv, edge_send, edge_recv) = (
        rest[:count],
        rest[count:],
    )
    place, line = lax.axis_index("seq"), lax.axis_index("head")
    seq, head = lax.axis_size("seq"), lax.axis_size("head")
    lines = [line, flipped(line, 1), flipped(line, 2), 3 - line]
    by_x, by_y, by_core = (flipped(place, bit) for bit in (SIDE_X, SIDE_Y, CORE))
    corner = flipped(by_x, SIDE_Y)
    to = lambda at, z: {"seq": at, "head": z}
    linear = place * head + line
    after, before = (linear + 1) % (seq * head), (linear + seq * head - 1) % (seq * head)
    sides = [to(at // head, at % head) for at in (after, before)]
    partners = [to(place, z) for z in lines[1:]] + [to(at, line) for at in (by_x, by_y, by_core)]
    partners += sides

    barrier = pltpu.get_barrier_semaphore()
    for partner in partners:
        pl.semaphore_signal(barrier, inc=1, device_id=partner, device_id_type=MESH)
    pl.semaphore_wait(barrier, len(partners))

    def remote(source, target, send_sem, recv_sem, partner):
        return pltpu.make_async_remote_copy(
            src_ref=source,
            dst_ref=target,
            send_sem=send_sem,
            recv_sem=recv_sem,
            device_id=partner,
            device_id_type=MESH,
        )

    copies = [pltpu.make_async_copy(shard, whole.at[place, line, 0], local.at[0])]
    copies += [
        pltpu.make_async_copy(other, target.at[0], local.at[1 + i])
        for i, (other, target) in enumerate(zip(others, lined))
    ]
    started = {}

    def start(row, r, source, at, z, partner):
        started[row, r] = remote(
            source, whole.at[at, z, 0], send.at[row, r], recv.at[row, r], partner
        )
        started[row, r].start()

    for r in (2, 1):
        start(0, r, shard, place, line, to(place, lines[r]))
    copies += [
        remote(edge, edges.at[i], edge_send.at[i], edge_recv.at[i], partner)
        for i, partner in enumerate(sides)
    ]
    for each in copies:
        each.start()
    for r in (0, 2, 1, 3):
        if r > 0:
            started[0, r].wait_recv()
        source = shard if r == 0 else whole.at[place, lines[r], 0]
        if r == 2:
            start(0, 3, source, place, lines[r], to(place, lines[1]))
        start(1, r, source, place, lines[r], to(by_x, line))
        start(2, r, source, place, lines[r], to(by_y, line))
        start(3, r, source, place, lines[r], to(by_core, line))
    more = {
        (i, r): remote(
            target.at[2] if r == 3 else other,
            target.at[r],
            line_send.at[i, r],
            line_recv.at[i, r],
            to(place, lines[2 if r == 2 else 1]),
        )
        for i, (other, target) in enumerate(zip(others, lined))
        for r in (2, 1, 3)
    }
    for (i, r), each in more.items():
        if r < 3:
            each.start()
    for r in (0, 2, 1, 3):
        z = lines[r]
        started[1, r].wait_recv()
        if r < 2:
            start(4, r, whole.at[by_x, z, 0], by_x, z, to(by_y, line))
        start(5, r, whole.at[by_x, z, 0], by_x, z, to(by_core, line))
        started[2, r].wait_recv()
        if r >= 2:
            start(4, r, whole.at[by_y, z, 0], by_y, z, to(by_x, line))
        start(6, r, whole.at[by_y, z, 0], by_y, z, to(by_core, line))
    for i in range(count):
        more[i, 2].wait_recv()
        more[i, 3].start()
    for r in (0, 2, 1, 3):
        z = lines[r]
        started[4, r].wait_recv()
        start(7, r, whole.at[corner, z, 0], corner, z, to(by_core, line))
    for (row, r), each in started.items():
        each.wait_send()
        if row in (3, 5, 6, 7):
            each.wait_recv()
    for (i, r), each in more.items():
        each.wait_send()
        if r != 2:
            each.wait_recv()
    for each in copies:
        each.wait()


def gather_first(shard, edge, others):
    seq, head = lax.axis_size("seq"), lax.axis_size("head")
    if not paired():
        return gather(shard[None]), jnp.stack([shift(edge, 1), shift(edge, -1)]), [None] * len(others)
    anywhere = pl.BlockSpec(memory_space=pl.ANY)
    count = len(others)
    dma = pltpu.SemaphoreType.DMA
    whole, edges, *lined = pl.pallas_call(
        gather_kernel,
        in_specs=[anywhere] * (2 + count),
        out_specs=[anywhere] * (2 + count),
        out_shape=[
            jax.ShapeDtypeStruct((seq, head, 1) + shard.shape, bf16),
            jax.ShapeDtypeStruct((2,) + edge.shape, bf16),
        ]
        + [jax.ShapeDtypeStruct((head,) + other.shape, bf16) for other in others],
        scratch_shapes=[
            dma((8, 4)),
            dma((8, 4)),
            dma((1 + count,)),
            dma((count, 4)),
            dma((count, 4)),
            dma((2,)),
            dma((2,)),
        ],
        compiler_params=pltpu.CompilerParams(collective_id=0, has_side_effects=True),
        cost_estimate=cost(100e9),
    )(shard, edge, *others)
    return whole, edges, lined


class Pieces:
    def __init__(self, shard, own=None):
        self.shard = shard
        self.columns = shard.shape[1]
        self.order = by_place(jnp.arange(lax.axis_size("head"), dtype=jnp.int32))
        if paired():
            if own is None:
                two = swap(shard, 2, "head")
                one = swap(jnp.stack([shard, two]), 1, "head")
                own = jnp.stack([shard, one[0], two, one[1]])
            self.own = own
        else:
            own = lax.all_gather(shard, "head")
            self.own = lax.all_gather(own, "seq", axis=1, tiled=True)
            self.pieces, self.offsets = [(self.own, 0)], jnp.zeros((1,), jnp.int32)

    def sides(self, *after):
        if paired():
            own = tie(self.own, *after) if after else self.own
            self.by_x, self.by_y = swap(own, SIDE_X), swap(own, SIDE_Y)
            return self.by_x, self.by_y
        return ()

    def far(self, *after):
        if not paired():
            return
        by_x, by_y = self.by_x[:2], self.by_y[2:]
        if after:
            by_x, by_y = tie(by_x, *after), tie(by_y, *after)
        far_a, far_b = swap(by_x, SIDE_Y), swap(by_y, SIDE_X)
        mine = [(self.own, 0), (self.by_x, 0), (self.by_y, 0), (far_a, 0), (far_b, 2)]
        self.pieces = mine + [(swap(piece, CORE), start) for piece, start in mine]
        sides = (0, SIDE_X, SIDE_Y, SIDE_X | SIDE_Y, SIDE_X | SIDE_Y)
        sides = sides + tuple(side | CORE for side in sides)
        rows = self.shard.shape[0]
        self.offsets = (lax.axis_index("seq") ^ jnp.array(sides, jnp.int32)) * rows

    @property
    def places(self):
        return self.own.shape[0]

    def specs(self):
        def spec(piece, start):
            last = piece.shape[0] - 1
            return pl.BlockSpec(
                (1,) + piece.shape[1:], lambda z, o, p: (jnp.clip(z - start, 0, last), 0, 0)
            )

        return [spec(piece, start) for piece, start in self.pieces]

    def fill(self, offsets, refs, weight):
        z = pl.program_id(0)
        for i, (ref, (piece, start)) in enumerate(zip(refs, self.pieces)):
            count, rows, _ = piece.shape

            def put():
                at = pl.multiple_of(offsets[i], 16)
                weight[pl.ds(at, rows)] = ref[0]

            if count == self.places:
                put()
            else:
                pl.when((z >= start) & (z < start + count))(put)


def grad_kernel(first, plane, left0, left1, right0, right1, send, keep, rows0, rows1):
    _, width, tokens = left0.shape

    @pl.when(pl.program_id(0) == 0)
    def _():
        for i in range(4):
            rows0[i * width : (i + 1) * width] = left0[plane[0] ^ i]
            rows1[i * width : (i + 1) * width] = left1[plane[0] ^ i]

    total = dot(rows0[...], right0[0, 0]) + dot(rows1[...], right1[0, 0])
    total = total.astype(bf16)
    far = first // 2
    near = 3 ^ far
    for i, at in enumerate((0, near)):
        keep[i, 0] = total[at * width : (at + 1) * width]
        at ^= far
        send[i, 0] = total[at * width : (at + 1) * width]


def weight_grads(plane, left0, left1, right0, right1, kind, start, first, light):
    count, _, tokens, columns = right0.shape
    count //= 2
    width = left0.shape[1]
    left = pl.BlockSpec(left0.shape, lambda z, p: (0, 0, 0))
    right = pl.BlockSpec((1, 1, tokens, columns), lambda z, p: (z + start, kind, 0, 0))
    out = pl.BlockSpec((2, 1, width, columns), lambda z, p: (0, z, 0, 0))
    shape = jax.ShapeDtypeStruct((2, count, width, columns), bf16)
    return pl.pallas_call(
        functools.partial(grad_kernel, first),
        grid_spec=pltpu.PrefetchScalarGridSpec(
            num_scalar_prefetch=1,
            grid=(count,),
            in_specs=[left, left, right, right],
            out_specs=[out, out],
            scratch_shapes=[pltpu.VMEM((4 * width, tokens), bf16)] * 2,
        ),
        out_shape=[shape, shape],
        compiler_params=pltpu.CompilerParams(vmem_limit_bytes=VMEM),
        cost_estimate=cost(1 if light else count * 20 * width * tokens * columns),
    )(plane, left0, left1, right0, right1)


class Left:
    def __init__(self, rows):
        self.rows = rows
        if paired():
            blocks = rows.T.reshape(4, 2, D // 8, -1)
            core = lax.axis_index("seq") % 2
            pick = lambda c: lax.dynamic_index_in_dim(blocks, c, 1, keepdims=False)
            self.near, self.far = pick(core), swap(pick(1 - core), CORE)

    def pending(self):
        return (self.far,) if paired() else ()


class Scatter:
    def __init__(self, left, right, relative=False, other=None, kind=0):
        self.right = right
        self.left = left
        self.relative = relative
        self.kind = kind
        if paired():
            self.other = swap(right, CORE) if other is None else other

    def given(self):
        return (self.other,) + self.left.pending() if paired() else ()

    def other_side(self):
        return (self.other,) if paired() else (None,)

    def first(self):
        made = self.products()
        self.go()
        return made

    def products(self, light=False):
        self.made = []
        if not paired():
            return ()
        half = self.right.shape[0] // 2
        plane = (lax.axis_index("seq") // 2).reshape(1)
        self.kept = []
        for start, side in ((0, SIDE_X), (half, SIDE_Y)):
            send, keep = weight_grads(
                plane,
                self.left.near,
                self.left.far,
                self.right,
                self.other,
                self.kind,
                start,
                side,
                light,
            )
            self.made.append(send)
            self.kept.append(keep)
        return tuple(self.made)

    def go(self, *after):
        if paired():
            made = [tie(send, *after) for send in self.made] if after else self.made
            self.arrived = [swap(send, side) for send, side in zip(made, (SIDE_X, SIDE_Y))]
            self.coming = self.arrived

    def second(self, *after):
        if not paired():
            return ()
        self.sums, made = [], []
        for keep, arrived, side in zip(self.kept, self.arrived, (SIDE_Y, SIDE_X)):
            if after:
                arrived = tie(arrived, *after)
            go = (keep[1].astype(f32) + arrived[1].astype(f32)).astype(bf16)
            stay = keep[0].astype(f32) + arrived[0].astype(f32)
            made.append(go)
            self.sums.append((stay, swap(go, side)))
        self.coming = [arrived for _, arrived in self.sums]
        return tuple(made)

    def pending(self):
        return tuple(self.coming) if paired() else ()

    def last(self, *after):
        if not paired():
            whole = jnp.einsum(
                "td,htc->hdc", self.left.rows, self.right[:, self.kind], preferred_element_type=f32
            ).astype(bf16)
            seq = lax.axis_size("seq")
            whole = whole.reshape(whole.shape[:1] + (seq, D // seq, -1))
            return lax.psum_scatter(whole, "seq", scatter_dimension=1)
        sums = []
        for stay, arrived in self.sums:
            if after:
                arrived = tie(arrived, *after)
            sums.append((stay + arrived.astype(f32)).astype(bf16))
        sums = jnp.concatenate(sums, axis=0)
        if self.relative:
            sums = by_place(sums)
        return sums


class Along:
    def __init__(self, blocks):
        if not paired():
            self.total = lax.psum_scatter(blocks, "head", scatter_dimension=0).astype(f32)
            self.coming, self.sent = (), ()
            return
        here = lax.axis_index("head")
        pick = lambda r: lax.dynamic_index_in_dim(blocks, here ^ r, 0, keepdims=False)
        self.kept = (pick(0), pick(2))
        sent = jnp.stack([pick(1), pick(3)])
        self.sent = (sent,)
        self.coming = (swap(sent, 1, "head"),)

    def go(self, *after):
        if not paired():
            return
        (arrived,) = self.coming
        if after:
            arrived = tie(arrived, *after)
        self.stay = self.kept[0].astype(f32) + arrived[0].astype(f32)
        sent = (self.kept[1].astype(f32) + arrived[1].astype(f32)).astype(bf16)
        self.sent = (sent,)
        self.coming = (swap(sent, 2, "head"),)

    def finish(self, *after):
        if not paired():
            return self.total
        (arrived,) = self.coming
        if after:
            arrived = tie(arrived, *after)
        return self.stay + arrived.astype(f32)


def whole_rows(ref, kind=0):
    block = ref[:, 0, kind]
    return block.reshape(D, block.shape[-1])


def weight_spec(weight, kinds=1, at=0):
    seq, _, _, _, columns = weight.shape
    return pl.BlockSpec((seq, 1, kinds, D // seq, columns), lambda z: (0, z, at, 0, 0))


def into_kernel(x_ref, w_ref, out_ref):
    out_ref[0] = dot(x_ref[...], whole_rows(w_ref)).astype(out_ref.dtype)


def into(x, weight, kind):
    count, columns = weight.shape[1], weight.shape[-1]
    tokens = x.shape[0]
    return pl.pallas_call(
        into_kernel,
        grid=(count,),
        in_specs=[
            pl.BlockSpec(x.shape, lambda z: (0, 0)),
            weight_spec(weight),
        ],
        out_specs=pl.BlockSpec((1, tokens, columns), lambda z: (z, 0, 0)),
        out_shape=jax.ShapeDtypeStruct((count, tokens, columns), kind),
        compiler_params=pltpu.CompilerParams(vmem_limit_bytes=VMEM),
        cost_estimate=cost(count * 3 * D * tokens * columns),
    )(x, weight)


def out_of_kernel(y_ref, w_ref, out_ref):
    @pl.when(pl.program_id(0) == 0)
    def _():
        out_ref[...] = jnp.zeros_like(out_ref)

    out_ref[...] += dot_rt(y_ref[0], whole_rows(w_ref))


def out_of(y, weight):
    count, tokens, columns = y.shape
    return pl.pallas_call(
        out_of_kernel,
        grid=(count,),
        in_specs=[
            pl.BlockSpec((1, tokens, columns), lambda z: (z, 0, 0)),
            weight_spec(weight),
        ],
        out_specs=pl.BlockSpec((tokens, D), lambda z: (0, 0)),
        out_shape=jax.ShapeDtypeStruct((tokens, D), f32),
        compiler_params=pltpu.CompilerParams(vmem_limit_bytes=VMEM),
        cost_estimate=cost(1),
    )(y, weight)


def into_pieces_kernel(lay, weights, offsets, places, x_ref, *refs):
    count = len(weights.pieces)
    refs, outs, weight = refs[:count], refs[count:-1], refs[-1]
    weights.fill(offsets, refs, weight)
    rows = dot(x_ref[...], weight[...])
    for b in range(lay.batch):
        here = slice(b * lay.tokens, (b + 1) * lay.tokens)
        for i in range(lay.splits):
            for j, out in enumerate(outs):
                out[b, i, 0, :, :WIDTH] = rows[here, lay.columns(i, j)[0]].astype(bf16)
                out[b, i, 0, :, WIDTH:] = jnp.zeros_like(out[b, i, 0, :, WIDTH:])


def into_pieces(lay, x, weights):
    count, columns = weights.places, weights.columns
    block = (lay.batch, lay.splits, 1, lay.tokens, LANES)
    return pl.pallas_call(
        functools.partial(into_pieces_kernel, lay, weights),
        grid_spec=pltpu.PrefetchScalarGridSpec(
            num_scalar_prefetch=2,
            grid=(count,),
            in_specs=[pl.BlockSpec(x.shape, lambda z, o, p: (0, 0))] + weights.specs(),
            out_specs=[pl.BlockSpec(block, lambda z, o, p: (0, 0, p[z], 0, 0))] * lay.heads,
            scratch_shapes=[pltpu.VMEM((D, columns), bf16)],
        ),
        out_shape=[jax.ShapeDtypeStruct(block[:2] + (count,) + block[3:], bf16)] * lay.heads,
        compiler_params=pltpu.CompilerParams(vmem_limit_bytes=VMEM),
        cost_estimate=cost(count * 3 * D * x.shape[0] * columns),
    )(weights.offsets, weights.order, x, *[piece for piece, _ in weights.pieces])


def out_of_pieces_kernel(lay, weights, offsets, places, *refs):
    ys, refs, (rows_ref, out_ref, weight) = refs[: lay.heads], refs[lay.heads : -3], refs[-3:]
    weights.fill(offsets, refs, weight)

    @pl.when(pl.program_id(0) == 0)
    def _():
        out_ref[...] = jnp.zeros_like(out_ref)

    end = lay.splits * lay.heads * WIDTH
    rows_ref[0, 0, :, end:] = jnp.zeros_like(rows_ref[0, 0, :, end:])
    for b in range(lay.batch):
        here = slice(b * lay.tokens, (b + 1) * lay.tokens)
        for i in range(lay.splits):
            for j, y_ref in enumerate(ys):
                rows_ref[0, 0, here, lay.columns(i, j)[0]] = y_ref[b, i, 0, :, :WIDTH]
    out_ref[...] += dot_rt(rows_ref[0, 0], weight[...])


def out_of_pieces(lay, ys, weights):
    count, columns = weights.places, weights.columns
    tokens = lay.batch * lay.tokens
    block = (lay.batch, lay.splits, 1, lay.tokens, LANES)
    return pl.pallas_call(
        functools.partial(out_of_pieces_kernel, lay, weights),
        grid_spec=pltpu.PrefetchScalarGridSpec(
            num_scalar_prefetch=2,
            grid=(count,),
            in_specs=[pl.BlockSpec(block, lambda z, o, p: (0, 0, p[z], 0, 0))] * lay.heads
            + weights.specs(),
            out_specs=[
                pl.BlockSpec((1, 1, tokens, columns), lambda z, o, p: (z, 0, 0, 0)),
                pl.BlockSpec((tokens, D), lambda z, o, p: (0, 0)),
            ],
            scratch_shapes=[pltpu.VMEM((D, columns), bf16)],
        ),
        out_shape=[
            jax.ShapeDtypeStruct((count, 1, tokens, columns), bf16),
            jax.ShapeDtypeStruct((tokens, D), f32),
        ],
        compiler_params=pltpu.CompilerParams(vmem_limit_bytes=VMEM),
        cost_estimate=cost(count * 3 * D * tokens * columns),
    )(weights.offsets, weights.order, *ys, *[piece for piece, _ in weights.pieces])


def spread_kernel(weights, offsets, places, x_ref, *refs):
    refs, (out_ref, weight) = refs[:-2], refs[-2:]
    weights.fill(offsets, refs, weight)
    out_ref[0] = dot(x_ref[...], weight[...])


def spread(x, weights):
    count, columns = weights.places, weights.columns
    tokens = x.shape[0]
    return pl.pallas_call(
        functools.partial(spread_kernel, weights),
        grid_spec=pltpu.PrefetchScalarGridSpec(
            num_scalar_prefetch=2,
            grid=(count,),
            in_specs=[pl.BlockSpec(x.shape, lambda z, o, p: (0, 0))] + weights.specs(),
            out_specs=pl.BlockSpec((1, tokens, columns), lambda z, o, p: (p[z], 0, 0)),
            scratch_shapes=[pltpu.VMEM((D, columns), bf16)],
        ),
        out_shape=jax.ShapeDtypeStruct((count, tokens, columns), f32),
        compiler_params=pltpu.CompilerParams(vmem_limit_bytes=VMEM),
        cost_estimate=cost(count * 3 * D * tokens * columns),
    )(weights.offsets, weights.order, x, *[piece for piece, _ in weights.pieces])


def collect_kernel(weights, offsets, places, y_ref, *refs):
    refs, (out_ref, weight) = refs[:-2], refs[-2:]
    weights.fill(offsets, refs, weight)

    @pl.when(pl.program_id(0) == 0)
    def _():
        out_ref[...] = jnp.zeros_like(out_ref)

    out_ref[...] += dot_rt(y_ref[0, 0], weight[...])


def collect(y, weights):
    count, _, tokens, columns = y.shape
    return pl.pallas_call(
        functools.partial(collect_kernel, weights),
        grid_spec=pltpu.PrefetchScalarGridSpec(
            num_scalar_prefetch=2,
            grid=(count,),
            in_specs=[pl.BlockSpec((1,) + y.shape[1:], lambda z, o, p: (p[z], 0, 0, 0))]
            + weights.specs(),
            out_specs=pl.BlockSpec((tokens, D), lambda z, o, p: (0, 0)),
            scratch_shapes=[pltpu.VMEM((D, columns), bf16)],
        ),
        out_shape=jax.ShapeDtypeStruct((tokens, D), f32),
        compiler_params=pltpu.CompilerParams(vmem_limit_bytes=VMEM),
        cost_estimate=cost(count * 3 * D * tokens * columns),
    )(weights.offsets, weights.order, y, *[piece for piece, _ in weights.pieces])


def hidden_kernel(x_ref, gu_ref, slope_ref, silu_ref, hidden_ref):
    gate = dot(x_ref[...], whole_rows(gu_ref, 0))
    sig = jax.nn.sigmoid(gate)
    silu = gate * sig
    up = dot(x_ref[...], whole_rows(gu_ref, 1))
    slope_ref[0] = (up * sig * (1.0 + gate * (1.0 - sig))).astype(bf16)
    silu_ref[0] = silu.astype(bf16)
    columns = gate.shape[1]
    hidden_ref[0, 0, :, :columns] = (silu * up).astype(bf16)
    hidden_ref[0, 0, :, columns:] = jnp.zeros_like(hidden_ref[0, 0, :, columns:])


def hidden_of(x, weight):
    count, columns = weight.shape[1], weight.shape[-1]
    padded = grouped(columns, LANES)
    tokens = x.shape[0]
    act = pl.BlockSpec((1, tokens, columns), lambda z: (z, 0, 0))
    kept = jax.ShapeDtypeStruct((count, tokens, columns), bf16)
    return pl.pallas_call(
        hidden_kernel,
        grid=(count,),
        in_specs=[pl.BlockSpec(x.shape, lambda z: (0, 0)), weight_spec(weight, kinds=2)],
        out_specs=[act, act, pl.BlockSpec((1, 1, tokens, padded), lambda z: (z, 0, 0, 0))],
        out_shape=[kept, kept, jax.ShapeDtypeStruct((count, 1, tokens, padded), bf16)],
        compiler_params=pltpu.CompilerParams(vmem_limit_bytes=VMEM),
        cost_estimate=cost(count * 6 * D * tokens * columns),
    )(x, weight)


def hidden_back_kernel(grad_ref, gu_ref, slope_ref, silu_ref, grads_ref, out_ref):
    @pl.when(pl.program_id(0) == 0)
    def _():
        out_ref[...] = jnp.zeros_like(out_ref)

    columns = slope_ref.shape[-1]
    grad_hidden = grad_ref[0, :, :columns]
    grad_gate = (grad_hidden * slope_ref[0].astype(f32)).astype(bf16)
    grad_up = (grad_hidden * silu_ref[0].astype(f32)).astype(bf16)
    grads_ref[0, 0, :, :columns] = grad_gate
    grads_ref[0, 1, :, :columns] = grad_up
    grads_ref[0, :, :, columns:] = jnp.zeros_like(grads_ref[0, :, :, columns:])
    out_ref[...] += dot_rt(grad_gate, whole_rows(gu_ref, 0)) + dot_rt(
        grad_up, whole_rows(gu_ref, 1)
    )


def hidden_back(grad, weight, slope, silu):
    count, columns = weight.shape[1], weight.shape[-1]
    padded = grouped(columns, LANES)
    tokens = grad.shape[1]
    act = pl.BlockSpec((1, tokens, columns), lambda z: (z, 0, 0))
    return pl.pallas_call(
        hidden_back_kernel,
        grid=(count,),
        in_specs=[
            pl.BlockSpec((1, tokens, padded), lambda z: (z, 0, 0)),
            weight_spec(weight, kinds=2),
            act,
            act,
        ],
        out_specs=[
            pl.BlockSpec((1, 2, tokens, padded), lambda z: (z, 0, 0, 0)),
            pl.BlockSpec((tokens, D), lambda z: (0, 0)),
        ],
        out_shape=[
            jax.ShapeDtypeStruct((count, 2, tokens, padded), bf16),
            jax.ShapeDtypeStruct((tokens, D), f32),
        ],
        compiler_params=pltpu.CompilerParams(vmem_limit_bytes=VMEM),
        cost_estimate=cost(1),
    )(grad, weight, slope, silu)


def inverse_rms(rows):
    return lax.rsqrt(jnp.mean(rows * rows, axis=-1, keepdims=True) + EPSILON)


def norm_back(rows, scale, gain, grad):
    unit = rows * scale
    scaled = gain * grad
    return scale * (scaled - unit * jnp.mean(scaled * unit, axis=-1, keepdims=True))


class Layout:
    def __init__(self, batch, tokens):
        seq, head = lax.axis_size("seq"), lax.axis_size("head")
        self.batch, self.tokens, self.head = batch, tokens, head
        self.splits = min(seq // batch, HEADS // head)
        self.heads = HEADS // (head * self.splits)
        self.parts = seq // (batch * self.splits)
        self.inner = seq // self.parts
        self.sets = LANES // FEAT
        self.key_rows = grouped(tokens // self.sets, 16)
        self.length = tokens * seq * head
        count = self.inner * head
        self.groups = None
        if self.parts > 1:
            self.groups = [list(range(k * count, (k + 1) * count)) for k in range(self.parts)]
            self.mates = [[k * count + i for k in range(self.parts)] for i in range(count)]

    def sequence(self):
        return lax.rem(lax.axis_index("seq"), self.inner) // self.splits

    def pack_keys(self, keys):
        lead, each = keys.shape[:-2], self.tokens // self.sets
        keys = keys.reshape(lead + (self.sets, each, FEAT))
        keys = jnp.swapaxes(keys, -3, -2).reshape(lead + (each, LANES))
        return jnp.pad(keys, [(0, 0)] * len(lead) + [(0, self.key_rows - each), (0, 0)])

    def unpack_keys(self, rows):
        lead, each = rows.shape[:-2], self.tokens // self.sets
        rows = rows[..., :each, :].reshape(lead + (each, self.sets, FEAT))
        return jnp.swapaxes(rows, -3, -2).reshape(lead + (self.tokens, FEAT))

    def columns(self, i, j):
        at = i * self.heads + j
        return slice(at * WIDTH, (at + 1) * WIDTH), slice(at * FEAT, (at + 1) * FEAT)

    def by_place(self, blocks):
        return blocks.reshape((self.batch, self.splits, self.head) + blocks.shape[1:])

    def exchange(self, blocks):
        return lax.all_to_all(blocks, BOTH, 0, 0, tiled=True, axis_index_groups=self.groups)

    def all_parts(self, rows):
        if self.parts > 1:
            rows = lax.all_gather(rows, BOTH, axis=0, tiled=True, axis_index_groups=self.mates)
        return rows

    def own_part(self, blocks):
        if self.parts > 1:
            count = blocks.shape[0] // self.parts
            part = lax.axis_index("seq") // self.inner
            blocks = lax.dynamic_slice_in_dim(blocks, part * count, count, 0)
        return blocks


def fill_values(chunk, main, values, queries):
    lane = lax.broadcasted_iota(jnp.int32, (chunk, LANES), 1)
    ones = jnp.where(lane < WIDTH + 2, 1.0, 0.0)

    def turn(i, _):
        here = pl.ds(pl.multiple_of(i * chunk, chunk), chunk)
        rows = main[here]
        values[here] = jnp.where(lane < WIDTH, rows.astype(f32), ones).astype(bf16)
        queries[here] = rows[:, WIDTH:]
        return 0

    lax.fori_loop(0, main.shape[0] // chunk, turn, 0)


def attend_kernel(chunk, main, keys, seg_col, seg_row, out_ref, low_ref, values, queries):
    at = pl.program_id(0)

    @pl.when(at == 0)
    def _():
        fill_values(chunk, main, values, queries)

    mine = seg_col[...]
    query = queries[pl.ds(pl.multiple_of(at * chunk, chunk), chunk)]

    def weighted(j, causal):
        here = pl.ds(pl.multiple_of(j * chunk, chunk), chunk)
        scores = dot_rt(query, keys[here])
        allowed = mine == seg_row[j]
        if causal:
            later = lax.broadcasted_iota(jnp.int32, scores.shape, 0)
            allowed &= later >= lax.broadcasted_iota(jnp.int32, scores.shape, 1)
        weights = jnp.where(allowed, 1.0 + scores * (1.0 + 0.5 * scores), 0.0).astype(bf16)
        return dot(weights, values[here])

    total = lax.fori_loop(
        0, at, lambda j, acc: acc + weighted(j, False), jnp.zeros((chunk, LANES), f32)
    )
    total = total + weighted(at, True)
    norm = total[:, WIDTH : WIDTH + 1]
    lane = lax.broadcasted_iota(jnp.int32, total.shape, 1)
    total = jnp.where(lane < WIDTH, total / norm, norm)
    out_ref[...] = total
    low_ref[...] = total.astype(bf16)


def attend(main, keys, seg):
    length = main.shape[0]
    chunk = min(512, length)
    steps = length // chunk
    part = pl.BlockSpec((chunk, LANES), lambda i: (i, 0))
    return pl.pallas_call(
        functools.partial(attend_kernel, chunk),
        grid=(steps,),
        in_specs=[
            pl.BlockSpec((length, LANES), lambda i: (0, 0)),
            pl.BlockSpec((length, FEAT), lambda i: (0, 0)),
            pl.BlockSpec((chunk, 1), lambda i: (i, 0)),
            pl.BlockSpec((steps, 1, chunk), lambda i: (0, 0, 0)),
        ],
        out_specs=[part, part],
        out_shape=[
            jax.ShapeDtypeStruct((length, LANES), f32),
            jax.ShapeDtypeStruct((length, LANES), bf16),
        ],
        scratch_shapes=[pltpu.VMEM((length, LANES), bf16), pltpu.VMEM((length, FEAT), bf16)],
        compiler_params=pltpu.CompilerParams(vmem_limit_bytes=VMEM),
        cost_estimate=cost(length * length * 12 * LANES),
    )(main, keys, seg.reshape(length, 1), seg.reshape(steps, 1, chunk))


def attend_back_kernel(
    chunk,
    main,
    keys,
    kept,
    grad,
    seg_col,
    seg_row,
    out_ref,
    gk_ref,
    values,
    queries,
    grad_n,
    grad_q,
):
    at = pl.program_id(0)
    steps = main.shape[0] // chunk

    @pl.when(at == 0)
    def _():
        fill_values(chunk, main, values, queries)
        grad_q[...] = jnp.zeros_like(grad_q)
        lane = lax.broadcasted_iota(jnp.int32, (chunk, LANES), 1)

        def turn(i, _):
            here = pl.ds(pl.multiple_of(i * chunk, chunk), chunk)
            rows = kept[here]
            low = jnp.where(lane < WIDTH, grad[here].astype(f32), 0.0)
            inverse = 1.0 / rows[:, WIDTH : WIDTH + 1]
            total = -jnp.sum(low * rows, axis=1, keepdims=True) * inverse
            high = total.astype(bf16).astype(f32)
            low = low * inverse
            low = jnp.where(lane == WIDTH, high, low)
            grad_n[here] = jnp.where(lane == WIDTH + 1, total - high, low).astype(bf16)
            return 0

        lax.fori_loop(0, steps, turn, 0)

    mine = seg_col[...]
    rows = pl.ds(pl.multiple_of(at * chunk, chunk), chunk)
    key, value = keys[rows], values[rows]
    key_t = key.astype(f32).T.astype(bf16)

    def turn(i, carry, causal):
        grad_k, grad_v = carry
        here = pl.ds(pl.multiple_of(i * chunk, chunk), chunk)
        query, grad_here = queries[here], grad_n[here]
        scores = dot_rt(key, query)
        allowed = mine == seg_row[i]
        if causal:
            key_at = lax.broadcasted_iota(jnp.int32, scores.shape, 0)
            allowed &= key_at <= lax.broadcasted_iota(jnp.int32, scores.shape, 1)
        weights = jnp.where(allowed, 1.0 + scores * (1.0 + 0.5 * scores), 0.0).astype(bf16)
        grad_s = dot_rt(value, grad_here) * (1.0 + scores)
        grad_s = jnp.where(allowed, grad_s, 0.0).astype(bf16)
        grad_q[:, here] += dot(key_t, grad_s)
        return grad_k + dot(grad_s, query), grad_v + dot(weights, grad_here)

    carry = (jnp.zeros((chunk, FEAT), f32), jnp.zeros((chunk, LANES), f32))
    carry = turn(at, carry, True)
    grad_k, grad_v = lax.fori_loop(at + 1, steps, lambda i, c: turn(i, c, False), carry)
    gk_ref[...] = (0.5 * grad_k).astype(bf16)
    out_ref[rows] = grad_v.astype(bf16)

    @pl.when(at == steps - 1)
    def _():
        def turn(i, _):
            here = pl.ds(pl.multiple_of(i * chunk, chunk), chunk)
            out_ref[here, WIDTH:] = (0.5 * grad_q[:, here].T).astype(bf16)
            return 0

        lax.fori_loop(0, steps, turn, 0)


def attend_back(main, keys, kept, grad, seg):
    length = main.shape[0]
    chunk = min(512, length)
    steps = length // chunk
    whole = pl.BlockSpec((length, LANES), lambda i: (0, 0))
    return pl.pallas_call(
        functools.partial(attend_back_kernel, chunk),
        grid=(steps,),
        in_specs=[
            whole,
            pl.BlockSpec((length, FEAT), lambda i: (0, 0)),
            whole,
            whole,
            pl.BlockSpec((chunk, 1), lambda i: (i, 0)),
            pl.BlockSpec((steps, 1, chunk), lambda i: (0, 0, 0)),
        ],
        out_specs=[whole, pl.BlockSpec((chunk, FEAT), lambda i: (i, 0))],
        out_shape=[
            jax.ShapeDtypeStruct((length, LANES), bf16),
            jax.ShapeDtypeStruct((length, FEAT), bf16),
        ],
        scratch_shapes=[
            pltpu.VMEM((length, LANES), bf16),
            pltpu.VMEM((length, FEAT), bf16),
            pltpu.VMEM((length, LANES), bf16),
            pltpu.VMEM((FEAT, length), f32),
        ],
        compiler_params=pltpu.CompilerParams(vmem_limit_bytes=VMEM),
        cost_estimate=cost(length * length * 24 * LANES),
    )(main, keys, kept, grad, seg.reshape(length, 1), seg.reshape(steps, 1, chunk))


def earlier(rows, before, distance):
    moved = pltpu.roll(rows, distance, 0)
    place = lax.broadcasted_iota(jnp.int32, rows.shape, 0)
    for i in range(distance):
        at = 2 - distance + i
        moved = jnp.where(place == i, before[at : at + 1], moved)
    return moved


def later(rows, after, distance):
    count = rows.shape[0]
    moved = pltpu.roll(rows, count - distance, 0)
    place = lax.broadcasted_iota(jnp.int32, rows.shape, 0)
    for i in range(distance):
        moved = jnp.where(place == count - distance + i, after[i : i + 1], moved)
    return moved


def short_filter(taps, same, values, before):
    one_back = earlier(values, before, 1) * same[:, 0:1]
    two_back = earlier(values, before, 2) * same[:, 1:2]
    return taps[0:1] * values + taps[1:2] * one_back + taps[2:3] * two_back, one_back, two_back


def project_kernel(lay, x_ref, side_ref, same_ref, taps_ref, w_ref, v_ref, f_ref, side_out, *outs):
    weight = whole_rows(w_ref)
    q_width, v_width = lay.splits * lay.heads * FEAT, v_ref.shape[-1]
    v_at, f_at = 2 * q_width, 2 * q_width + v_width
    full = dot(x_ref[...], weight)
    side = dot(side_ref[...], weight)
    low = full[:, v_at:f_at].astype(bf16)
    v_ref[0] = low
    f_ref[0] = full[:, f_at:]
    side_v = side[:, v_at:f_at].astype(bf16).astype(f32)
    side_out[0, 0] = side_v
    side_out[0, 1] = side[:, f_at:]
    taps = taps_ref[0]
    for b in range(lay.batch):
        rows = slice(b * lay.tokens, (b + 1) * lay.tokens)
        pre = full[rows, f_at:]
        filtered, _, _ = short_filter(
            taps, same_ref[rows], low[rows].astype(f32), side_v[2 * b : 2 * b + 2]
        )
        mixed = filtered * (pre * jax.nn.sigmoid(pre))
        query = 0.5 * full[rows, :q_width].astype(bf16).astype(f32)
        key = 0.5 * full[rows, q_width:v_at].astype(bf16).astype(f32)
        for i in range(lay.splits):
            for j in range(lay.heads):
                main, k_ref = outs[2 * j : 2 * j + 2]
                v_cols, q_cols = lay.columns(i, j)
                main[b, i, 0, :, :WIDTH] = mixed[:, v_cols].astype(bf16)
                main[b, i, 0, :, WIDTH:] = query[:, q_cols].astype(bf16)
                k_ref[b, i, 0] = key[:, q_cols].astype(bf16)


def project(lay, x, side, same, taps, weight):
    tokens, head = x.shape[0], lay.head
    v_width = taps.shape[-1]
    beside = side.shape[0]
    to_all = lambda width: pl.BlockSpec(
        (lay.batch, lay.splits, 1, lay.tokens, width), lambda z: (0, 0, z, 0, 0)
    )
    shape = lambda width: jax.ShapeDtypeStruct(
        (lay.batch, lay.splits, head, lay.tokens, width), bf16
    )
    kept = pl.BlockSpec((1, tokens, v_width), lambda z: (z, 0, 0))
    return pl.pallas_call(
        functools.partial(project_kernel, lay),
        grid=(head,),
        in_specs=[
            pl.BlockSpec(x.shape, lambda z: (0, 0)),
            pl.BlockSpec(side.shape, lambda z: (0, 0)),
            pl.BlockSpec(same.shape, lambda z: (0, 0)),
            pl.BlockSpec((1, 3, v_width), lambda z: (z, 0, 0)),
            weight_spec(weight),
        ],
        out_specs=[
            kept,
            kept,
            pl.BlockSpec((1, 2, beside, v_width), lambda z: (z, 0, 0, 0)),
        ]
        + [to_all(LANES), to_all(FEAT)] * lay.heads,
        out_shape=[
            jax.ShapeDtypeStruct((head, tokens, v_width), bf16),
            jax.ShapeDtypeStruct((head, tokens, v_width), f32),
            jax.ShapeDtypeStruct((head, 2, beside, v_width), f32),
        ]
        + [shape(LANES), shape(FEAT)] * lay.heads,
        compiler_params=pltpu.CompilerParams(vmem_limit_bytes=VMEM),
        cost_estimate=cost(head * 3 * D * tokens * weight.shape[-1]),
    )(x, side, same, taps, weight)


def project_back_kernel(
    lay, v_ref, f_ref, side_ref, same_ref, taps_ref, gk_ref, *refs
):
    backs, (out_ref, tap_ref, mixed, after) = refs[:-4], refs[-4:]
    q_width, v_width = gk_ref.shape[-1], v_ref.shape[-1]
    v_at, f_at = 2 * q_width, 2 * q_width + v_width
    taps = taps_ref[0]
    below = lay.tokens + lay.key_rows
    tap_ref[...] = jnp.zeros_like(tap_ref)
    out_ref[0, :, q_width:v_at] = gk_ref[0]
    for b in range(lay.batch):
        rows = slice(b * lay.tokens, (b + 1) * lay.tokens)
        for i in range(lay.splits):
            for j, back in enumerate(backs):
                v_cols, q_cols = lay.columns(i, j)
                block = back[b, i, 0, : lay.tokens]
                mixed[:, v_cols] = block[:, :WIDTH].astype(f32)
                out_ref[0, rows, q_cols] = block[:, WIDTH:]
                after[:, v_cols] = back[b, i, 0, below : below + 16, :WIDTH].astype(f32)
        grad_mixed = mixed[...]
        pre = f_ref[0, rows]
        sig = jax.nn.sigmoid(pre)
        values = v_ref[0, rows].astype(f32)
        same = same_ref[rows]
        at = 2 * b
        filtered, one_back, two_back = short_filter(
            taps, same, values, side_ref[0, 0, at : at + 2]
        )
        grad = grad_mixed * pre * sig
        at = 2 * (lay.batch + b)
        pre_after = side_ref[0, 1, at : at + 2]
        grad_after = after[0:2] * pre_after * jax.nn.sigmoid(pre_after)
        grad_v = (
            taps[0:1] * grad
            + taps[1:2] * later(grad, grad_after, 1) * same[:, 2:3]
            + taps[2:3] * later(grad, grad_after, 2) * same[:, 3:4]
        )
        out_ref[0, rows, v_at:f_at] = grad_v.astype(bf16)
        grad_f = grad_mixed * filtered * sig * (1.0 + pre * (1.0 - sig))
        out_ref[0, rows, f_at:] = grad_f.astype(bf16)
        for k, term in enumerate((values, one_back, two_back)):
            tap_ref[0, k : k + 1] += jnp.sum(grad * term, axis=0, keepdims=True)


def project_back(lay, backs, grad_keys, values, pre, side, same, taps):
    head, tokens, v_width = values.shape
    columns = 2 * (grad_keys.shape[-1] + v_width)
    kept = pl.BlockSpec((1, tokens, v_width), lambda z: (z, 0, 0))
    return pl.pallas_call(
        functools.partial(project_back_kernel, lay),
        grid=(head,),
        in_specs=[
            kept,
            kept,
            pl.BlockSpec((1,) + side.shape[1:], lambda z: (z, 0, 0, 0)),
            pl.BlockSpec(same.shape, lambda z: (0, 0)),
            pl.BlockSpec((1, 3, v_width), lambda z: (z, 0, 0)),
            pl.BlockSpec((1,) + grad_keys.shape[1:], lambda z: (z, 0, 0)),
        ]
        + [
            pl.BlockSpec(
                (lay.batch, lay.splits, 1) + back.shape[3:], lambda z: (0, 0, z, 0, 0)
            )
            for back in backs
        ],
        out_specs=[
            pl.BlockSpec((1, tokens, columns), lambda z: (z, 0, 0)),
            pl.BlockSpec((1, 3, v_width), lambda z: (z, 0, 0)),
        ],
        out_shape=[
            jax.ShapeDtypeStruct((head, tokens, columns), bf16),
            jax.ShapeDtypeStruct((head, 3, v_width), f32),
        ],
        scratch_shapes=[
            pltpu.VMEM((lay.tokens, v_width), f32),
            pltpu.VMEM((16, v_width), f32),
        ],
        compiler_params=pltpu.CompilerParams(vmem_limit_bytes=VMEM),
        cost_estimate=cost(1),
    )(values, pre, side, same, taps, grad_keys, *backs)


def shift(block, distance):
    devices = range(lax.axis_size("seq") * lax.axis_size("head"))
    return lax.ppermute(
        block, BOTH, [(i, i + distance) for i in devices if i + distance in devices]
    )


def local(
    tokens,
    cotangent,
    segment_ids,
    query_weight,
    key_weight,
    value_weight,
    filter_weight,
    out_weight,
    gate_weight,
    up_weight,
    down_weight,
    norm_gain,
    ffn_gain,
    conv_taps,
):
    seq, head = lax.axis_size("seq"), lax.axis_size("head")
    batch, span, _ = tokens.shape
    count = batch * span
    length = segment_ids.shape[1] * seq
    place = lax.axis_index("seq") * head + lax.axis_index("head")
    heads_here = HEADS // head
    qk_width, v_width = heads_here * FEAT, heads_here * WIDTH
    ff_width = gate_weight.shape[1]

    lay = Layout(batch, span)
    out_pad = grouped(v_width, LANES) - v_width
    first = jnp.concatenate([query_weight, key_weight, value_weight, filter_weight], axis=1)
    rows_here, columns = first.shape
    small = [norm_gain, ffn_gain, conv_taps.reshape(-1), segment_ids.astype(bf16).reshape(-1)]
    ends = [0]
    for part in small:
        ends.append(ends[-1] + part.size)
    below = grouped(-(-ends[-1] // columns), 16)
    small = jnp.pad(jnp.concatenate(small), (0, below * columns - ends[-1]))
    ff_pad = grouped(ff_width, LANES) - ff_width
    down_shard = jnp.pad(down_weight, ((0, 0), (0, ff_pad)))
    out_shard = jnp.pad(out_weight.T, ((0, 0), (0, out_pad)))
    edge = jnp.stack([tokens[:, -2:], tokens[:, :2]]).reshape(-1, D)
    edge = jnp.pad(edge, ((0, grouped(edge.shape[0], 16) - edge.shape[0]), (0, 0)))
    first_w, edges, lined = gather_first(
        jnp.concatenate([first, small.reshape(below, columns)]), edge, [down_shard, out_shard]
    )
    beside = jnp.concatenate([edges[0, : 2 * batch], edges[1, 2 * batch : 4 * batch]])
    gate_up_w = gather(tie(jnp.stack([gate_weight, up_weight]), first_w))
    down_w = Pieces(down_shard, lined[0])

    small = first_w[:, :, 0, rows_here:].reshape(seq, head, -1).astype(f32)
    part = lambda i: small[:, :, ends[i] : ends[i + 1]]
    gain_one, gain_two = part(0)[:, 0].reshape(1, D), part(1)[:, 0].reshape(1, D)
    taps = jnp.transpose(part(2).reshape(seq, head, 3, -1), (1, 2, 0, 3))
    taps = taps.reshape(head, 3, v_width)
    segs = jnp.swapaxes(part(3)[:, 0].reshape(seq, batch, -1), 0, 1).reshape(batch, length)
    x = tokens.reshape(count, D).astype(f32)
    cot_low = cotangent.reshape(count, D)

    def normed_of(rows):
        scale = inverse_rms(rows)
        return scale, (rows * scale * gain_one).astype(bf16)

    scale_one, normed = normed_of(x)
    _, normed_beside = normed_of(beside.astype(f32))
    around = lax.dynamic_slice(
        jnp.pad(segs, ((0, 0), (2, 2)), constant_values=-1.0),
        (0, place * span),
        (batch, span + 4),
    )
    seg_here = around[:, 2:-2]
    others = (around[:, 1:-3], around[:, :-4], around[:, 3:-1], around[:, 4:])
    same = jnp.stack([(seg_here == other).astype(f32) for other in others], axis=-1)
    same = same.reshape(count, 4)
    cot_left = Left(cot_low)
    normed = tie(normed, down_w.own, *cot_left.pending())
    out_w = Pieces(out_shard, lined[1])
    out_sides = out_w.sides(first_w)
    down_sides = down_w.sides(first_w)
    v_low, filter_pre, side, *sent = project(lay, normed, normed_beside, same, taps, first_w)
    my_seg = lax.dynamic_index_in_dim(segs, lay.sequence(), 0, keepdims=False)
    heads = range(lay.heads)
    mains, all_keys, kept, low = [], [], [], []
    for j in heads:
        blocks = jnp.concatenate([sent[2 * j], lay.pack_keys(sent[2 * j + 1])], axis=3)
        if j > 0:
            blocks = tie(blocks, mains[-1])
        blocks = lay.exchange(blocks.reshape(-1, span + lay.key_rows, LANES))
        mains.append(lay.all_parts(blocks[:, :span].reshape(-1, LANES)))
        all_keys.append(lay.all_parts(lay.unpack_keys(blocks[:, span:]).reshape(-1, FEAT)))
    mains[-1] = tie(mains[-1], *out_sides, *down_sides)
    out_w.far(mains[-1])
    down_w.far(mains[-1])
    for j in heads:
        attended, sent = attend(mains[j], all_keys[j], my_seg)
        kept.append(attended)
        blocks = lay.own_part(sent.reshape(-1, span, LANES))
        if j > 0:
            blocks = tie(blocks, low[-1])
        low.append(lay.exchange(blocks))
    low[-1] = tie(low[-1], *[piece for piece, _ in down_w.pieces[3:5]])
    att_low, projected = out_of_pieces(lay, [lay.by_place(blocks) for blocks in low], out_w)

    residual = x + projected
    scale_two = inverse_rms(residual)
    normed_two = (residual * scale_two * gain_two).astype(bf16)
    out_sum = Scatter(None, att_low, True)
    normed_two = tie(
        normed_two, out_sum.other_side(), *[piece for piece, _ in down_w.pieces]
    )
    slope, silu, hidden = hidden_of(normed_two, gate_up_w)
    down_sum = Scatter(cot_left, hidden)

    grad_hidden = spread(tie(cot_low, hidden), down_w)
    down_sum.right = tie(down_sum.right, grad_hidden)
    down_sends = down_sum.first()
    grads_gu, back_two = hidden_back(tie(grad_hidden, *down_sends), gate_up_w, slope, silu)
    two_left = Left(normed_two)
    gate_sum = Scatter(two_left, grads_gu)
    up_sum = Scatter(two_left, grads_gu, False, *gate_sum.other_side(), kind=1)
    gain_two_grad = jnp.sum(back_two * residual * scale_two, axis=0)
    grad_residual = cot_low.astype(f32) + norm_back(residual, scale_two, gain_two, back_two)
    grad_res_low = grad_residual.astype(bf16)

    sent = [rows.reshape(-1, span, LANES) for rows in into_pieces(lay, grad_res_low, out_w)]
    arrived = [lay.exchange(blocks) for blocks in sent]
    out_sum.left = Left(tie(grad_res_low, *sent))
    gate_sum.right = tie(gate_sum.right, *sent)
    made = gate_sum.products()
    down_sends = down_sum.second(*made)
    for terms in (up_sum, out_sum):
        terms.right = tie(terms.right, *down_sends)
    up_sum.right = tie(up_sum.right, *arrived[1:])
    made += up_sum.products() + out_sum.products()
    gate_sum.go(*down_sends)
    arrived[0] = tie(arrived[0], *made)
    backs, grad_keys = [], []
    for j in heads:
        grad_rows = lay.all_parts(arrived[j].reshape(-1, LANES))
        if j == lay.heads - 1:
            if j > 0:
                grad_rows = tie(grad_rows, sent)
            up_sum.go(grad_rows, *gate_sum.pending())
            down_sum = Along(down_sum.last(grad_rows))
            grad_rows = tie(grad_rows, *gate_sum.pending(), *down_sum.sent)
        grad_main, grad_key = attend_back(mains[j], all_keys[j], kept[j], grad_rows, my_seg)
        if j == lay.heads - 1:
            grad_main = tie(grad_main, *up_sum.pending(), *down_sum.coming)
        blocks = grad_main.reshape(-1, span, LANES)
        ahead = jnp.pad(blocks[1:, :16], ((0, 1), (0, 0), (0, 0)))
        packed = lay.pack_keys(grad_key.reshape(-1, span, FEAT))
        sent = lay.own_part(jnp.concatenate([blocks, packed, ahead], axis=1))
        if j > 0:
            sent = tie(sent, backs[-1])
        blocks = lay.exchange(sent)
        grad_keys.append(lay.unpack_keys(blocks[:, span : span + lay.key_rows]))
        backs.append(lay.by_place(blocks))
    gate_sum.second(sent)
    up_sum.second(sent)
    down_sum.go(sent)
    backs[-1] = tie(backs[-1], *gate_sum.pending(), *up_sum.pending(), *down_sum.coming)
    out_sum.go(backs[-1])

    grad_keys = jnp.stack([lay.by_place(rows) for rows in grad_keys])
    grad_keys = jnp.transpose(grad_keys, (3, 1, 4, 2, 0, 5)).reshape(head, count, -1)
    grad_first, tap_grads = project_back(
        lay, backs, grad_keys, v_low, filter_pre, side, same, taps
    )
    tap_grads = jnp.swapaxes(tap_grads, 0, 1).reshape(3, D)
    gate_up_sum = Along(jnp.stack([gate_sum.last(grad_first), up_sum.last(grad_first)], axis=1))
    grad_first = tie(grad_first, *out_sum.pending())
    first_sum = Scatter(Left(tie(normed, grad_first)), grad_first[:, None])
    out_sends = out_sum.second(*first_sum.given())
    first_sum.right = tie(first_sum.right, *out_sends)
    first_sum.products(True)
    first_sum.go()
    back_one = out_of(tie(grad_first, *first_sum.made), first_w)
    gate_up_sum.go(back_one)
    gain_one_grad = jnp.sum(back_one * x * scale_one, axis=0)
    first_sends = first_sum.second(back_one)
    out_sum = Along(out_sum.last(*first_sends))
    first_sum = Along(first_sum.last(*out_sum.sent))
    gate_up_grad = gate_up_sum.finish(*first_sum.sent)
    down_grad = down_sum.finish(*first_sum.sent)
    ffn_out = collect(tie(hidden, *first_sum.sent), down_w)
    layer_output = (residual + ffn_out).astype(bf16).reshape(tokens.shape)
    out_sum.go(*first_sum.sent)
    first_sum.go(*out_sum.sent)
    out_grad = out_sum.finish(*first_sum.sent)
    first_grad = first_sum.finish()
    grad_x = (grad_residual + norm_back(x, scale_one, gain_one, back_one)).astype(bf16)
    tokens_grad = grad_x.reshape(tokens.shape)

    small = jnp.concatenate([jnp.stack([gain_one_grad, gain_two_grad]), tap_grads], axis=0)
    small = tie(small, *first_sum.sent)
    small = jnp.swapaxes(small.reshape(5, head * seq, -1), 0, 1)
    small = lax.all_to_all(small, ("head", "seq"), 0, 0, tiled=True)
    small = jnp.sum(small, axis=0)

    q_end, k_end, v_end = qk_width, 2 * qk_width, 2 * qk_width + v_width
    return (
        layer_output,
        tokens_grad,
        first_grad[:, :q_end],
        first_grad[:, q_end:k_end],
        first_grad[:, k_end:v_end],
        first_grad[:, v_end:],
        out_grad[:, :v_width].astype(f32).T,
        gate_up_grad[0][:, :ff_width].astype(f32),
        gate_up_grad[1][:, :ff_width].astype(f32),
        down_grad[:, :ff_width].astype(f32),
        small[0],
        small[1],
        small[2:],
    )


def solution(mesh):
    rows = P(None, BOTH, None)
    return jax.shard_map(
        local,
        mesh=mesh,
        in_specs=(
            rows,
            rows,
            P(None, "seq"),
            P("seq", "head"),
            P("seq", "head"),
            P("seq", "head"),
            P("seq", "head"),
            P("head", "seq"),
            P("seq", "head"),
            P("seq", "head"),
            P("seq", "head"),
            P("seq"),
            P("seq"),
            P(None, ("head", "seq")),
        ),
        out_specs=(
            rows,
            rows,
            P("seq", "head"),
            P("seq", "head"),
            P("seq", "head"),
            P("seq", "head"),
            P("head", "seq"),
            P("seq", "head"),
            P("seq", "head"),
            P("seq", "head"),
            P(("head", "seq")),
            P(("head", "seq")),
            P(None, ("head", "seq")),
        ),
        check_vma=False,
    )
```

```python
import functools

import jax
import jax.numpy as jnp
from jax import lax
from jax.experimental import pallas as pl
from jax.experimental.pallas import tpu as pltpu
from jax.sharding import PartitionSpec as P

D = 1792
HEADS = 16
FEAT = 16
WIDTH = D // HEADS
LANES = 128
VMEM = 60 * 2**20
EPSILON = 1e-06
BOTH = ("seq", "head")
CORE, SIDE_X, SIDE_Y = 1, 2, 4

f32 = jnp.float32
bf16 = jnp.bfloat16
MESH = pl.DeviceIdType.MESH


def grouped(value, multiple):
    return -(-value // multiple) * multiple


def cost(flops):
    return pl.CostEstimate(flops=int(flops), bytes_accessed=1, transcendentals=0)


def dot(left, right):
    return jnp.dot(left, right, preferred_element_type=f32)


def dot_rt(left, right):
    return lax.dot_general(left, right, (((1,), (1,)), ((), ())), preferred_element_type=f32)


def dot_lt(left, right):
    return lax.dot_general(left, right, (((0,), (0,)), ((), ())), preferred_element_type=f32)


def swap(block, bit, axis="seq"):
    devices = range(lax.axis_size(axis))
    return lax.ppermute(block, axis, [(i, i ^ bit) for i in devices])


def paired():
    return lax.axis_size("seq") == 8 and lax.axis_size("head") == 4


def tie(value, *others):
    return lax.optimization_barrier((value, others))[0]


def gather(shard):
    whole = lax.all_gather(shard, BOTH)
    return whole.reshape((lax.axis_size("seq"), lax.axis_size("head")) + shard.shape)


def by_place(blocks):
    if not paired():
        return blocks
    here = lax.axis_index("head")
    if blocks.ndim == 1:
        return blocks ^ here
    pick = lambda r: lax.dynamic_index_in_dim(blocks, here ^ r, 0, keepdims=False)
    return jnp.stack([pick(r) for r in range(4)])


def flipped(here, bit):
    return here + bit - 2 * bit * ((here // bit) % 2)


def gather_kernel(shard, edge, *refs):
    count = (len(refs) - 9) // 2
    others, (whole, edges), rest = refs[:count], refs[count : count + 2], refs[count + 2 :]
    lined, (send, recv, local, line_send, line_recv, edge_send, edge_recv) = (
        rest[:count],
        rest[count:],
    )
    place, line = lax.axis_index("seq"), lax.axis_index("head")
    seq, head = lax.axis_size("seq"), lax.axis_size("head")
    lines = [line, flipped(line, 1), flipped(line, 2), 3 - line]
    by_x, by_y, by_core = (flipped(place, bit) for bit in (SIDE_X, SIDE_Y, CORE))
    corner = flipped(by_x, SIDE_Y)
    to = lambda at, z: {"seq": at, "head": z}
    linear = place * head + line
    after, before = (linear + 1) % (seq * head), (linear + seq * head - 1) % (seq * head)
    sides = [to(at // head, at % head) for at in (after, before)]
    partners = [to(place, z) for z in lines[1:]] + [to(at, line) for at in (by_x, by_y, by_core)]
    partners += sides

    barrier = pltpu.get_barrier_semaphore()
    for partner in partners:
        pl.semaphore_signal(barrier, inc=1, device_id=partner, device_id_type=MESH)
    pl.semaphore_wait(barrier, len(partners))

    def remote(source, target, send_sem, recv_sem, partner):
        return pltpu.make_async_remote_copy(
            src_ref=source,
            dst_ref=target,
            send_sem=send_sem,
            recv_sem=recv_sem,
            device_id=partner,
            device_id_type=MESH,
        )

    copies = [pltpu.make_async_copy(shard, whole.at[place, line, 0], local.at[0])]
    copies += [
        pltpu.make_async_copy(other, target.at[0], local.at[1 + i])
        for i, (other, target) in enumerate(zip(others, lined))
    ]
    started = {}

    def start(row, r, source, at, z, partner):
        started[row, r] = remote(
            source, whole.at[at, z, 0], send.at[row, r], recv.at[row, r], partner
        )
        started[row, r].start()

    for r in (2, 1):
        start(0, r, shard, place, line, to(place, lines[r]))
    copies += [
        remote(edge, edges.at[i], edge_send.at[i], edge_recv.at[i], partner)
        for i, partner in enumerate(sides)
    ]
    for each in copies:
        each.start()
    for r in (0, 2, 1, 3):
        if r > 0:
            started[0, r].wait_recv()
        source = shard if r == 0 else whole.at[place, lines[r], 0]
        if r == 2:
            start(0, 3, source, place, lines[r], to(place, lines[1]))
        start(1, r, source, place, lines[r], to(by_x, line))
        start(2, r, source, place, lines[r], to(by_y, line))
        start(3, r, source, place, lines[r], to(by_core, line))
    more = {
        (i, r): remote(
            target.at[2] if r == 3 else other,
            target.at[r],
            line_send.at[i, r],
            line_recv.at[i, r],
            to(place, lines[2 if r == 2 else 1]),
        )
        for i, (other, target) in enumerate(zip(others, lined))
        for r in (2, 1, 3)
    }
    for (i, r), each in more.items():
        if r < 3:
            each.start()
    for r in (0, 2, 1, 3):
        z = lines[r]
        started[1, r].wait_recv()
        if r < 2:
            start(4, r, whole.at[by_x, z, 0], by_x, z, to(by_y, line))
        start(5, r, whole.at[by_x, z, 0], by_x, z, to(by_core, line))
        started[2, r].wait_recv()
        if r >= 2:
            start(4, r, whole.at[by_y, z, 0], by_y, z, to(by_x, line))
        start(6, r, whole.at[by_y, z, 0], by_y, z, to(by_core, line))
    for i in range(count):
        more[i, 2].wait_recv()
        more[i, 3].start()
    for r in (0, 2, 1, 3):
        z = lines[r]
        started[4, r].wait_recv()
        start(7, r, whole.at[corner, z, 0], corner, z, to(by_core, line))
    for (row, r), each in started.items():
        each.wait_send()
        if row in (3, 5, 6, 7):
            each.wait_recv()
    for (i, r), each in more.items():
        each.wait_send()
        if r != 2:
            each.wait_recv()
    for each in copies:
        each.wait()


def gather_first(shard, edge, others):
    seq, head = lax.axis_size("seq"), lax.axis_size("head")
    if not paired():
        return gather(shard[None]), jnp.stack([shift(edge, 1), shift(edge, -1)]), [None] * len(others)
    anywhere = pl.BlockSpec(memory_space=pl.ANY)
    count = len(others)
    dma = pltpu.SemaphoreType.DMA
    whole, edges, *lined = pl.pallas_call(
        gather_kernel,
        in_specs=[anywhere] * (2 + count),
        out_specs=[anywhere] * (2 + count),
        out_shape=[
            jax.ShapeDtypeStruct((seq, head, 1) + shard.shape, bf16),
            jax.ShapeDtypeStruct((2,) + edge.shape, bf16),
        ]
        + [jax.ShapeDtypeStruct((head,) + other.shape, bf16) for other in others],
        scratch_shapes=[
            dma((8, 4)),
            dma((8, 4)),
            dma((1 + count,)),
            dma((count, 4)),
            dma((count, 4)),
            dma((2,)),
            dma((2,)),
        ],
        compiler_params=pltpu.CompilerParams(collective_id=0, has_side_effects=True),
        cost_estimate=cost(100e9),
    )(shard, edge, *others)
    return whole, edges, lined


class Pieces:
    def __init__(self, shard, own=None):
        self.shard = shard
        self.columns = shard.shape[1]
        self.order = by_place(jnp.arange(lax.axis_size("head"), dtype=jnp.int32))
        if paired():
            if own is None:
                two = swap(shard, 2, "head")
                one = swap(jnp.stack([shard, two]), 1, "head")
                own = jnp.stack([shard, one[0], two, one[1]])
            self.own = own
        else:
            own = lax.all_gather(shard, "head")
            self.own = lax.all_gather(own, "seq", axis=1, tiled=True)
            self.pieces, self.offsets = [(self.own, 0)], jnp.zeros((1,), jnp.int32)

    def sides(self, *after):
        if paired():
            own = tie(self.own, *after) if after else self.own
            self.by_x, self.by_y = swap(own, SIDE_X), swap(own, SIDE_Y)
            return self.by_x, self.by_y
        return ()

    def far(self, *after):
        if not paired():
            return
        by_x, by_y = self.by_x[:2], self.by_y[2:]
        if after:
            by_x, by_y = tie(by_x, *after), tie(by_y, *after)
        far_a, far_b = swap(by_x, SIDE_Y), swap(by_y, SIDE_X)
        mine = [(self.own, 0), (self.by_x, 0), (self.by_y, 0), (far_a, 0), (far_b, 2)]
        self.pieces = mine + [(swap(piece, CORE), start) for piece, start in mine]
        sides = (0, SIDE_X, SIDE_Y, SIDE_X | SIDE_Y, SIDE_X | SIDE_Y)
        sides = sides + tuple(side | CORE for side in sides)
        rows = self.shard.shape[0]
        self.offsets = (lax.axis_index("seq") ^ jnp.array(sides, jnp.int32)) * rows

    @property
    def places(self):
        return self.own.shape[0]

    def specs(self):
        def spec(piece, start):
            last = piece.shape[0] - 1
            return pl.BlockSpec(
                (1,) + piece.shape[1:], lambda z, o, p: (jnp.clip(z - start, 0, last), 0, 0)
            )

        return [spec(piece, start) for piece, start in self.pieces]

    def fill(self, offsets, refs, weight):
        z = pl.program_id(0)
        for i, (ref, (piece, start)) in enumerate(zip(refs, self.pieces)):
            count, rows, _ = piece.shape

            def put():
                at = pl.multiple_of(offsets[i], 16)
                weight[pl.ds(at, rows)] = ref[0]

            if count == self.places:
                put()
            else:
                pl.when((z >= start) & (z < start + count))(put)


def grad_kernel(first, plane, left0, left1, right0, right1, send, keep, rows0, rows1):
    _, width, tokens = left0.shape

    @pl.when(pl.program_id(0) == 0)
    def _():
        for i in range(4):
            rows0[i * width : (i + 1) * width] = left0[plane[0] ^ i]
            rows1[i * width : (i + 1) * width] = left1[plane[0] ^ i]

    total = dot(rows0[...], right0[0, 0]) + dot(rows1[...], right1[0, 0])
    total = total.astype(bf16)
    far = first // 2
    near = 3 ^ far
    for i, at in enumerate((0, near)):
        keep[i, 0] = total[at * width : (at + 1) * width]
        at ^= far
        send[i, 0] = total[at * width : (at + 1) * width]


def weight_grads(plane, left0, left1, right0, right1, kind, start, first, light):
    count, _, tokens, columns = right0.shape
    count //= 2
    width = left0.shape[1]
    left = pl.BlockSpec(left0.shape, lambda z, p: (0, 0, 0))
    right = pl.BlockSpec((1, 1, tokens, columns), lambda z, p: (z + start, kind, 0, 0))
    out = pl.BlockSpec((2, 1, width, columns), lambda z, p: (0, z, 0, 0))
    shape = jax.ShapeDtypeStruct((2, count, width, columns), bf16)
    return pl.pallas_call(
        functools.partial(grad_kernel, first),
        grid_spec=pltpu.PrefetchScalarGridSpec(
            num_scalar_prefetch=1,
            grid=(count,),
            in_specs=[left, left, right, right],
            out_specs=[out, out],
            scratch_shapes=[pltpu.VMEM((4 * width, tokens), bf16)] * 2,
        ),
        out_shape=[shape, shape],
        compiler_params=pltpu.CompilerParams(vmem_limit_bytes=VMEM),
        cost_estimate=cost(1 if light else count * 20 * width * tokens * columns),
    )(plane, left0, left1, right0, right1)


class Left:
    def __init__(self, rows):
        self.rows = rows
        if paired():
            blocks = rows.T.reshape(4, 2, D // 8, -1)
            core = lax.axis_index("seq") % 2
            pick = lambda c: lax.dynamic_index_in_dim(blocks, c, 1, keepdims=False)
            self.near, self.far = pick(core), swap(pick(1 - core), CORE)

    def pending(self):
        return (self.far,) if paired() else ()


class Scatter:
    def __init__(self, left, right, relative=False, other=None, kind=0):
        self.right = right
        self.left = left
        self.relative = relative
        self.kind = kind
        if paired():
            self.other = swap(right, CORE) if other is None else other

    def given(self):
        return (self.other,) + self.left.pending() if paired() else ()

    def other_side(self):
        return (self.other,) if paired() else (None,)

    def first(self):
        made = self.products()
        self.go()
        return made

    def products(self, light=False):
        self.made = []
        if not paired():
            return ()
        half = self.right.shape[0] // 2
        plane = (lax.axis_index("seq") // 2).reshape(1)
        self.kept = []
        for start, side in ((0, SIDE_X), (half, SIDE_Y)):
            send, keep = weight_grads(
                plane,
                self.left.near,
                self.left.far,
                self.right,
                self.other,
                self.kind,
                start,
                side,
                light,
            )
            self.made.append(send)
            self.kept.append(keep)
        return tuple(self.made)

    def go(self, *after):
        if paired():
            made = [tie(send, *after) for send in self.made] if after else self.made
            self.arrived = [swap(send, side) for send, side in zip(made, (SIDE_X, SIDE_Y))]
            self.coming = self.arrived

    def second(self, *after):
        if not paired():
            return ()
        self.sums, made = [], []
        for keep, arrived, side in zip(self.kept, self.arrived, (SIDE_Y, SIDE_X)):
            if after:
                arrived = tie(arrived, *after)
            go = (keep[1].astype(f32) + arrived[1].astype(f32)).astype(bf16)
            stay = keep[0].astype(f32) + arrived[0].astype(f32)
            made.append(go)
            self.sums.append((stay, swap(go, side)))
        self.coming = [arrived for _, arrived in self.sums]
        return tuple(made)

    def pending(self):
        return tuple(self.coming) if paired() else ()

    def last(self, *after):
        if not paired():
            whole = jnp.einsum(
                "td,htc->hdc", self.left.rows, self.right[:, self.kind], preferred_element_type=f32
            ).astype(bf16)
            seq = lax.axis_size("seq")
            whole = whole.reshape(whole.shape[:1] + (seq, D // seq, -1))
            return lax.psum_scatter(whole, "seq", scatter_dimension=1)
        sums = []
        for stay, arrived in self.sums:
            if after:
                arrived = tie(arrived, *after)
            sums.append((stay + arrived.astype(f32)).astype(bf16))
        sums = jnp.concatenate(sums, axis=0)
        if self.relative:
            sums = by_place(sums)
        return sums


class Along:
    def __init__(self, blocks):
        if not paired():
            self.total = lax.psum_scatter(blocks, "head", scatter_dimension=0).astype(f32)
            self.coming, self.sent = (), ()
            return
        here = lax.axis_index("head")
        pick = lambda r: lax.dynamic_index_in_dim(blocks, here ^ r, 0, keepdims=False)
        self.kept = (pick(0), pick(2))
        sent = jnp.stack([pick(1), pick(3)])
        self.sent = (sent,)
        self.coming = (swap(sent, 1, "head"),)

    def go(self, *after):
        if not paired():
            return
        (arrived,) = self.coming
        if after:
            arrived = tie(arrived, *after)
        self.stay = self.kept[0].astype(f32) + arrived[0].astype(f32)
        sent = (self.kept[1].astype(f32) + arrived[1].astype(f32)).astype(bf16)
        self.sent = (sent,)
        self.coming = (swap(sent, 2, "head"),)

    def finish(self, *after):
        if not paired():
            return self.total
        (arrived,) = self.coming
        if after:
            arrived = tie(arrived, *after)
        return self.stay + arrived.astype(f32)


def whole_rows(ref, kind=0):
    block = ref[:, 0, kind]
    return block.reshape(D, block.shape[-1])


def weight_spec(weight, kinds=1, at=0):
    seq, _, _, _, columns = weight.shape
    return pl.BlockSpec((seq, 1, kinds, D // seq, columns), lambda z: (0, z, at, 0, 0))


def into_kernel(x_ref, w_ref, out_ref):
    out_ref[0] = dot(x_ref[...], whole_rows(w_ref)).astype(out_ref.dtype)


def into(x, weight, kind):
    count, columns = weight.shape[1], weight.shape[-1]
    tokens = x.shape[0]
    return pl.pallas_call(
        into_kernel,
        grid=(count,),
        in_specs=[
            pl.BlockSpec(x.shape, lambda z: (0, 0)),
            weight_spec(weight),
        ],
        out_specs=pl.BlockSpec((1, tokens, columns), lambda z: (z, 0, 0)),
        out_shape=jax.ShapeDtypeStruct((count, tokens, columns), kind),
        compiler_params=pltpu.CompilerParams(vmem_limit_bytes=VMEM),
        cost_estimate=cost(count * 3 * D * tokens * columns),
    )(x, weight)


def out_of_kernel(y_ref, w_ref, out_ref):
    @pl.when(pl.program_id(0) == 0)
    def _():
        out_ref[...] = jnp.zeros_like(out_ref)

    out_ref[...] += dot_rt(y_ref[0], whole_rows(w_ref))


def out_of(y, weight):
    count, tokens, columns = y.shape
    return pl.pallas_call(
        out_of_kernel,
        grid=(count,),
        in_specs=[
            pl.BlockSpec((1, tokens, columns), lambda z: (z, 0, 0)),
            weight_spec(weight),
        ],
        out_specs=pl.BlockSpec((tokens, D), lambda z: (0, 0)),
        out_shape=jax.ShapeDtypeStruct((tokens, D), f32),
        compiler_params=pltpu.CompilerParams(vmem_limit_bytes=VMEM),
        cost_estimate=cost(1),
    )(y, weight)


def into_pieces_kernel(lay, weights, offsets, places, x_ref, *refs):
    count = len(weights.pieces)
    refs, outs, weight = refs[:count], refs[count:-1], refs[-1]
    weights.fill(offsets, refs, weight)
    rows = dot(x_ref[...], weight[...])
    for b in range(lay.batch):
        here = slice(b * lay.tokens, (b + 1) * lay.tokens)
        for i in range(lay.splits):
            for j, out in enumerate(outs):
                out[b, i, 0, :, :WIDTH] = rows[here, lay.columns(i, j)[0]].astype(bf16)
                out[b, i, 0, :, WIDTH:] = jnp.zeros_like(out[b, i, 0, :, WIDTH:])


def into_pieces(lay, x, weights):
    count, columns = weights.places, weights.columns
    block = (lay.batch, lay.splits, 1, lay.tokens, LANES)
    return pl.pallas_call(
        functools.partial(into_pieces_kernel, lay, weights),
        grid_spec=pltpu.PrefetchScalarGridSpec(
            num_scalar_prefetch=2,
            grid=(count,),
            in_specs=[pl.BlockSpec(x.shape, lambda z, o, p: (0, 0))] + weights.specs(),
            out_specs=[pl.BlockSpec(block, lambda z, o, p: (0, 0, p[z], 0, 0))] * lay.heads,
            scratch_shapes=[pltpu.VMEM((D, columns), bf16)],
        ),
        out_shape=[jax.ShapeDtypeStruct(block[:2] + (count,) + block[3:], bf16)] * lay.heads,
        compiler_params=pltpu.CompilerParams(vmem_limit_bytes=VMEM),
        cost_estimate=cost(count * 3 * D * x.shape[0] * columns),
    )(weights.offsets, weights.order, x, *[piece for piece, _ in weights.pieces])


def out_of_pieces_kernel(lay, weights, offsets, places, *refs):
    ys, refs, (rows_ref, out_ref, weight) = refs[: lay.heads], refs[lay.heads : -3], refs[-3:]
    weights.fill(offsets, refs, weight)

    @pl.when(pl.program_id(0) == 0)
    def _():
        out_ref[...] = jnp.zeros_like(out_ref)

    end = lay.splits * lay.heads * WIDTH
    rows_ref[0, 0, :, end:] = jnp.zeros_like(rows_ref[0, 0, :, end:])
    for b in range(lay.batch):
        here = slice(b * lay.tokens, (b + 1) * lay.tokens)
        for i in range(lay.splits):
            for j, y_ref in enumerate(ys):
                rows_ref[0, 0, here, lay.columns(i, j)[0]] = y_ref[b, i, 0, :, :WIDTH]
    out_ref[...] += dot_rt(rows_ref[0, 0], weight[...])


def out_of_pieces(lay, ys, weights):
    count, columns = weights.places, weights.columns
    tokens = lay.batch * lay.tokens
    block = (lay.batch, lay.splits, 1, lay.tokens, LANES)
    return pl.pallas_call(
        functools.partial(out_of_pieces_kernel, lay, weights),
        grid_spec=pltpu.PrefetchScalarGridSpec(
            num_scalar_prefetch=2,
            grid=(count,),
            in_specs=[pl.BlockSpec(block, lambda z, o, p: (0, 0, p[z], 0, 0))] * lay.heads
            + weights.specs(),
            out_specs=[
                pl.BlockSpec((1, 1, tokens, columns), lambda z, o, p: (z, 0, 0, 0)),
                pl.BlockSpec((tokens, D), lambda z, o, p: (0, 0)),
            ],
            scratch_shapes=[pltpu.VMEM((D, columns), bf16)],
        ),
        out_shape=[
            jax.ShapeDtypeStruct((count, 1, tokens, columns), bf16),
            jax.ShapeDtypeStruct((tokens, D), f32),
        ],
        compiler_params=pltpu.CompilerParams(vmem_limit_bytes=VMEM),
        cost_estimate=cost(count * 3 * D * tokens * columns),
    )(weights.offsets, weights.order, *ys, *[piece for piece, _ in weights.pieces])


def spread_kernel(weights, offsets, places, x_ref, *refs):
    refs, (out_ref, weight) = refs[:-2], refs[-2:]
    weights.fill(offsets, refs, weight)
    out_ref[0] = dot(x_ref[...], weight[...])


def spread(x, weights):
    count, columns = weights.places, weights.columns
    tokens = x.shape[0]
    return pl.pallas_call(
        functools.partial(spread_kernel, weights),
        grid_spec=pltpu.PrefetchScalarGridSpec(
            num_scalar_prefetch=2,
            grid=(count,),
            in_specs=[pl.BlockSpec(x.shape, lambda z, o, p: (0, 0))] + weights.specs(),
            out_specs=pl.BlockSpec((1, tokens, columns), lambda z, o, p: (p[z], 0, 0)),
            scratch_shapes=[pltpu.VMEM((D, columns), bf16)],
        ),
        out_shape=jax.ShapeDtypeStruct((count, tokens, columns), f32),
        compiler_params=pltpu.CompilerParams(vmem_limit_bytes=VMEM),
        cost_estimate=cost(count * 3 * D * tokens * columns),
    )(weights.offsets, weights.order, x, *[piece for piece, _ in weights.pieces])


def collect_kernel(weights, offsets, places, y_ref, *refs):
    refs, (out_ref, weight) = refs[:-2], refs[-2:]
    weights.fill(offsets, refs, weight)

    @pl.when(pl.program_id(0) == 0)
    def _():
        out_ref[...] = jnp.zeros_like(out_ref)

    out_ref[...] += dot_rt(y_ref[0, 0], weight[...])


def collect(y, weights):
    count, _, tokens, columns = y.shape
    return pl.pallas_call(
        functools.partial(collect_kernel, weights),
        grid_spec=pltpu.PrefetchScalarGridSpec(
            num_scalar_prefetch=2,
            grid=(count,),
            in_specs=[pl.BlockSpec((1,) + y.shape[1:], lambda z, o, p: (p[z], 0, 0, 0))]
            + weights.specs(),
            out_specs=pl.BlockSpec((tokens, D), lambda z, o, p: (0, 0)),
            scratch_shapes=[pltpu.VMEM((D, columns), bf16)],
        ),
        out_shape=jax.ShapeDtypeStruct((tokens, D), f32),
        compiler_params=pltpu.CompilerParams(vmem_limit_bytes=VMEM),
        cost_estimate=cost(count * 3 * D * tokens * columns),
    )(weights.offsets, weights.order, y, *[piece for piece, _ in weights.pieces])


def hidden_kernel(x_ref, gu_ref, slope_ref, silu_ref, hidden_ref):
    gate = dot(x_ref[...], whole_rows(gu_ref, 0))
    sig = jax.nn.sigmoid(gate)
    silu = gate * sig
    up = dot(x_ref[...], whole_rows(gu_ref, 1))
    slope_ref[0] = (up * sig * (1.0 + gate * (1.0 - sig))).astype(bf16)
    silu_ref[0] = silu.astype(bf16)
    columns = gate.shape[1]
    hidden_ref[0, 0, :, :columns] = (silu * up).astype(bf16)
    hidden_ref[0, 0, :, columns:] = jnp.zeros_like(hidden_ref[0, 0, :, columns:])


def hidden_of(x, weight):
    count, columns = weight.shape[1], weight.shape[-1]
    padded = grouped(columns, LANES)
    tokens = x.shape[0]
    act = pl.BlockSpec((1, tokens, columns), lambda z: (z, 0, 0))
    kept = jax.ShapeDtypeStruct((count, tokens, columns), bf16)
    return pl.pallas_call(
        hidden_kernel,
        grid=(count,),
        in_specs=[pl.BlockSpec(x.shape, lambda z: (0, 0)), weight_spec(weight, kinds=2)],
        out_specs=[act, act, pl.BlockSpec((1, 1, tokens, padded), lambda z: (z, 0, 0, 0))],
        out_shape=[kept, kept, jax.ShapeDtypeStruct((count, 1, tokens, padded), bf16)],
        compiler_params=pltpu.CompilerParams(vmem_limit_bytes=VMEM),
        cost_estimate=cost(count * 6 * D * tokens * columns),
    )(x, weight)


def hidden_back_kernel(grad_ref, gu_ref, slope_ref, silu_ref, grads_ref, out_ref):
    @pl.when(pl.program_id(0) == 0)
    def _():
        out_ref[...] = jnp.zeros_like(out_ref)

    columns = slope_ref.shape[-1]
    grad_hidden = grad_ref[0, :, :columns]
    grad_gate = (grad_hidden * slope_ref[0].astype(f32)).astype(bf16)
    grad_up = (grad_hidden * silu_ref[0].astype(f32)).astype(bf16)
    grads_ref[0, 0, :, :columns] = grad_gate
    grads_ref[0, 1, :, :columns] = grad_up
    grads_ref[0, :, :, columns:] = jnp.zeros_like(grads_ref[0, :, :, columns:])
    out_ref[...] += dot_rt(grad_gate, whole_rows(gu_ref, 0)) + dot_rt(
        grad_up, whole_rows(gu_ref, 1)
    )


def hidden_back(grad, weight, slope, silu):
    count, columns = weight.shape[1], weight.shape[-1]
    padded = grouped(columns, LANES)
    tokens = grad.shape[1]
    act = pl.BlockSpec((1, tokens, columns), lambda z: (z, 0, 0))
    return pl.pallas_call(
        hidden_back_kernel,
        grid=(count,),
        in_specs=[
            pl.BlockSpec((1, tokens, padded), lambda z: (z, 0, 0)),
            weight_spec(weight, kinds=2),
            act,
            act,
        ],
        out_specs=[
            pl.BlockSpec((1, 2, tokens, padded), lambda z: (z, 0, 0, 0)),
            pl.BlockSpec((tokens, D), lambda z: (0, 0)),
        ],
        out_shape=[
            jax.ShapeDtypeStruct((count, 2, tokens, padded), bf16),
            jax.ShapeDtypeStruct((tokens, D), f32),
        ],
        compiler_params=pltpu.CompilerParams(vmem_limit_bytes=VMEM),
        cost_estimate=cost(1),
    )(grad, weight, slope, silu)


def inverse_rms(rows):
    return lax.rsqrt(jnp.mean(rows * rows, axis=-1, keepdims=True) + EPSILON)


def norm_back(rows, scale, gain, grad):
    unit = rows * scale
    scaled = gain * grad
    return scale * (scaled - unit * jnp.mean(scaled * unit, axis=-1, keepdims=True))


class Layout:
    def __init__(self, batch, tokens):
        seq, head = lax.axis_size("seq"), lax.axis_size("head")
        self.batch, self.tokens, self.head = batch, tokens, head
        self.splits = min(seq // batch, HEADS // head)
        self.heads = HEADS // (head * self.splits)
        self.parts = seq // (batch * self.splits)
        self.inner = seq // self.parts
        self.sets = LANES // FEAT
        self.key_rows = grouped(tokens // self.sets, 16)
        self.length = tokens * seq * head
        count = self.inner * head
        self.groups = None
        if self.parts > 1:
            self.groups = [list(range(k * count, (k + 1) * count)) for k in range(self.parts)]
            self.mates = [[k * count + i for k in range(self.parts)] for i in range(count)]

    def sequence(self):
        return lax.rem(lax.axis_index("seq"), self.inner) // self.splits

    def pack_keys(self, keys):
        lead, each = keys.shape[:-2], self.tokens // self.sets
        keys = keys.reshape(lead + (self.sets, each, FEAT))
        keys = jnp.swapaxes(keys, -3, -2).reshape(lead + (each, LANES))
        return jnp.pad(keys, [(0, 0)] * len(lead) + [(0, self.key_rows - each), (0, 0)])

    def unpack_keys(self, rows):
        lead, each = rows.shape[:-2], self.tokens // self.sets
        rows = rows[..., :each, :].reshape(lead + (each, self.sets, FEAT))
        return jnp.swapaxes(rows, -3, -2).reshape(lead + (self.tokens, FEAT))

    def columns(self, i, j):
        at = i * self.heads + j
        return slice(at * WIDTH, (at + 1) * WIDTH), slice(at * FEAT, (at + 1) * FEAT)

    def by_place(self, blocks):
        return blocks.reshape((self.batch, self.splits, self.head) + blocks.shape[1:])

    def exchange(self, blocks):
        return lax.all_to_all(blocks, BOTH, 0, 0, tiled=True, axis_index_groups=self.groups)

    def all_parts(self, rows):
        if self.parts > 1:
            rows = lax.all_gather(rows, BOTH, axis=0, tiled=True, axis_index_groups=self.mates)
        return rows

    def own_part(self, blocks):
        if self.parts > 1:
            count = blocks.shape[0] // self.parts
            part = lax.axis_index("seq") // self.inner
            blocks = lax.dynamic_slice_in_dim(blocks, part * count, count, 0)
        return blocks


def fill_values(chunk, main, values, queries):
    lane = lax.broadcasted_iota(jnp.int32, (chunk, LANES), 1)
    ones = jnp.where(lane < WIDTH + 2, 1.0, 0.0)

    def turn(i, _):
        here = pl.ds(pl.multiple_of(i * chunk, chunk), chunk)
        rows = main[here]
        values[here] = jnp.where(lane < WIDTH, rows.astype(f32), ones).astype(bf16)
        queries[here] = rows[:, WIDTH:]
        return 0

    lax.fori_loop(0, main.shape[0] // chunk, turn, 0)


def attend_kernel(chunk, main, keys, seg_col, seg_row, out_ref, low_ref, values, queries):
    at = pl.program_id(0)

    @pl.when(at == 0)
    def _():
        fill_values(chunk, main, values, queries)

    mine = seg_col[...]
    query = queries[pl.ds(pl.multiple_of(at * chunk, chunk), chunk)]

    def weighted(j, causal):
        here = pl.ds(pl.multiple_of(j * chunk, chunk), chunk)
        scores = dot_rt(query, keys[here])
        allowed = mine == seg_row[j]
        if causal:
            later = lax.broadcasted_iota(jnp.int32, scores.shape, 0)
            allowed &= later >= lax.broadcasted_iota(jnp.int32, scores.shape, 1)
        weights = jnp.where(allowed, 1.0 + scores * (1.0 + 0.5 * scores), 0.0).astype(bf16)
        return dot(weights, values[here])

    total = lax.fori_loop(
        0, at, lambda j, acc: acc + weighted(j, False), jnp.zeros((chunk, LANES), f32)
    )
    total = total + weighted(at, True)
    norm = total[:, WIDTH : WIDTH + 1]
    lane = lax.broadcasted_iota(jnp.int32, total.shape, 1)
    total = jnp.where(lane < WIDTH, total / norm, norm)
    out_ref[...] = total
    low_ref[...] = total.astype(bf16)


def attend(main, keys, seg):
    length = main.shape[0]
    chunk = min(512, length)
    steps = length // chunk
    part = pl.BlockSpec((chunk, LANES), lambda i: (i, 0))
    return pl.pallas_call(
        functools.partial(attend_kernel, chunk),
        grid=(steps,),
        in_specs=[
            pl.BlockSpec((length, LANES), lambda i: (0, 0)),
            pl.BlockSpec((length, FEAT), lambda i: (0, 0)),
            pl.BlockSpec((chunk, 1), lambda i: (i, 0)),
            pl.BlockSpec((steps, 1, chunk), lambda i: (0, 0, 0)),
        ],
        out_specs=[part, part],
        out_shape=[
            jax.ShapeDtypeStruct((length, LANES), f32),
            jax.ShapeDtypeStruct((length, LANES), bf16),
        ],
        scratch_shapes=[pltpu.VMEM((length, LANES), bf16), pltpu.VMEM((length, FEAT), bf16)],
        compiler_params=pltpu.CompilerParams(vmem_limit_bytes=VMEM),
        cost_estimate=cost(length * length * 12 * LANES),
    )(main, keys, seg.reshape(length, 1), seg.reshape(steps, 1, chunk))


def attend_back_kernel(
    chunk,
    main,
    keys,
    kept,
    grad,
    seg_col,
    seg_row,
    out_ref,
    gk_ref,
    values,
    queries,
    grad_n,
    grad_q,
):
    at = pl.program_id(0)
    steps = main.shape[0] // chunk

    @pl.when(at == 0)
    def _():
        fill_values(chunk, main, values, queries)
        grad_q[...] = jnp.zeros_like(grad_q)
        lane = lax.broadcasted_iota(jnp.int32, (chunk, LANES), 1)

        def turn(i, _):
            here = pl.ds(pl.multiple_of(i * chunk, chunk), chunk)
            rows = kept[here]
            low = jnp.where(lane < WIDTH, grad[here].astype(f32), 0.0)
            inverse = 1.0 / rows[:, WIDTH : WIDTH + 1]
            total = -jnp.sum(low * rows, axis=1, keepdims=True) * inverse
            high = total.astype(bf16).astype(f32)
            low = low * inverse
            low = jnp.where(lane == WIDTH, high, low)
            grad_n[here] = jnp.where(lane == WIDTH + 1, total - high, low).astype(bf16)
            return 0

        lax.fori_loop(0, steps, turn, 0)

    mine = seg_col[...]
    rows = pl.ds(pl.multiple_of(at * chunk, chunk), chunk)
    key, value = keys[rows], values[rows]
    key_t = key.astype(f32).T.astype(bf16)

    def turn(i, carry, causal):
        grad_k, grad_v = carry
        here = pl.ds(pl.multiple_of(i * chunk, chunk), chunk)
        query, grad_here = queries[here], grad_n[here]
        scores = dot_rt(key, query)
        allowed = mine == seg_row[i]
        if causal:
            key_at = lax.broadcasted_iota(jnp.int32, scores.shape, 0)
            allowed &= key_at <= lax.broadcasted_iota(jnp.int32, scores.shape, 1)
        weights = jnp.where(allowed, 1.0 + scores * (1.0 + 0.5 * scores), 0.0).astype(bf16)
        grad_s = dot_rt(value, grad_here) * (1.0 + scores)
        grad_s = jnp.where(allowed, grad_s, 0.0).astype(bf16)
        grad_q[:, here] += dot(key_t, grad_s)
        return grad_k + dot(grad_s, query), grad_v + dot(weights, grad_here)

    carry = (jnp.zeros((chunk, FEAT), f32), jnp.zeros((chunk, LANES), f32))
    carry = turn(at, carry, True)
    grad_k, grad_v = lax.fori_loop(at + 1, steps, lambda i, c: turn(i, c, False), carry)
    gk_ref[...] = (0.5 * grad_k).astype(bf16)
    out_ref[rows] = grad_v.astype(bf16)

    @pl.when(at == steps - 1)
    def _():
        def turn(i, _):
            here = pl.ds(pl.multiple_of(i * chunk, chunk), chunk)
            out_ref[here, WIDTH:] = (0.5 * grad_q[:, here].T).astype(bf16)
            return 0

        lax.fori_loop(0, steps, turn, 0)


def attend_back(main, keys, kept, grad, seg):
    length = main.shape[0]
    chunk = min(512, length)
    steps = length // chunk
    whole = pl.BlockSpec((length, LANES), lambda i: (0, 0))
    return pl.pallas_call(
        functools.partial(attend_back_kernel, chunk),
        grid=(steps,),
        in_specs=[
            whole,
            pl.BlockSpec((length, FEAT), lambda i: (0, 0)),
            whole,
            whole,
            pl.BlockSpec((chunk, 1), lambda i: (i, 0)),
            pl.BlockSpec((steps, 1, chunk), lambda i: (0, 0, 0)),
        ],
        out_specs=[whole, pl.BlockSpec((chunk, FEAT), lambda i: (i, 0))],
        out_shape=[
            jax.ShapeDtypeStruct((length, LANES), bf16),
            jax.ShapeDtypeStruct((length, FEAT), bf16),
        ],
        scratch_shapes=[
            pltpu.VMEM((length, LANES), bf16),
            pltpu.VMEM((length, FEAT), bf16),
            pltpu.VMEM((length, LANES), bf16),
            pltpu.VMEM((FEAT, length), f32),
        ],
        compiler_params=pltpu.CompilerParams(vmem_limit_bytes=VMEM),
        cost_estimate=cost(length * length * 24 * LANES),
    )(main, keys, kept, grad, seg.reshape(length, 1), seg.reshape(steps, 1, chunk))


def earlier(rows, before, distance):
    moved = pltpu.roll(rows, distance, 0)
    place = lax.broadcasted_iota(jnp.int32, rows.shape, 0)
    for i in range(distance):
        at = 2 - distance + i
        moved = jnp.where(place == i, before[at : at + 1], moved)
    return moved


def later(rows, after, distance):
    count = rows.shape[0]
    moved = pltpu.roll(rows, count - distance, 0)
    place = lax.broadcasted_iota(jnp.int32, rows.shape, 0)
    for i in range(distance):
        moved = jnp.where(place == count - distance + i, after[i : i + 1], moved)
    return moved


def short_filter(taps, same, values, before):
    one_back = earlier(values, before, 1) * same[:, 0:1]
    two_back = earlier(values, before, 2) * same[:, 1:2]
    return taps[0:1] * values + taps[1:2] * one_back + taps[2:3] * two_back, one_back, two_back


def project_kernel(lay, x_ref, side_ref, same_ref, taps_ref, w_ref, v_ref, f_ref, side_out, *outs):
    weight = whole_rows(w_ref)
    q_width, v_width = lay.splits * lay.heads * FEAT, v_ref.shape[-1]
    v_at, f_at = 2 * q_width, 2 * q_width + v_width
    full = dot(x_ref[...], weight)
    side = dot(side_ref[...], weight)
    low = full[:, v_at:f_at].astype(bf16)
    v_ref[0] = low
    f_ref[0] = full[:, f_at:]
    side_v = side[:, v_at:f_at].astype(bf16).astype(f32)
    side_out[0, 0] = side_v
    side_out[0, 1] = side[:, f_at:]
    taps = taps_ref[0]
    for b in range(lay.batch):
        rows = slice(b * lay.tokens, (b + 1) * lay.tokens)
        pre = full[rows, f_at:]
        filtered, _, _ = short_filter(
            taps, same_ref[rows], low[rows].astype(f32), side_v[2 * b : 2 * b + 2]
        )
        mixed = filtered * (pre * jax.nn.sigmoid(pre))
        query = 0.5 * full[rows, :q_width].astype(bf16).astype(f32)
        key = 0.5 * full[rows, q_width:v_at].astype(bf16).astype(f32)
        for i in range(lay.splits):
            for j in range(lay.heads):
                main, k_ref = outs[2 * j : 2 * j + 2]
                v_cols, q_cols = lay.columns(i, j)
                main[b, i, 0, :, :WIDTH] = mixed[:, v_cols].astype(bf16)
                main[b, i, 0, :, WIDTH:] = query[:, q_cols].astype(bf16)
                k_ref[b, i, 0] = key[:, q_cols].astype(bf16)


def project(lay, x, side, same, taps, weight):
    tokens, head = x.shape[0], lay.head
    v_width = taps.shape[-1]
    beside = side.shape[0]
    to_all = lambda width: pl.BlockSpec(
        (lay.batch, lay.splits, 1, lay.tokens, width), lambda z: (0, 0, z, 0, 0)
    )
    shape = lambda width: jax.ShapeDtypeStruct(
        (lay.batch, lay.splits, head, lay.tokens, width), bf16
    )
    kept = pl.BlockSpec((1, tokens, v_width), lambda z: (z, 0, 0))
    return pl.pallas_call(
        functools.partial(project_kernel, lay),
        grid=(head,),
        in_specs=[
            pl.BlockSpec(x.shape, lambda z: (0, 0)),
            pl.BlockSpec(side.shape, lambda z: (0, 0)),
            pl.BlockSpec(same.shape, lambda z: (0, 0)),
            pl.BlockSpec((1, 3, v_width), lambda z: (z, 0, 0)),
            weight_spec(weight),
        ],
        out_specs=[
            kept,
            kept,
            pl.BlockSpec((1, 2, beside, v_width), lambda z: (z, 0, 0, 0)),
        ]
        + [to_all(LANES), to_all(FEAT)] * lay.heads,
        out_shape=[
            jax.ShapeDtypeStruct((head, tokens, v_width), bf16),
            jax.ShapeDtypeStruct((head, tokens, v_width), f32),
            jax.ShapeDtypeStruct((head, 2, beside, v_width), f32),
        ]
        + [shape(LANES), shape(FEAT)] * lay.heads,
        compiler_params=pltpu.CompilerParams(vmem_limit_bytes=VMEM),
        cost_estimate=cost(head * 3 * D * tokens * weight.shape[-1]),
    )(x, side, same, taps, weight)


def project_back_kernel(
    lay, v_ref, f_ref, side_ref, same_ref, taps_ref, gk_ref, *refs
):
    backs, (out_ref, tap_ref, mixed, after) = refs[:-4], refs[-4:]
    q_width, v_width = gk_ref.shape[-1], v_ref.shape[-1]
    v_at, f_at = 2 * q_width, 2 * q_width + v_width
    taps = taps_ref[0]
    below = lay.tokens + lay.key_rows
    tap_ref[...] = jnp.zeros_like(tap_ref)
    out_ref[0, :, q_width:v_at] = gk_ref[0]
    for b in range(lay.batch):
        rows = slice(b * lay.tokens, (b + 1) * lay.tokens)
        for i in range(lay.splits):
            for j, back in enumerate(backs):
                v_cols, q_cols = lay.columns(i, j)
                block = back[b, i, 0, : lay.tokens]
                mixed[:, v_cols] = block[:, :WIDTH].astype(f32)
                out_ref[0, rows, q_cols] = block[:, WIDTH:]
                after[:, v_cols] = back[b, i, 0, below : below + 16, :WIDTH].astype(f32)
        grad_mixed = mixed[...]
        pre = f_ref[0, rows]
        sig = jax.nn.sigmoid(pre)
        values = v_ref[0, rows].astype(f32)
        same = same_ref[rows]
        at = 2 * b
        filtered, one_back, two_back = short_filter(
            taps, same, values, side_ref[0, 0, at : at + 2]
        )
        grad = grad_mixed * pre * sig
        at = 2 * (lay.batch + b)
        pre_after = side_ref[0, 1, at : at + 2]
        grad_after = after[0:2] * pre_after * jax.nn.sigmoid(pre_after)
        grad_v = (
            taps[0:1] * grad
            + taps[1:2] * later(grad, grad_after, 1) * same[:, 2:3]
            + taps[2:3] * later(grad, grad_after, 2) * same[:, 3:4]
        )
        out_ref[0, rows, v_at:f_at] = grad_v.astype(bf16)
        grad_f = grad_mixed * filtered * sig * (1.0 + pre * (1.0 - sig))
        out_ref[0, rows, f_at:] = grad_f.astype(bf16)
        for k, term in enumerate((values, one_back, two_back)):
            tap_ref[0, k : k + 1] += jnp.sum(grad * term, axis=0, keepdims=True)


def project_back(lay, backs, grad_keys, values, pre, side, same, taps):
    head, tokens, v_width = values.shape
    columns = 2 * (grad_keys.shape[-1] + v_width)
    kept = pl.BlockSpec((1, tokens, v_width), lambda z: (z, 0, 0))
    return pl.pallas_call(
        functools.partial(project_back_kernel, lay),
        grid=(head,),
        in_specs=[
            kept,
            kept,
            pl.BlockSpec((1,) + side.shape[1:], lambda z: (z, 0, 0, 0)),
            pl.BlockSpec(same.shape, lambda z: (0, 0)),
            pl.BlockSpec((1, 3, v_width), lambda z: (z, 0, 0)),
            pl.BlockSpec((1,) + grad_keys.shape[1:], lambda z: (z, 0, 0)),
        ]
        + [
            pl.BlockSpec(
                (lay.batch, lay.splits, 1) + back.shape[3:], lambda z: (0, 0, z, 0, 0)
            )
            for back in backs
        ],
        out_specs=[
            pl.BlockSpec((1, tokens, columns), lambda z: (z, 0, 0)),
            pl.BlockSpec((1, 3, v_width), lambda z: (z, 0, 0)),
        ],
        out_shape=[
            jax.ShapeDtypeStruct((head, tokens, columns), bf16),
            jax.ShapeDtypeStruct((head, 3, v_width), f32),
        ],
        scratch_shapes=[
            pltpu.VMEM((lay.tokens, v_width), f32),
            pltpu.VMEM((16, v_width), f32),
        ],
        compiler_params=pltpu.CompilerParams(vmem_limit_bytes=VMEM),
        cost_estimate=cost(1),
    )(values, pre, side, same, taps, grad_keys, *backs)


def shift(block, distance):
    devices = range(lax.axis_size("seq") * lax.axis_size("head"))
    return lax.ppermute(
        block, BOTH, [(i, i + distance) for i in devices if i + distance in devices]
    )


def local(
    tokens,
    cotangent,
    segment_ids,
    query_weight,
    key_weight,
    value_weight,
    filter_weight,
    out_weight,
    gate_weight,
    up_weight,
    down_weight,
    norm_gain,
    ffn_gain,
    conv_taps,
):
    seq, head = lax.axis_size("seq"), lax.axis_size("head")
    batch, span, _ = tokens.shape
    count = batch * span
    length = segment_ids.shape[1] * seq
    place = lax.axis_index("seq") * head + lax.axis_index("head")
    heads_here = HEADS // head
    qk_width, v_width = heads_here * FEAT, heads_here * WIDTH
    ff_width = gate_weight.shape[1]

    lay = Layout(batch, span)
    out_pad = grouped(v_width, LANES) - v_width
    first = jnp.concatenate([query_weight, key_weight, value_weight, filter_weight], axis=1)
    rows_here, columns = first.shape
    small = [norm_gain, ffn_gain, conv_taps.reshape(-1), segment_ids.astype(bf16).reshape(-1)]
    ends = [0]
    for part in small:
        ends.append(ends[-1] + part.size)
    below = grouped(-(-ends[-1] // columns), 16)
    small = jnp.pad(jnp.concatenate(small), (0, below * columns - ends[-1]))
    ff_pad = grouped(ff_width, LANES) - ff_width
    down_shard = jnp.pad(down_weight, ((0, 0), (0, ff_pad)))
    out_shard = jnp.pad(out_weight.T, ((0, 0), (0, out_pad)))
    edge = jnp.stack([tokens[:, -2:], tokens[:, :2]]).reshape(-1, D)
    edge = jnp.pad(edge, ((0, grouped(edge.shape[0], 16) - edge.shape[0]), (0, 0)))
    first_w, edges, lined = gather_first(
        jnp.concatenate([first, small.reshape(below, columns)]), edge, [down_shard, out_shard]
    )
    beside = jnp.concatenate([edges[0, : 2 * batch], edges[1, 2 * batch : 4 * batch]])
    gate_up_w = gather(tie(jnp.stack([gate_weight, up_weight]), first_w))
    down_w = Pieces(down_shard, lined[0])

    small = first_w[:, :, 0, rows_here:].reshape(seq, head, -1).astype(f32)
    part = lambda i: small[:, :, ends[i] : ends[i + 1]]
    gain_one, gain_two = part(0)[:, 0].reshape(1, D), part(1)[:, 0].reshape(1, D)
    taps = jnp.transpose(part(2).reshape(seq, head, 3, -1), (1, 2, 0, 3))
    taps = taps.reshape(head, 3, v_width)
    segs = jnp.swapaxes(part(3)[:, 0].reshape(seq, batch, -1), 0, 1).reshape(batch, length)
    x = tokens.reshape(count, D).astype(f32)
    cot_low = cotangent.reshape(count, D)

    def normed_of(rows):
        scale = inverse_rms(rows)
        return scale, (rows * scale * gain_one).astype(bf16)

    scale_one, normed = normed_of(x)
    _, normed_beside = normed_of(beside.astype(f32))
    around = lax.dynamic_slice(
        jnp.pad(segs, ((0, 0), (2, 2)), constant_values=-1.0),
        (0, place * span),
        (batch, span + 4),
    )
    seg_here = around[:, 2:-2]
    others = (around[:, 1:-3], around[:, :-4], around[:, 3:-1], around[:, 4:])
    same = jnp.stack([(seg_here == other).astype(f32) for other in others], axis=-1)
    same = same.reshape(count, 4)
    cot_left = Left(cot_low)
    normed = tie(normed, down_w.own, *cot_left.pending())
    out_w = Pieces(out_shard, lined[1])
    out_sides = out_w.sides(first_w)
    down_sides = down_w.sides(first_w)
    v_low, filter_pre, side, *sent = project(lay, normed, normed_beside, same, taps, first_w)
    my_seg = lax.dynamic_index_in_dim(segs, lay.sequence(), 0, keepdims=False)
    heads = range(lay.heads)
    mains, all_keys, kept, low = [], [], [], []
    for j in heads:
        blocks = jnp.concatenate([sent[2 * j], lay.pack_keys(sent[2 * j + 1])], axis=3)
        if j > 0:
            blocks = tie(blocks, mains[-1])
        blocks = lay.exchange(blocks.reshape(-1, span + lay.key_rows, LANES))
        mains.append(lay.all_parts(blocks[:, :span].reshape(-1, LANES)))
        all_keys.append(lay.all_parts(lay.unpack_keys(blocks[:, span:]).reshape(-1, FEAT)))
    mains[-1] = tie(mains[-1], *out_sides, *down_sides)
    out_w.far(mains[-1])
    down_w.far(mains[-1])
    for j in heads:
        attended, sent = attend(mains[j], all_keys[j], my_seg)
        kept.append(attended)
        blocks = lay.own_part(sent.reshape(-1, span, LANES))
        if j > 0:
            blocks = tie(blocks, low[-1])
        low.append(lay.exchange(blocks))
    low[-1] = tie(low[-1], *[piece for piece, _ in down_w.pieces[3:5]])
    att_low, projected = out_of_pieces(lay, [lay.by_place(blocks) for blocks in low], out_w)

    residual = x + projected
    scale_two = inverse_rms(residual)
    normed_two = (residual * scale_two * gain_two).astype(bf16)
    out_sum = Scatter(None, att_low, True)
    normed_two = tie(
        normed_two, out_sum.other_side(), *[piece for piece, _ in down_w.pieces]
    )
    slope, silu, hidden = hidden_of(normed_two, gate_up_w)
    down_sum = Scatter(cot_left, hidden)

    grad_hidden = spread(tie(cot_low, hidden), down_w)
    down_sum.right = tie(down_sum.right, grad_hidden)
    down_sends = down_sum.first()
    grads_gu, back_two = hidden_back(tie(grad_hidden, *down_sends), gate_up_w, slope, silu)
    two_left = Left(normed_two)
    gate_sum = Scatter(two_left, grads_gu)
    up_sum = Scatter(two_left, grads_gu, False, *gate_sum.other_side(), kind=1)
    grad_residual = cot_low.astype(f32) + norm_back(residual, scale_two, gain_two, back_two)
    grad_res_low = grad_residual.astype(bf16)

    sent = [rows.reshape(-1, span, LANES) for rows in into_pieces(lay, grad_res_low, out_w)]
    arrived = [lay.exchange(blocks) for blocks in sent]
    out_sum.left = Left(tie(grad_res_low, *sent))
    gate_sum.right = tie(gate_sum.right, *sent)
    made = gate_sum.products()
    down_sends = down_sum.second(*made)
    for terms in (up_sum, out_sum):
        terms.right = tie(terms.right, *down_sends)
    up_sum.right = tie(up_sum.right, *arrived[1:])
    made += up_sum.products() + out_sum.products()
    gain_two_grad = jnp.sum(tie(back_two, *made) * residual * scale_two, axis=0)
    gate_sum.go(*down_sends)
    arrived[0] = tie(arrived[0], *made)
    backs, grad_keys = [], []
    for j in heads:
        grad_rows = lay.all_parts(arrived[j].reshape(-1, LANES))
        if j == lay.heads - 1:
            if j > 0:
                grad_rows = tie(grad_rows, sent)
            up_sum.go(grad_rows, *gate_sum.pending())
            down_sum = Along(down_sum.last(grad_rows))
            grad_rows = tie(grad_rows, *gate_sum.pending(), *down_sum.sent)
        grad_main, grad_key = attend_back(mains[j], all_keys[j], kept[j], grad_rows, my_seg)
        if j == lay.heads - 1:
            grad_main = tie(grad_main, *up_sum.pending(), *down_sum.coming)
        blocks = grad_main.reshape(-1, span, LANES)
        ahead = jnp.pad(blocks[1:, :16], ((0, 1), (0, 0), (0, 0)))
        packed = lay.pack_keys(grad_key.reshape(-1, span, FEAT))
        sent = lay.own_part(jnp.concatenate([blocks, packed, ahead], axis=1))
        if j > 0:
            sent = tie(sent, backs[-1])
        blocks = lay.exchange(sent)
        grad_keys.append(lay.unpack_keys(blocks[:, span : span + lay.key_rows]))
        backs.append(lay.by_place(blocks))
    gate_sum.second(sent)
    up_sum.second(sent)
    down_sum.go(sent)
    backs[-1] = tie(backs[-1], *gate_sum.pending(), *up_sum.pending(), *down_sum.coming)
    out_sum.go(backs[-1])

    grad_keys = jnp.stack([lay.by_place(rows) for rows in grad_keys])
    grad_keys = jnp.transpose(grad_keys, (3, 1, 4, 2, 0, 5)).reshape(head, count, -1)
    grad_first, tap_grads = project_back(
        lay, backs, grad_keys, v_low, filter_pre, side, same, taps
    )
    tap_grads = jnp.swapaxes(tap_grads, 0, 1).reshape(3, D)
    gate_up_sum = Along(jnp.stack([gate_sum.last(grad_first), up_sum.last(grad_first)], axis=1))
    grad_first = tie(grad_first, *out_sum.pending())
    first_sum = Scatter(Left(tie(normed, grad_first)), grad_first[:, None])
    out_sends = out_sum.second(*first_sum.given())
    first_sum.right = tie(first_sum.right, *out_sends)
    first_sum.products(True)
    first_sum.go()
    back_one = out_of(tie(grad_first, *first_sum.made), first_w)
    gate_up_sum.go(back_one)
    gain_one_grad = jnp.sum(back_one * x * scale_one, axis=0)
    first_sends = first_sum.second(back_one)
    out_sum = Along(out_sum.last(*first_sends))
    first_sum = Along(first_sum.last(*out_sum.sent))
    gate_up_grad = gate_up_sum.finish(*first_sum.sent)
    down_grad = down_sum.finish(*first_sum.sent)
    ffn_out = collect(tie(hidden, *first_sum.sent), down_w)
    layer_output = (residual + ffn_out).astype(bf16).reshape(tokens.shape)
    out_sum.go(*first_sum.sent)
    first_sum.go(*out_sum.sent)
    out_grad = out_sum.finish(*first_sum.sent)
    first_grad = first_sum.finish()
    grad_x = (grad_residual + norm_back(x, scale_one, gain_one, back_one)).astype(bf16)
    tokens_grad = grad_x.reshape(tokens.shape)

    small = jnp.concatenate([jnp.stack([gain_one_grad, gain_two_grad]), tap_grads], axis=0)
    small = tie(small, *first_sum.sent)
    small = jnp.swapaxes(small.reshape(5, head * seq, -1), 0, 1)
    small = lax.all_to_all(small, ("head", "seq"), 0, 0, tiled=True)
    small = jnp.sum(small, axis=0)

    q_end, k_end, v_end = qk_width, 2 * qk_width, 2 * qk_width + v_width
    return (
        layer_output,
        tokens_grad,
        first_grad[:, :q_end],
        first_grad[:, q_end:k_end],
        first_grad[:, k_end:v_end],
        first_grad[:, v_end:],
        out_grad[:, :v_width].astype(f32).T,
        gate_up_grad[0][:, :ff_width].astype(f32),
        gate_up_grad[1][:, :ff_width].astype(f32),
        down_grad[:, :ff_width].astype(f32),
        small[0],
        small[1],
        small[2:],
    )


def solution(mesh):
    rows = P(None, BOTH, None)
    return jax.shard_map(
        local,
        mesh=mesh,
        in_specs=(
            rows,
            rows,
            P(None, "seq"),
            P("seq", "head"),
            P("seq", "head"),
            P("seq", "head"),
            P("seq", "head"),
            P("head", "seq"),
            P("seq", "head"),
            P("seq", "head"),
            P("seq", "head"),
            P("seq"),
            P("seq"),
            P(None, ("head", "seq")),
        ),
        out_specs=(
            rows,
            rows,
            P("seq", "head"),
            P("seq", "head"),
            P("seq", "head"),
            P("seq", "head"),
            P("head", "seq"),
            P("seq", "head"),
            P("seq", "head"),
            P("seq", "head"),
            P(("head", "seq")),
            P(("head", "seq")),
            P(None, ("head", "seq")),
        ),
        check_vma=False,
    )
```
